256 devices in a mesh: seq: 64 (over y, z, core), head: 4 (over x).
Axes of the slice: x: 4, y: 4, z: 8, core: 2. Of those that a mesh axis runs over, the one named last changes fastest.
Arguments:
- query_rows: bfloat16 [65536, 1024], P('seq', 'head'), may hold values from -150 to 150
- key_rows: bfloat16 [65536, 1024], P('seq', 'head'), may hold values from -150 to 150
- value_rows: bfloat16 [65536, 1024], P('seq', 'head'), may hold values from -8 to 8
- segment: int32 [65536], P('seq'), may hold values from 0 to 254, as said below
- w_out: bfloat16 [1024, 1024], P('head'), may hold values from -0.5 to 0.5
Outputs:
- projected: bfloat16 [65536, 1024], P(('seq', 'head'))
The draws below stay inside these ranges and needn't reach their ends.
Inputs may be any that keep to these rules, and one draw needn't show every extreme that they name: segment ids never fall along the sequence; each segment has 1 to 512 tokens, one of them exactly 512.
All inputs are finite; a program needn't handle non-finite values.
Results may differ from the reference program's by a relative error of at most 0.0069.
Values may be sent and summed in bfloat16 or wider, within the bound.
A program may use at most 128 MiB of HBM per device.

```python
import jax
import jax.numpy as jnp
from jax import lax

HEADS = 16
HEAD_DIM = 64
D = 1024
BLOCK = 256
LEVELS = 6
TOKENS = 65536


def spread_groups(values):
    return jnp.repeat(values, 2 ** (LEVELS - 1), axis=0)


def draw_key_rows(key, part):
    key = jax.random.fold_in(key, 3)
    base_key = jax.random.fold_in(key, 0)
    group_key = jax.random.fold_in(key, 2)
    group_rows = TOKENS // 2 ** (LEVELS - 1)
    base = 0.7 * jax.random.normal(base_key, (TOKENS, D), jnp.float32)
    groups = 1.5 * jax.random.normal(group_key, (group_rows, D), jnp.float32)
    result = base + spread_groups(groups)
    return jnp.clip(result, -150.0, 150.0).astype(jnp.bfloat16)


def draw_query_rows(key, part):
    key = jax.random.fold_in(key, 5)
    base_key = jax.random.fold_in(key, 0)
    group_key = jax.random.fold_in(key, 2)
    group_rows = TOKENS // 2 ** (LEVELS - 1)
    base = 0.7 * jax.random.normal(base_key, (TOKENS, D), jnp.float32)
    groups = 1.5 * jax.random.normal(group_key, (group_rows, D), jnp.float32)
    result = base + spread_groups(groups)
    return jnp.clip(result, -150.0, 150.0).astype(jnp.bfloat16)


def draw_value_rows(key, part):
    key = jax.random.fold_in(key, 9)
    base_key, group_key = jax.random.split(key)
    group_rows = TOKENS // 2 ** (LEVELS - 1)
    base = jax.random.normal(base_key, (TOKENS, D), jnp.float32)
    groups = jax.random.normal(group_key, (group_rows, D), jnp.float32)
    return jnp.clip(base + spread_groups(groups), -8.0, 8.0).astype(jnp.bfloat16)


def draw_segment(key, part):
    key = jax.random.fold_in(key, 7)
    block_total = TOKENS // BLOCK
    offsets = jax.random.randint(key, (block_total,), 1, BLOCK, jnp.int32)
    offsets = offsets.at[3].set(offsets[1])
    position = jnp.arange(TOKENS, dtype=jnp.int32)
    block_of = position // BLOCK
    within = position % BLOCK
    before = jnp.maximum(block_of - 1, 0) - (block_of > 2).astype(jnp.int32)
    crossed = (block_of >= 1) & (block_of != 2) & (within >= jnp.take(offsets, block_of))
    return (before + crossed.astype(jnp.int32)).astype(jnp.int32)


def steps_of(stream_key, shape, shards, low, largest):
    def one(axis_at, parts):
        draws = jax.random.uniform(jax.random.fold_in(jax.random.fold_in(stream_key, 6), axis_at), (parts,), jnp.float32, low / len(shards), largest / len(shards))
        return jnp.repeat(jnp.exp(draws), shape[axis_at] // parts).reshape((-1,) + (1,) * (len(shape) - axis_at - 1))

    factor_of = one(*shards[0])
    for cut in shards[1:]:
        factor_of = factor_of * one(*cut)
    return factor_of


def scatter_about(rng, extent, spread, bound, pieces=(), kind=jnp.bfloat16):
    values = spread * jax.random.normal(rng, extent, jnp.float32)
    if pieces:
        values = values * steps_of(rng, extent, pieces, -0.22, 0.18)
    return jnp.clip(values, -bound, bound).astype(kind)


def setup_inputs(seed: int = 0) -> dict:
    key_of = jax.random.split(jax.random.key(seed), 6)
    query_rows = draw_query_rows(jax.random.fold_in(key_of[5], 71), 0)
    key_rows = draw_key_rows(jax.random.fold_in(key_of[5], 71), 0)
    value_rows = draw_value_rows(jax.random.fold_in(key_of[5], 71), 0)
    segment = draw_segment(jax.random.fold_in(key_of[5], 71), 0)
    w_out = scatter_about(key_of[4], (D, D), (D // 8) ** -0.5, 0.5, ((0, 4),))
    return dict(query_rows=query_rows, key_rows=key_rows, value_rows=value_rows, segment=segment, w_out=w_out)


NEG_FILL = -1e30


def block_attend(queries, key_block, value_block, allowed):
    scaling = HEAD_DIM ** -0.5
    scores = jnp.einsum('nqhd,nkhd->nhqk', queries.astype(jnp.float32), key_block.astype(jnp.float32)) * scaling
    mask_full = allowed[:, None]
    scores = jnp.where(mask_full, scores, NEG_FILL)
    peaks = jnp.max(scores, axis=-1)
    weights = jnp.where(mask_full, jnp.exp(scores - peaks[..., None]), 0.0)
    totals = jnp.sum(weights, axis=-1)
    rounded = lax.optimization_barrier(weights.astype(jnp.bfloat16)).astype(jnp.float32)
    weighted = jnp.einsum('nhqk,nkhd->nqhd', rounded, value_block.astype(jnp.float32))
    return jnp.swapaxes(peaks, 1, 2), jnp.swapaxes(totals, 1, 2), weighted


def level_terms(coarse_q, coarse_k, coarse_v, seg_pad, level):
    row_count = coarse_q.shape[0]
    block_count = row_count // BLOCK
    padding = ((BLOCK, BLOCK), (0, 0), (0, 0))
    keys_pad = jnp.pad(coarse_k, padding)
    values_pad = jnp.pad(coarse_v, padding)

    def single_block(block_index):
        first_row = (block_index * BLOCK).astype(jnp.int32)
        queries = lax.dynamic_slice_in_dim(coarse_q, first_row, BLOCK, 0)[None]
        key_block = lax.dynamic_slice_in_dim(keys_pad, first_row, 3 * BLOCK, 0)[None]
        value_block = lax.dynamic_slice_in_dim(values_pad, first_row, 3 * BLOCK, 0)[None]
        neighbour = block_index + jnp.arange(3, dtype=jnp.int32) - 1
        usable = (neighbour >= 0) & (neighbour < block_count)
        if level > 0:
            usable = usable & (jnp.arange(3) != 1)
        allowed = jnp.broadcast_to(jnp.repeat(usable, BLOCK)[None, :], (BLOCK, 3 * BLOCK))
        if level == 0:
            own_seg = lax.dynamic_slice_in_dim(seg_pad, first_row + BLOCK, BLOCK, 0)
            near_seg = lax.dynamic_slice_in_dim(seg_pad, first_row, 3 * BLOCK, 0)
            allowed = allowed & (own_seg[:, None] == near_seg[None, :])
        peaks, totals, weighted = block_attend(queries, key_block, value_block, allowed[None])
        return peaks[0], totals[0], weighted[0]

    peaks, totals, weighted = lax.map(single_block, jnp.arange(block_count, dtype=jnp.int32))
    return (peaks.reshape(row_count, HEADS), totals.reshape(row_count, HEADS),
            weighted.reshape(row_count, HEADS, HEAD_DIM))


def reference(query_rows, key_rows, value_rows, segment, w_out):
    shape_heads = (TOKENS, HEADS, HEAD_DIM)
    sources = (query_rows.reshape(shape_heads), key_rows.reshape(shape_heads), value_rows.reshape(shape_heads))
    seg_pad = jnp.pad(segment, (BLOCK, BLOCK), constant_values=-1)
    run_peak = None
    run_total = None
    run_sum = None
    for level in range(LEVELS):
        group = 2 ** level
        coarse = [jnp.mean(source.astype(jnp.float32).reshape(TOKENS // group, group, HEADS, HEAD_DIM), axis=1).astype(jnp.bfloat16) for source in sources]
        peaks, totals, weighted = level_terms(coarse[0], coarse[1], coarse[2], seg_pad, level)
        peaks = jnp.repeat(peaks, group, axis=0)
        totals = jnp.repeat(totals, group, axis=0)
        weighted = jnp.repeat(weighted, group, axis=0)
        if level == 0:
            run_peak, run_total, run_sum = peaks, totals, weighted
        else:
            new_peak = jnp.maximum(run_peak, peaks)
            old_scale = jnp.exp(run_peak - new_peak)
            new_scale = jnp.exp(peaks - new_peak)
            run_total = run_total * old_scale + totals * new_scale
            run_sum = run_sum * old_scale[..., None] + weighted * new_scale[..., None]
            run_peak = new_peak
    attention = (run_sum / run_total[..., None]).reshape(TOKENS, D).astype(jnp.bfloat16)
    return jnp.dot(attention, w_out, preferred_element_type=jnp.float32).astype(jnp.bfloat16)
```

```python
import jax
import jax.numpy as jnp
from jax import lax
from jax.experimental import pallas as pl
from jax.experimental.pallas import tpu as pltpu
from jax.sharding import PartitionSpec as P

MESH = pl.DeviceIdType.MESH
F32 = jnp.float32
BF16 = jnp.bfloat16

SEQ = 64
HEADX = 4
BLOCK = 256
ROWS = 1024
NEG = -1e30
BIG = 1e30

SEG_P, SEG_N, L0_P, L0_N, L1_P, L1_N, L2_P, L2_N = range(8)
KV3, KV4, KV5, Q3, RES3 = range(8, 13)
Q45, RES45, WG, WF, AT = 12, 15, 18, 21, 24
N_SEM = 28


def averaging():
    row = lax.broadcasted_iota(jnp.int32, (BLOCK, BLOCK), 0)
    token = lax.broadcasted_iota(jnp.int32, (BLOCK, BLOCK), 1)
    result = jnp.zeros((BLOCK, BLOCK), F32)
    base = 0
    for level in range(1, 6):
        count = BLOCK >> level
        first = (row - base) << level
        hit = (row >= base) & (row < base + count) & (token >= first) & (token < first + (1 << level))
        result = jnp.where(hit, 0.5**level, result)
        base += count
    return result.astype(BF16)


def scores_of(q, k):
    return lax.dot_general(q, k, (((1,), (1,)), ((), ())), preferred_element_type=F32)


def attend(q, keys, values, biases, present):
    scores = [scores_of(q, k) for k in keys]
    if biases is not None:
        scores = [s + b for s, b in zip(scores, biases)]
    tops = [jnp.max(s, axis=1, keepdims=True) for s in scores]
    if present is not None:
        tops = [jnp.where(ok, t, NEG) for ok, t in zip(present, tops)]
    peak = tops[0]
    for t in tops[1:]:
        peak = jnp.maximum(peak, t)
    total = None
    for index, (s, v) in enumerate(zip(scores, values)):
        shift = peak if present is None else jnp.where(present[index], peak, BIG)
        probs = jnp.exp(s - shift).astype(BF16)
        part = jnp.dot(probs, v, preferred_element_type=F32)
        total = part if total is None else total + part
    return total, peak


def pair(q, keys, values, biases, present, low_half, lo, hi):
    even, even_peak = attend(q * lo, keys, [v * lo + hi for v in values], biases, present)
    odd, odd_peak = attend(q * hi, keys, [v * hi + lo for v in values], biases, present)
    num = jnp.where(low_half, even, odd)
    total = pltpu.roll(jnp.where(low_half, odd, even), 64, 1)
    peak = jnp.where(low_half, even_peak, odd_peak)
    return num, total, peak


def merge(a, b):
    peak = jnp.maximum(a[2], b[2])
    scale_a, scale_b = jnp.exp(a[2] - peak), jnp.exp(b[2] - peak)
    return a[0] * scale_a + b[0] * scale_b, a[1] * scale_a + b[1] * scale_b, peak


def expand(parts, ref):
    count = parts[0].shape[0]
    for index, part in enumerate(parts):
        ref[index, pl.ds(0, count, stride=2), :] = part
        ref[index, pl.ds(1, count, stride=2), :] = part
    return tuple(ref[index, 0 : 2 * count, :] for index in range(3))


def kernel(
    q_hbm, k_hbm, v_hbm, seg_hbm, w_hbm, out_ref,
    q0, kv0, segi, segf, q1, kv1, q2, kv2,
    s3, r3, sq3, rq3, s4, r4, s5, r5, sq45, rq45,
    st0, st1, st2, st3, rs3, srow, rrow, ex, at, ra, wbuf,
    local, snd, rcv,
):
    i = lax.axis_index("seq")
    x = lax.axis_index("head")
    core = lax.rem(i, 2)
    chip = lax.div(i, 2)
    g4, a4 = lax.div(i, 4), lax.rem(i, 4)
    g5, a5 = lax.div(i, 8), lax.rem(i, 8)
    sibling = i + 1 - 2 * core
    right, left = lax.rem(i + 1, SEQ), lax.rem(i + SEQ - 1, SEQ)

    def remote(src, dst, slot, device):
        return pltpu.make_async_remote_copy(
            src_ref=src, dst_ref=dst, send_sem=snd.at[slot], recv_sem=rcv.at[slot], device_id=device, device_id_type=MESH
        )

    loads = []
    for p in range(2):
        lanes = pl.ds(128 * p, 128)
        loads.append(pltpu.make_async_copy(k_hbm.at[:, lanes], kv0.at[0, p, pl.ds(BLOCK, ROWS)], local.at[p]))
        loads.append(pltpu.make_async_copy(v_hbm.at[:, lanes], kv0.at[1, p, pl.ds(BLOCK, ROWS)], local.at[2 + p]))
        loads.append(pltpu.make_async_copy(q_hbm.at[:, lanes], q0.at[p], local.at[4 + p]))
    loads.append(pltpu.make_async_copy(seg_hbm, segi.at[1], local.at[6]))
    load_w = pltpu.make_async_copy(w_hbm, wbuf.at[x], local.at[7])
    for load in loads:
        load.start()
    load_w.start()

    barrier = pltpu.get_barrier_semaphore()

    def greet(seq, head):
        pl.semaphore_signal(barrier, inc=1, device_id={"seq": seq, "head": head}, device_id_type=MESH)

    blocks4 = [lax.rem(g4 + 1, SEQ // 4), lax.rem(g4 + SEQ // 4 - 1, SEQ // 4)]
    blocks5 = [lax.rem(g5 + 1, SEQ // 8), lax.rem(g5 + SEQ // 8 - 1, SEQ // 8)]
    for block in blocks5:
        for j in range(8):
            greet(block * 8 + j, x)
    for block in blocks4:
        for j in range(4):
            greet(block * 4 + j, x)
    for d in range(1, 4):
        greet(g4 * 4 + lax.rem(a4 + d, 4), x)
        greet(i, lax.rem(x + d, HEADX))

    lane = lax.broadcasted_iota(jnp.int32, (1, 128), 1)
    low_half = lane < 64
    lo_f = jnp.where(low_half, 1.0, 0.0).astype(F32)
    lo = lo_f.astype(BF16)
    hi = (1.0 - lo_f).astype(BF16)
    means = averaging()
    for load in loads:
        load.wait()
    last_k, last_v, last_q = [], [], []
    for t in range(4):
        rows = pl.ds(BLOCK + BLOCK * t, BLOCK)
        ck, cv = [
            jnp.dot(means, jnp.concatenate([kv0[n, 0, rows, :], kv0[n, 1, rows, :]], axis=1), preferred_element_type=F32)
            for n in range(2)
        ]
        own = pl.ds(BLOCK * t, BLOCK)
        cq = 0.125 * jnp.dot(means, jnp.concatenate([q0[0, own, :], q0[1, own, :]], axis=1), preferred_element_type=F32)
        for p in range(2):
            lanes = slice(128 * p, 128 * p + 128)
            q1[p, pl.ds(128 * t, 128), :] = cq[0:128, lanes].astype(BF16)
            q2[p, pl.ds(64 * t, 64), :] = cq[128:192, lanes].astype(BF16)
            sq3[p, pl.ds(32 * t, 32), :] = cq[192:224, lanes].astype(BF16)
            for n, c in enumerate((ck, cv)):
                kv1[n, p, pl.ds(BLOCK + 128 * t, 128), :] = c[0:128, lanes].astype(BF16)
                kv2[n, p, pl.ds(BLOCK + 64 * t, 64), :] = c[128:192, lanes].astype(BF16)
                s3[p, n, pl.ds(32 * t, 32), :] = c[192:224, lanes].astype(BF16)
        for h in range(4):
            s4[h, pl.ds(16 * t, 16), :] = packed(ck[224:240], cv[224:240], h, low_half).astype(BF16)
            sq45[h, pl.ds(16 * t, 16), :] = packed(cq[224:240], None, h, low_half).astype(BF16)
        last_k.append(ck[240:248])
        last_v.append(cv[240:248])
        last_q.append(cq[240:248])
    k5, v5, q5 = [jnp.concatenate(rows, axis=0) for rows in (last_k, last_v, last_q)]
    for h in range(4):
        s5[h] = packed(k5, v5, h, low_half).astype(BF16)
        sq45[h, pl.ds(64, 32), :] = packed(q5, None, h, low_half).astype(BF16)

    pl.semaphore_wait(barrier, 30)
    sends = []

    def send(src, dst, slot, seq, head=x):
        copy = remote(src, dst, slot, {"seq": seq, "head": head})
        copy.start()
        return copy

    half = pl.ds(128 * core, 128)
    for d in (1, 3, 2):
        sends.append(send(w_hbm.at[half], wbuf.at[x, half], WG + d, i, lax.rem(x + d, HEADX)))
    sends.append(send(sq3.at[1 - core], rq3.at[core], Q3, sibling))
    for d in range(1, 4):
        other = lax.rem(a4 + d, 4)
        sends.append(send(sq45.at[other], rq45.at[a4], Q45 + d, g4 * 4 + other))
    for direction, block in enumerate(blocks5):
        for j in range(8):
            send(s5.at[j % 4], r5.at[direction, a5], KV5, block * 8 + j)
    for direction, block in enumerate(blocks4):
        for j in range(4):
            send(s4.at[j], r4.at[direction, a4], KV4, block * 4 + j)
    for direction, by in enumerate((1, SEQ // 2 - 1)):
        beside = lax.rem(chip + by, SEQ // 2)
        for p in range(2):
            send(s3.at[p], r3.at[direction, :, core], KV3, beside * 2 + p)
    sends.append(send(segi.at[1], segi.at[0], SEG_P, right))
    sends.append(send(segi.at[1], segi.at[2], SEG_N, left))
    for ref, count, slot in ((kv2, 256, L2_P), (kv1, 512, L1_P), (kv0, 1024, L0_P)):
        sends.append(
            send(ref.at[:, :, pl.ds(count, BLOCK)], ref.at[:, :, pl.ds(0, BLOCK)], slot, right)
        )
        sends.append(
            send(ref.at[:, :, pl.ds(BLOCK, BLOCK)], ref.at[:, :, pl.ds(BLOCK + count, BLOCK)], slot + 1, left)
        )
    rq3[core] = sq3[core]
    rq45[a4] = sq45[a4]

    def received(ref, slot):
        pltpu.make_async_copy(ref, ref, rcv.at[slot]).wait()

    def sent(ref, slot):
        pltpu.make_async_copy(ref, ref, snd.at[slot]).wait()

    received(segi.at[0], SEG_P)
    received(segi.at[2], SEG_N)
    for n in range(3):
        segf[pl.ds(8 * n, 8), :] = segi[n].astype(F32)

    def bias_of(b, j):
        exists = (4 * i + b + j >= 1) & (4 * i + b + j <= 4 * SEQ)
        first = 6 + 2 * (b + j)
        return [jnp.where(exists, segf[pl.ds(first + n, 1), :], -1.0) for n in range(2)]

    def level0(b, p):
        queries = q0[p, pl.ds(pl.multiple_of(b * BLOCK, BLOCK), BLOCK), :] * jnp.asarray(0.125, BF16)
        own = [
            jnp.transpose(jnp.broadcast_to(segf[pl.ds(8 + 2 * b + n, 1), :], (128, 128))) for n in range(2)
        ]
        own = jnp.concatenate(own, axis=0)
        keys, values, biases = [], [], []
        for j in range(3):
            rows = pl.ds(pl.multiple_of((b + j) * BLOCK, BLOCK), BLOCK)
            keys.append(kv0[0, p, rows, :])
            values.append(kv0[1, p, rows, :])
            biases.append(
                jnp.concatenate([jnp.where(own == near, 0.0, NEG) for near in bias_of(b, j)], axis=1)
            )
        state = pair(queries, keys, values, biases, None, low_half, lo, hi)
        for n in range(3):
            st0[n, p, pl.ds(pl.multiple_of(b * BLOCK, BLOCK), BLOCK), :] = state[n]

    @pl.loop(0, 4)
    def _(u):
        level0(1 + lax.div(u, 2), lax.rem(u, 2))

    for d in (1, 3, 2):
        owner = lax.rem(x + HEADX - d, HEADX)
        received(wbuf.at[owner, half], WG + d)
        sends.append(send(wbuf.at[owner, half], wbuf.at[owner, half], WF + d, sibling))

    for d in range(1, 4):
        received(rq45.at[lax.rem(a4 + 4 - d, 4)], Q45 + d)

    def one_head(ref, queries, first, rows, place, count):
        block_rows = ref.shape[1] * ref.shape[2]
        tiles = [ref[n].reshape(block_rows, 128) for n in range(2)]
        out, peak = attend(queries, tiles, [t * hi + lo for t in tiles], None, (place > 0, place < count - 1))
        out = jnp.where((lane >= 32) & low_half, peak, out)
        for n in range(4):
            srow[n, pl.ds(first, rows), :] = out[n * rows : (n + 1) * rows]

    received(r5, KV5)
    one_head(r5, rq45[:, 64:96, :].reshape(128, 128), 64, 32, g5, SEQ // 8)
    received(r4, KV4)
    one_head(r4, rq45[:, 0:64, :].reshape(256, 128), 0, 64, g4, SEQ // 4)
    for d in range(1, 4):
        other = lax.rem(a4 + d, 4)
        sends.append(send(srow.at[other], rrow.at[a4], RES45 + d, g4 * 4 + other))
    rrow[a4] = srow[a4]

    received(r3, KV3)
    received(rq3.at[1 - core], Q3)
    state = pair(
        rq3[...].reshape(256, 128),
        [r3[n, 0].reshape(256, 128) for n in range(2)],
        [r3[n, 1].reshape(256, 128) for n in range(2)],
        None,
        (chip > 0, chip < SEQ // 2 - 1),
        low_half, lo, hi,
    )
    for n in range(3):
        for m in range(2):
            rs3[m, n] = state[n][128 * m : 128 * m + 128]
    sends.append(send(rs3.at[1 - core], st3.at[core], RES3, sibling))
    st3[core] = rs3[core]

    received(kv2.at[:, :, pl.ds(0, BLOCK)], L2_P)
    received(kv2.at[:, :, pl.ds(2 * BLOCK, BLOCK)], L2_N)

    @pl.loop(0, 2)
    def _(p):
        sides = [pl.ds(0, BLOCK), pl.ds(2 * BLOCK, BLOCK)]
        state = pair(
            q2[p], [kv2[0, p, s, :] for s in sides], [kv2[1, p, s, :] for s in sides],
            None, (i > 0, i < SEQ - 1), low_half, lo, hi,
        )
        for n in range(3):
            st2[n, p] = state[n]

    received(kv1.at[:, :, pl.ds(0, BLOCK)], L1_P)
    received(kv1.at[:, :, pl.ds(3 * BLOCK, BLOCK)], L1_N)

    @pl.loop(0, 4)
    def _(u):
        b, p = lax.div(u, 2), lax.rem(u, 2)
        own = pl.ds(pl.multiple_of(b * BLOCK, BLOCK), BLOCK)
        sides = [own, pl.ds(pl.multiple_of((b + 2) * BLOCK, BLOCK), BLOCK)]
        place = 2 * i + b
        state = pair(
            q1[p, own, :], [kv1[0, p, s, :] for s in sides], [kv1[1, p, s, :] for s in sides],
            None, (place > 0, place < 2 * SEQ - 1), low_half, lo, hi,
        )
        for n in range(3):
            st1[n, p, own, :] = state[n]

    for d in range(1, 4):
        received(rrow.at[lax.rem(a4 + 4 - d, 4)], RES45 + d)
    received(st3.at[1 - core], RES3)
    for p in range(2):

        def far(rows):
            even, odd = rrow[2 * p, rows, :], rrow[2 * p + 1, rows, :]
            num = jnp.where(low_half, pltpu.roll(even, 64, 1), odd)
            total = jnp.where(low_half, even[:, 0:1], odd[:, 0:1])
            return num, total, jnp.where(low_half, even[:, 32:33], odd[:, 32:33])

        state = merge(expand(far(slice(64, 96)), ex), far(slice(0, 64)))
        state = merge(expand(state, ex), tuple(st3[p, n] for n in range(3)))
        state = merge(expand(state, ex), tuple(st2[n, p] for n in range(3)))
        state = merge(expand(state, ex), tuple(st1[n, p] for n in range(3)))
        for n in range(3):
            st1[n, p] = state[n]

    def finish(t):
        for p in range(2):
            coarse = expand(tuple(st1[n, p, pl.ds(128 * t, 128), :] for n in range(3)), ex)
            num, total, _ = merge(tuple(st0[n, p, pl.ds(BLOCK * t, BLOCK), :] for n in range(3)), coarse)
            at[t, :, 128 * p : 128 * p + 128] = (num / total).astype(BF16)

        @pl.when(x == t)
        def _():
            ra[t] = at[t]

        @pl.when(x != t)
        def _():
            d = lax.rem(t + HEADX - x, HEADX)
            send(at.at[t], ra.at[x], AT + d, i, t)

    finish(1)
    finish(2)

    received(kv0.at[:, :, pl.ds(0, BLOCK)], L0_P)
    received(kv0.at[:, :, pl.ds(5 * BLOCK, BLOCK)], L0_N)

    @pl.loop(0, 4)
    def _(u):
        level0(3 * lax.div(u, 2), lax.rem(u, 2))

    finish(0)
    finish(3)

    load_w.wait()
    for d in range(1, 4):
        received(wbuf.at[lax.rem(x + HEADX - d, HEADX), pl.ds(128 * (1 - core), 128)], WF + d)
    for d in range(1, 4):
        received(ra.at[lax.rem(x + HEADX - d, HEADX)], AT + d)
    for n in range(4):
        columns = pl.ds(256 * n, 256)
        total = jnp.dot(ra[0], wbuf[0, :, columns], preferred_element_type=F32)
        for m in range(1, 4):
            total += jnp.dot(ra[m], wbuf[m, :, columns], preferred_element_type=F32)
        out_ref[:, columns] = total.astype(BF16)

    for copy in sends:
        copy.wait_send()
    sent(r5, KV5)
    sent(r4, KV4)
    sent(r3, KV3)
    for d in range(1, 4):
        sent(at.at[lax.rem(x + d, HEADX)], AT + d)


def packed(first, second, h, low_half):
    lanes = slice(128 * (h // 2), 128 * (h // 2) + 128)
    first = first[:, lanes]
    if h % 2:
        first = pltpu.roll(first, 64, 1)
    if second is None:
        return jnp.where(low_half, first, 0.0)
    second = second[:, lanes]
    if h % 2 == 0:
        second = pltpu.roll(second, 64, 1)
    return jnp.where(low_half, first, second)


def on_device(query_rows, key_rows, value_rows, segment, w_out):
    vmem = pltpu.VMEM
    return pl.pallas_call(
        kernel,
        out_shape=jax.ShapeDtypeStruct((BLOCK, 1024), BF16),
        in_specs=[pl.BlockSpec(memory_space=pl.ANY)] * 5,
        out_specs=pl.BlockSpec(memory_space=vmem),
        scratch_shapes=[
            vmem((2, ROWS, 128), BF16),
            vmem((2, 2, ROWS + 512, 128), BF16),
            vmem((3, 8, 128), jnp.int32),
            vmem((24, 128), F32),
            vmem((2, 512, 128), BF16),
            vmem((2, 2, 1024, 128), BF16),
            vmem((2, 256, 128), BF16),
            vmem((2, 2, 768, 128), BF16),
            vmem((2, 2, 128, 128), BF16),
            vmem((2, 2, 2, 128, 128), BF16),
            vmem((2, 128, 128), BF16),
            vmem((2, 128, 128), BF16),
            vmem((4, 64, 128), BF16),
            vmem((2, 4, 64, 128), BF16),
            vmem((4, 32, 128), BF16),
            vmem((2, 8, 32, 128), BF16),
            vmem((4, 96, 128), BF16),
            vmem((4, 96, 128), BF16),
            vmem((3, 2, ROWS, 128), F32),
            vmem((3, 2, 512, 128), F32),
            vmem((3, 2, 256, 128), F32),
            vmem((2, 3, 128, 128), F32),
            vmem((2, 3, 128, 128), F32),
            vmem((4, 96, 128), F32),
            vmem((4, 96, 128), F32),
            vmem((3, 512, 128), F32),
            vmem((4, BLOCK, 256), BF16),
            vmem((4, BLOCK, 256), BF16),
            vmem((4, 256, 1024), BF16),
            pltpu.SemaphoreType.DMA((8,)),
            pltpu.SemaphoreType.DMA((N_SEM,)),
            pltpu.SemaphoreType.DMA((N_SEM,)),
        ],
        compiler_params=pltpu.CompilerParams(
            collective_id=0, has_side_effects=True, vmem_limit_bytes=48 * 2**20
        ),
        name="block_attention",
    )(query_rows, key_rows, value_rows, segment.reshape(8, 128), w_out)


def solution(mesh):
    placed = (P("seq", "head"), P("seq", "head"), P("seq", "head"), P("seq"), P("head", None))
    return jax.shard_map(
        on_device, mesh=mesh, in_specs=placed, out_specs=P(("seq", "head"), None), check_vma=False
    )
```

```python
import jax
import jax.numpy as jnp
from jax import lax
from jax.experimental import pallas as pl
from jax.experimental.pallas import tpu as pltpu
from jax.sharding import PartitionSpec as P

MESH = pl.DeviceIdType.MESH
F32 = jnp.float32
BF16 = jnp.bfloat16

SEQ = 64
HEADX = 4
BLOCK = 256
ROWS = 1024
NEG = -1e30
BIG = 1e30

SEG_P, SEG_N, L0_P, L0_N, L1_P, L1_N, L2_P, L2_N = range(8)
KV3, KV4, KV5, KV5_Y, Q3, Q5, RES3, RES5 = range(8, 16)
Q4, RES4 = 15, 18
W_L, W_R, W2_L, W2_R, W_ON_L, W_ON_R, W_ON_2 = range(22, 29)
AT_L, AT_R, VIA, AT_2 = 29, 31, 33, 35
N_SEM = 37

OWNER5 = (0, 1, 6, 7)


def averaging():
    row = lax.broadcasted_iota(jnp.int32, (BLOCK, BLOCK), 0)
    token = lax.broadcasted_iota(jnp.int32, (BLOCK, BLOCK), 1)
    result = jnp.zeros((BLOCK, BLOCK), F32)
    base = 0
    for level in range(1, 6):
        count = BLOCK >> level
        first = (row - base) << level
        hit = (row >= base) & (row < base + count) & (token >= first) & (token < first + (1 << level))
        result = jnp.where(hit, 0.5**level, result)
        base += count
    return result.astype(BF16)


def scores_of(q, k):
    return lax.dot_general(q, k, (((1,), (1,)), ((), ())), preferred_element_type=F32)


def attend(q, keys, values, biases, present):
    scores = [scores_of(q, k) for k in keys]
    if biases is not None:
        scores = [s + b for s, b in zip(scores, biases)]
    tops = [jnp.max(s, axis=1, keepdims=True) for s in scores]
    if present is not None:
        tops = [jnp.where(ok, t, NEG) for ok, t in zip(present, tops)]
    peak = tops[0]
    for t in tops[1:]:
        peak = jnp.maximum(peak, t)
    total = None
    for index, (s, v) in enumerate(zip(scores, values)):
        shift = peak if present is None else jnp.where(present[index], peak, BIG)
        probs = jnp.exp(s - shift).astype(BF16)
        part = jnp.dot(probs, v, preferred_element_type=F32)
        total = part if total is None else total + part
    return total, peak


def pair(q, keys, values, biases, present, low_half, lo, hi):
    even, even_peak = attend(q * lo, keys, [v * lo + hi for v in values], biases, present)
    odd, odd_peak = attend(q * hi, keys, [v * hi + lo for v in values], biases, present)
    num = jnp.where(low_half, even, odd)
    total = pltpu.roll(jnp.where(low_half, odd, even), 64, 1)
    peak = jnp.where(low_half, even_peak, odd_peak)
    return num, total, peak


def merge(a, b):
    peak = jnp.maximum(a[2], b[2])
    scale_a, scale_b = jnp.exp(a[2] - peak), jnp.exp(b[2] - peak)
    return a[0] * scale_a + b[0] * scale_b, a[1] * scale_a + b[1] * scale_b, peak


def expand(parts, ref):
    count = parts[0].shape[0]
    for index, part in enumerate(parts):
        ref[index, pl.ds(0, count, stride=2), :] = part
        ref[index, pl.ds(1, count, stride=2), :] = part
    return tuple(ref[index, 0 : 2 * count, :] for index in range(3))


def kernel(
    q_hbm, k_hbm, v_hbm, seg_hbm, w_hbm, out_ref,
    q0, kv0, segi, segf, q1, kv1, q2, kv2,
    s3, r3, sq3, rq3, s4, r4, s5, r5, sq4, rq4, sq5, rq5,
    st0, st1, st2, st3, rs3, srow4, rrow4, srow5, rrow5, ex, at, ra, via, wbuf,
    local, snd, rcv,
):
    i = lax.axis_index("seq")
    x = lax.axis_index("head")
    core = lax.rem(i, 2)
    chip = lax.div(i, 2)
    g4, a4 = lax.div(i, 4), lax.rem(i, 4)
    g5, a5 = lax.div(i, 8), lax.rem(i, 8)
    sibling = i + 1 - 2 * core
    right, left = lax.rem(i + 1, SEQ), lax.rem(i + SEQ - 1, SEQ)
    x_up, x_down, x_far = [lax.rem(x + d, HEADX) for d in (1, 3, 2)]
    late = lax.rem(g5, 2)
    beside5 = g5 + 1 - 2 * late
    owner5 = (a5 < 2) | (a5 >= 6)
    head5 = jnp.where(a5 < 2, a5, lax.rem(a5, 4))
    y_on = lax.rem(i + SEQ + 16 - 32 * late, SEQ)

    def remote(src, dst, slot, device):
        return pltpu.make_async_remote_copy(
            src_ref=src, dst_ref=dst, send_sem=snd.at[slot], recv_sem=rcv.at[slot], device_id=device, device_id_type=MESH
        )

    loads = []
    for p in range(2):
        lanes = pl.ds(128 * p, 128)
        loads.append(pltpu.make_async_copy(k_hbm.at[:, lanes], kv0.at[0, p, pl.ds(BLOCK, ROWS)], local.at[p]))
        loads.append(pltpu.make_async_copy(v_hbm.at[:, lanes], kv0.at[1, p, pl.ds(BLOCK, ROWS)], local.at[2 + p]))
        loads.append(pltpu.make_async_copy(q_hbm.at[:, lanes], q0.at[p], local.at[4 + p]))
    loads.append(pltpu.make_async_copy(seg_hbm, segi.at[1], local.at[6]))
    load_w = pltpu.make_async_copy(w_hbm, wbuf.at[x], local.at[7])
    for load in loads:
        load.start()
    load_w.start()

    barrier = pltpu.get_barrier_semaphore()

    def greet(seq, head):
        pl.semaphore_signal(barrier, inc=1, device_id={"seq": seq, "head": head}, device_id_type=MESH)

    blocks4 = [lax.rem(g4 + 1, SEQ // 4), lax.rem(g4 + SEQ // 4 - 1, SEQ // 4)]
    for j in range(8):
        greet(beside5 * 8 + j, x)
    for block in blocks4:
        for j in range(4):
            greet(block * 4 + j, x)
    for d in range(1, 8):
        greet(g5 * 8 + lax.rem(a5 + d, 8), x)
    for other in (x_up, x_down):
        greet(i, other)
    greet(lax.rem(i + 16, SEQ), x)
    greet(lax.rem(i + SEQ - 16, SEQ), x)

    lane = lax.broadcasted_iota(jnp.int32, (1, 128), 1)
    low_half = lane < 64
    lo_f = jnp.where(low_half, 1.0, 0.0).astype(F32)
    lo = lo_f.astype(BF16)
    hi = (1.0 - lo_f).astype(BF16)
    means = averaging()
    for load in loads:
        load.wait()
    last_k, last_v, last_q = [], [], []
    for t in range(4):
        rows = pl.ds(BLOCK + BLOCK * t, BLOCK)
        ck, cv = [
            jnp.dot(means, jnp.concatenate([kv0[n, 0, rows, :], kv0[n, 1, rows, :]], axis=1), preferred_element_type=F32)
            for n in range(2)
        ]
        own = pl.ds(BLOCK * t, BLOCK)
        cq = 0.125 * jnp.dot(means, jnp.concatenate([q0[0, own, :], q0[1, own, :]], axis=1), preferred_element_type=F32)
        for p in range(2):
            lanes = slice(128 * p, 128 * p + 128)
            q1[p, pl.ds(128 * t, 128), :] = cq[0:128, lanes].astype(BF16)
            q2[p, pl.ds(64 * t, 64), :] = cq[128:192, lanes].astype(BF16)
            sq3[p, pl.ds(32 * t, 32), :] = cq[192:224, lanes].astype(BF16)
            for n, c in enumerate((ck, cv)):
                kv1[n, p, pl.ds(BLOCK + 128 * t, 128), :] = c[0:128, lanes].astype(BF16)
                kv2[n, p, pl.ds(BLOCK + 64 * t, 64), :] = c[128:192, lanes].astype(BF16)
                s3[p, n, pl.ds(32 * t, 32), :] = c[192:224, lanes].astype(BF16)
        for h in range(4):
            s4[h, pl.ds(16 * t, 16), :] = packed(ck[224:240], cv[224:240], h, low_half).astype(BF16)
            sq4[h, pl.ds(16 * t, 16), :] = packed(cq[224:240], None, h, low_half).astype(BF16)
        last_k.append(ck[240:248])
        last_v.append(cv[240:248])
        last_q.append(cq[240:248])
    k5, v5, q5 = [jnp.concatenate(rows, axis=0) for rows in (last_k, last_v, last_q)]
    for h in range(4):
        s5[h] = packed(k5, v5, h, low_half).astype(BF16)
        sq5[h] = packed(q5, None, h, low_half).astype(BF16)

    segf[pl.ds(8, 8), :] = segi[1].astype(F32)

    def bias_of(b, j):
        exists = (4 * i + b + j >= 1) & (4 * i + b + j <= 4 * SEQ)
        first = 6 + 2 * (b + j)
        return [jnp.where(exists, segf[pl.ds(first + n, 1), :], -1.0) for n in range(2)]

    def level0(b, p):
        queries = q0[p, pl.ds(pl.multiple_of(b * BLOCK, BLOCK), BLOCK), :] * jnp.asarray(0.125, BF16)
        own = [
            jnp.transpose(jnp.broadcast_to(segf[pl.ds(8 + 2 * b + n, 1), :], (128, 128))) for n in range(2)
        ]
        own = jnp.concatenate(own, axis=0)
        keys, values, biases = [], [], []
        for j in range(3):
            rows = pl.ds(pl.multiple_of((b + j) * BLOCK, BLOCK), BLOCK)
            keys.append(kv0[0, p, rows, :])
            values.append(kv0[1, p, rows, :])
            biases.append(
                jnp.concatenate([jnp.where(own == near, 0.0, NEG) for near in bias_of(b, j)], axis=1)
            )
        state = pair(queries, keys, values, biases, None, low_half, lo, hi)
        for n in range(3):
            st0[n, p, pl.ds(pl.multiple_of(b * BLOCK, BLOCK), BLOCK), :] = state[n]

    @pl.when(late == 0)
    def _():
        @pl.loop(0, 4)
        def _(u):
            level0(1 + lax.div(u, 2), lax.rem(u, 2))

    pl.semaphore_wait(barrier, 27)
    sends = []

    def send(src, dst, slot, seq, head=x):
        copy = remote(src, dst, slot, {"seq": seq, "head": head})
        copy.start()
        return copy

    def received(ref, slot):
        pltpu.make_async_copy(ref, ref, rcv.at[slot]).wait()

    def sent(ref, slot):
        pltpu.make_async_copy(ref, ref, snd.at[slot]).wait()

    def to_sides(ref, count, skip, slot):
        n = BLOCK - skip
        sends.append(send(ref.at[:, :, pl.ds(count, n)], ref.at[:, :, pl.ds(0, n)], slot, right))
        sends.append(
            send(
                ref.at[:, :, pl.ds(BLOCK + skip, n)], ref.at[:, :, pl.ds(BLOCK + count + skip, n)], slot + 1, left
            )
        )

    half = pl.ds(128 * core, 128)
    sends.append(send(w_hbm.at[half], wbuf.at[x, half], W_L, i, x_up))
    sends.append(send(w_hbm.at[half], wbuf.at[x, half], W_R, i, x_down))
    for h in range(4):
        send(s5.at[h], r5.at[late, a5], KV5, beside5 * 8 + OWNER5[h])

        @pl.when(a5 != OWNER5[h])
        def _():
            send(sq5.at[h], rq5.at[a5], Q5, g5 * 8 + OWNER5[h])

        @pl.when(a5 == OWNER5[h])
        def _():
            rq5[a5] = sq5[h]

    for direction, block in enumerate(blocks4):
        for j in range(4):
            send(s4.at[j], r4.at[direction, a4], KV4, block * 4 + j)
    for d in range(1, 4):
        other = lax.rem(a4 + d, 4)
        sends.append(send(sq4.at[other], rq4.at[a4], Q4 + d, g4 * 4 + other))
    sends.append(send(sq3.at[1 - core], rq3.at[core], Q3, sibling))
    for direction, by in enumerate((1, SEQ // 2 - 1)):
        beside = lax.rem(chip + by, SEQ // 2)
        for p in range(2):
            send(s3.at[p], r3.at[direction, :, core], KV3, beside * 2 + p)
    sends.append(send(segi.at[1], segi.at[0], SEG_P, right))
    sends.append(send(segi.at[1], segi.at[2], SEG_N, left))
    to_sides(kv0, ROWS, 0, L0_P)
    to_sides(kv2, 256, 64, L2_P)
    to_sides(kv1, 512, 128, L1_P)
    rq3[core] = sq3[core]
    rq4[a4] = sq4[a4]

    @pl.when(late == 1)
    def _():
        @pl.loop(0, 4)
        def _(u):
            level0(1 + lax.div(u, 2), lax.rem(u, 2))

    @pl.when(owner5)
    def _():
        received(r5.at[1 - late], KV5)
        send(r5.at[1 - late], r5.at[late], KV5_Y, y_on)

    quarter = [pl.ds(128 * core, 64), pl.ds(128 * core + 64, 64)]
    received(wbuf.at[x_down, half], W_L)
    sends.append(send(wbuf.at[x_down, quarter[0]], wbuf.at[x_down, quarter[0]], W2_L, i, x_up))
    sends.append(send(wbuf.at[x_down, half], wbuf.at[x_down, half], W_ON_L, sibling))
    received(wbuf.at[x_up, half], W_R)
    sends.append(send(wbuf.at[x_up, quarter[1]], wbuf.at[x_up, quarter[1]], W2_R, i, x_down))
    sends.append(send(wbuf.at[x_up, half], wbuf.at[x_up, half], W_ON_R, sibling))

    def one_head(ref, queries, place, count):
        tiles = [ref[n].reshape(BLOCK, 128) for n in range(2)]
        out, peak = attend(queries, tiles, [t * hi + lo for t in tiles], None, (place > 0, place < count - 1))
        return jnp.where((lane >= 32) & low_half, peak, out)

    for d in range(1, 4):
        received(rq4.at[lax.rem(a4 + 4 - d, 4)], Q4 + d)
    received(r4, KV4)
    srow4[...] = one_head(r4, rq4[...].reshape(BLOCK, 128), g4, SEQ // 4).reshape(4, 64, 128)
    for d in range(1, 4):
        other = lax.rem(a4 + d, 4)
        sends.append(send(srow4.at[other], rrow4.at[a4], RES4 + d, g4 * 4 + other))
    rrow4[a4] = srow4[a4]

    @pl.when(owner5)
    def _():
        received(rq5.at[pl.ds(0, 7)], Q5)
        received(r5.at[late], KV5_Y)
        srow5[...] = one_head(r5, rq5[...].reshape(BLOCK, 128), g5, SEQ // 8).reshape(8, 32, 128)
        for d in range(1, 8):
            other = lax.rem(a5 + d, 8)
            send(srow5.at[other], rrow5.at[head5], RES5, g5 * 8 + other)
        rrow5[head5] = srow5[a5]

    received(r3, KV3)
    received(rq3.at[1 - core], Q3)
    state = pair(
        rq3[...].reshape(BLOCK, 128),
        [r3[n, 0].reshape(BLOCK, 128) for n in range(2)],
        [r3[n, 1].reshape(BLOCK, 128) for n in range(2)],
        None,
        (chip > 0, chip < SEQ // 2 - 1),
        low_half, lo, hi,
    )
    for n in range(3):
        for m in range(2):
            rs3[m, n] = state[n][128 * m : 128 * m + 128]
    sends.append(send(rs3.at[1 - core], st3.at[core], RES3, sibling))
    st3[core] = rs3[core]

    received(segi.at[0], SEG_P)
    received(segi.at[2], SEG_N)
    segf[pl.ds(0, 8), :] = segi[0].astype(F32)
    segf[pl.ds(16, 8), :] = segi[2].astype(F32)
    for side, (first, row1, row2) in enumerate(((0, 128, 192), (5 * BLOCK, 3 * BLOCK, 2 * BLOCK))):
        received(kv0.at[:, :, pl.ds(first, BLOCK)], L0_P + side)
        for n in range(2):
            rim = jnp.concatenate([kv0[n, p, pl.ds(first, BLOCK), :] for p in range(2)], axis=1)
            rim = jnp.dot(means[:192], rim, preferred_element_type=F32).astype(BF16)
            for p in range(2):
                kv1[n, p, pl.ds(row1, 128), :] = rim[:128, 128 * p : 128 * p + 128]
                kv2[n, p, pl.ds(row2, 64), :] = rim[128:, 128 * p : 128 * p + 128]

    received(kv2.at[:, :, pl.ds(0, 192)], L2_P)
    received(kv2.at[:, :, pl.ds(2 * BLOCK + 64, 192)], L2_N)

    @pl.loop(0, 2)
    def _(p):
        sides = [pl.ds(0, BLOCK), pl.ds(2 * BLOCK, BLOCK)]
        state = pair(
            q2[p], [kv2[0, p, s, :] for s in sides], [kv2[1, p, s, :] for s in sides],
            None, (i > 0, i < SEQ - 1), low_half, lo, hi,
        )
        for n in range(3):
            st2[n, p] = state[n]

    received(kv1.at[:, :, pl.ds(0, 128)], L1_P)
    received(kv1.at[:, :, pl.ds(3 * BLOCK + 128, 128)], L1_N)

    @pl.loop(0, 4)
    def _(u):
        b, p = lax.div(u, 2), lax.rem(u, 2)
        own = pl.ds(pl.multiple_of(b * BLOCK, BLOCK), BLOCK)
        sides = [own, pl.ds(pl.multiple_of((b + 2) * BLOCK, BLOCK), BLOCK)]
        place = 2 * i + b
        state = pair(
            q1[p, own, :], [kv1[0, p, s, :] for s in sides], [kv1[1, p, s, :] for s in sides],
            None, (place > 0, place < 2 * SEQ - 1), low_half, lo, hi,
        )
        for n in range(3):
            st1[n, p, own, :] = state[n]

    received(wbuf.at[x_far, quarter[0]], W2_L)
    received(wbuf.at[x_far, quarter[1]], W2_R)
    sends.append(send(wbuf.at[x_far, half], wbuf.at[x_far, half], W_ON_2, sibling))

    for d in range(1, 4):
        received(rrow4.at[lax.rem(a4 + 4 - d, 4)], RES4 + d)

    @pl.when(owner5)
    def _():
        received(rrow5.at[pl.ds(0, 3)], RES5)

    @pl.when(jnp.logical_not(owner5))
    def _():
        received(rrow5, RES5)

    received(st3.at[1 - core], RES3)
    for p in range(2):

        def far(ref):
            even, odd = ref[2 * p], ref[2 * p + 1]
            num = jnp.where(low_half, pltpu.roll(even, 64, 1), odd)
            total = jnp.where(low_half, even[:, 0:1], odd[:, 0:1])
            return num, total, jnp.where(low_half, even[:, 32:33], odd[:, 32:33])

        state = merge(expand(far(rrow5), ex), far(rrow4))
        state = merge(expand(state, ex), tuple(st3[p, n] for n in range(3)))
        state = merge(expand(state, ex), tuple(st2[n, p] for n in range(3)))
        state = merge(expand(state, ex), tuple(st1[n, p] for n in range(3)))
        for n in range(3):
            st1[n, p] = state[n]

    def finish(t, p):
        coarse = expand(tuple(st1[n, p, pl.ds(pl.multiple_of(128 * t, 128), 128), :] for n in range(3)), ex)
        fine = tuple(st0[n, p, pl.ds(pl.multiple_of(BLOCK * t, BLOCK), BLOCK), :] for n in range(3))
        num, total, _ = merge(fine, coarse)
        attention = (num / total).astype(BF16)
        d = lax.rem(t + HEADX - x, HEADX)
        at[t, p] = attention

        @pl.when(d == 0)
        def _():
            ra[x, p] = attention

        @pl.when(d == 1)
        def _():
            send(at.at[t, p], ra.at[x, p], AT_L + p, i, x_up)

        @pl.when(d == 3)
        def _():
            send(at.at[t, p], ra.at[x, p], AT_R + p, i, x_down)

        @pl.when(d == 2)
        def _():
            send(at.at[t, p], via.at[p], VIA + p, i, x_down if p else x_up)

    for t in (1, 2):
        for p in range(2):
            finish(t, p)

    first = jnp.where(x < 2, 3, 0)
    for t in (first, 3 - first):
        for p in range(2):
            level0(t, p)
            finish(t, p)
    received(via.at[0], VIA)
    sends.append(send(via.at[0], ra.at[x_down, 0], AT_2, i, x_up))
    received(via.at[1], VIA + 1)
    sends.append(send(via.at[1], ra.at[x_up, 1], AT_2 + 1, i, x_down))

    load_w.wait()
    other_half = pl.ds(128 * (1 - core), 128)
    for owner, slot in ((x_down, W_ON_L), (x_up, W_ON_R), (x_far, W_ON_2)):
        received(wbuf.at[owner, other_half], slot)
    for p in range(2):
        for owner, slot in ((x_down, AT_L), (x_up, AT_R), (x_far, AT_2)):
            received(ra.at[owner, p], slot + p)
    for n in range(4):
        columns = pl.ds(256 * n, 256)
        total = None
        for m in range(4):
            rows = jnp.concatenate([ra[m, 0], ra[m, 1]], axis=1)
            part = jnp.dot(rows, wbuf[m, :, columns], preferred_element_type=F32)
            total = part if total is None else total + part
        out_ref[:, columns] = total.astype(BF16)

    for copy in sends:
        copy.wait_send()
    sent(s5, KV5)
    for h in range(4):

        @pl.when(a5 != OWNER5[h])
        def _():
            sent(sq5.at[h], Q5)

    @pl.when(owner5)
    def _():
        sent(r5.at[0], KV5_Y)
        sent(srow5.at[pl.ds(0, 7)], RES5)

    sent(r4, KV4)
    sent(r3, KV3)
    for p in range(2):
        for slot in (AT_L, AT_R, VIA):
            sent(at.at[0, p], slot + p)


def packed(first, second, h, low_half):
    lanes = slice(128 * (h // 2), 128 * (h // 2) + 128)
    first = first[:, lanes]
    if h % 2:
        first = pltpu.roll(first, 64, 1)
    if second is None:
        return jnp.where(low_half, first, 0.0)
    second = second[:, lanes]
    if h % 2 == 0:
        second = pltpu.roll(second, 64, 1)
    return jnp.where(low_half, first, second)


def on_device(query_rows, key_rows, value_rows, segment, w_out):
    vmem = pltpu.VMEM
    return pl.pallas_call(
        kernel,
        out_shape=jax.ShapeDtypeStruct((BLOCK, 1024), BF16),
        in_specs=[pl.BlockSpec(memory_space=pl.ANY)] * 5,
        out_specs=pl.BlockSpec(memory_space=vmem),
        scratch_shapes=[
            vmem((2, ROWS, 128), BF16),
            vmem((2, 2, ROWS + 512, 128), BF16),
            vmem((3, 8, 128), jnp.int32),
            vmem((24, 128), F32),
            vmem((2, 512, 128), BF16),
            vmem((2, 2, 1024, 128), BF16),
            vmem((2, 256, 128), BF16),
            vmem((2, 2, 768, 128), BF16),
            vmem((2, 2, 128, 128), BF16),
            vmem((2, 2, 2, 128, 128), BF16),
            vmem((2, 128, 128), BF16),
            vmem((2, 128, 128), BF16),
            vmem((4, 64, 128), BF16),
            vmem((2, 4, 64, 128), BF16),
            vmem((4, 32, 128), BF16),
            vmem((2, 8, 32, 128), BF16),
            vmem((4, 64, 128), BF16),
            vmem((4, 64, 128), BF16),
            vmem((4, 32, 128), BF16),
            vmem((8, 32, 128), BF16),
            vmem((3, 2, ROWS, 128), F32),
            vmem((3, 2, 512, 128), F32),
            vmem((3, 2, 256, 128), F32),
            vmem((2, 3, 128, 128), F32),
            vmem((2, 3, 128, 128), F32),
            vmem((4, 64, 128), F32),
            vmem((4, 64, 128), F32),
            vmem((8, 32, 128), F32),
            vmem((4, 32, 128), F32),
            vmem((3, 512, 128), F32),
            vmem((4, 2, BLOCK, 128), BF16),
            vmem((4, 2, BLOCK, 128), BF16),
            vmem((2, BLOCK, 128), BF16),
            vmem((4, 256, 1024), BF16),
            pltpu.SemaphoreType.DMA((8,)),
            pltpu.SemaphoreType.DMA((N_SEM,)),
            pltpu.SemaphoreType.DMA((N_SEM,)),
        ],
        compiler_params=pltpu.CompilerParams(
            collective_id=0, has_side_effects=True, vmem_limit_bytes=62 * 2**20
        ),
        name="block_attention",
    )(query_rows, key_rows, value_rows, segment.reshape(8, 128), w_out)


def solution(mesh):
    placed = (P("seq", "head"), P("seq", "head"), P("seq", "head"), P("seq"), P("head", None))
    return jax.shard_map(
        on_device, mesh=mesh, in_specs=placed, out_specs=P(("seq", "head"), None), check_vma=False
    )
```

```python
import jax
import jax.numpy as jnp
from jax import lax
from jax.experimental import pallas as pl
from jax.experimental.pallas import tpu as pltpu
from jax.sharding import PartitionSpec as P

MESH = pl.DeviceIdType.MESH
F32 = jnp.float32
BF16 = jnp.bfloat16

SEQ = 64
HEADX = 4
BLOCK = 256
ROWS = 1024
NEG = -1e30
BIG = 1e30

SEG_P, SEG_N, L0_P, L0_N, L1_P, L1_N, L2_P, L2_N = range(8)
KV3, KV4, KV5, KV5_Y, Q3, Q5, RES3, RES5 = range(8, 16)
Q4, RES4 = 15, 18
W_L, W_R, W2_L, W2_R, W_ON_L, W_ON_R, W_ON_2 = range(22, 29)
AT_L, AT_R, VIA, AT_2 = 29, 31, 33, 35
STAT, FAR = 36, 39
N_SEM = 43

OWNER5 = (0, 1, 6, 7)


def averaging():
    row = lax.broadcasted_iota(jnp.int32, (BLOCK, BLOCK), 0)
    token = lax.broadcasted_iota(jnp.int32, (BLOCK, BLOCK), 1)
    result = jnp.zeros((BLOCK, BLOCK), F32)
    base = 0
    for level in range(1, 6):
        count = BLOCK >> level
        first = (row - base) << level
        hit = (row >= base) & (row < base + count) & (token >= first) & (token < first + (1 << level))
        result = jnp.where(hit, 0.5**level, result)
        base += count
    return result.astype(BF16)


def scores_of(q, k):
    return lax.dot_general(q, k, (((1,), (1,)), ((), ())), preferred_element_type=F32)


def attend(q, keys, values, biases, present):
    scores = [scores_of(q, k) for k in keys]
    if biases is not None:
        scores = [s + b for s, b in zip(scores, biases)]
    tops = [jnp.max(s, axis=1, keepdims=True) for s in scores]
    if present is not None:
        tops = [jnp.where(ok, t, NEG) for ok, t in zip(present, tops)]
    peak = tops[0]
    for t in tops[1:]:
        peak = jnp.maximum(peak, t)
    total = None
    for index, (s, v) in enumerate(zip(scores, values)):
        shift = peak if present is None else jnp.where(present[index], peak, BIG)
        probs = jnp.exp(s - shift).astype(BF16)
        part = jnp.dot(probs, v, preferred_element_type=F32)
        total = part if total is None else total + part
    return total, peak


def pair(q, keys, values, biases, present, low_half, lo, hi):
    even, even_peak = attend(q * lo, keys, [v * lo + hi for v in values], biases, present)
    odd, odd_peak = attend(q * hi, keys, [v * hi + lo for v in values], biases, present)
    num = jnp.where(low_half, even, odd)
    total = pltpu.roll(jnp.where(low_half, odd, even), 64, 1)
    peak = jnp.where(low_half, even_peak, odd_peak)
    return num, total, peak


def merge(a, b):
    peak = jnp.maximum(a[2], b[2])
    scale_a, scale_b = jnp.exp(a[2] - peak), jnp.exp(b[2] - peak)
    return a[0] * scale_a + b[0] * scale_b, a[1] * scale_a + b[1] * scale_b, peak


def expand(parts, ref):
    count = parts[0].shape[0]
    for index, part in enumerate(parts):
        ref[index, pl.ds(0, count, stride=2), :] = part
        ref[index, pl.ds(1, count, stride=2), :] = part
    return tuple(ref[index, 0 : 2 * count, :] for index in range(3))


def kernel(
    q_hbm, k_hbm, v_hbm, seg_hbm, w_hbm, out_ref,
    q0, kv0, segi, segf, q1, kv1, q2, kv2,
    s3, r3, sq3, rq3, s4, r4, s5, r5, sq4, rq4, sq5, rq5,
    st0, st1, st2, st3, rs3, srow4, rrow4, srow5, rrow5, ex, at, ra, via, sstat, rstat, sfar, rfar, near, wbuf,
    local, snd, rcv,
):
    i = lax.axis_index("seq")
    x = lax.axis_index("head")
    core = lax.rem(i, 2)
    chip = lax.div(i, 2)
    g4, a4 = lax.div(i, 4), lax.rem(i, 4)
    g5, a5 = lax.div(i, 8), lax.rem(i, 8)
    sibling = i + 1 - 2 * core
    right, left = lax.rem(i + 1, SEQ), lax.rem(i + SEQ - 1, SEQ)
    x_up, x_down, x_far = [lax.rem(x + d, HEADX) for d in (1, 3, 2)]
    late = lax.rem(g5, 2)
    beside5 = g5 + 1 - 2 * late
    owner5 = (a5 < 2) | (a5 >= 6)
    head5 = jnp.where(a5 < 2, a5, lax.rem(a5, 4))
    y_on = lax.rem(i + SEQ + 16 - 32 * late, SEQ)

    def remote(src, dst, slot, device):
        return pltpu.make_async_remote_copy(
            src_ref=src, dst_ref=dst, send_sem=snd.at[slot], recv_sem=rcv.at[slot], device_id=device, device_id_type=MESH
        )

    loads = []
    for p in range(2):
        lanes = pl.ds(128 * p, 128)
        loads.append(pltpu.make_async_copy(k_hbm.at[:, lanes], kv0.at[0, p, pl.ds(BLOCK, ROWS)], local.at[p]))
        loads.append(pltpu.make_async_copy(v_hbm.at[:, lanes], kv0.at[1, p, pl.ds(BLOCK, ROWS)], local.at[2 + p]))
        loads.append(pltpu.make_async_copy(q_hbm.at[:, lanes], q0.at[p], local.at[4 + p]))
    loads.append(pltpu.make_async_copy(seg_hbm, segi.at[1], local.at[6]))
    load_w = pltpu.make_async_copy(w_hbm, wbuf.at[x], local.at[7])
    for load in loads:
        load.start()
    load_w.start()

    barrier = pltpu.get_barrier_semaphore()

    def greet(seq, head):
        pl.semaphore_signal(barrier, inc=1, device_id={"seq": seq, "head": head}, device_id_type=MESH)

    blocks4 = [lax.rem(g4 + 1, SEQ // 4), lax.rem(g4 + SEQ // 4 - 1, SEQ // 4)]
    for j in range(8):
        greet(beside5 * 8 + j, x)
    for block in blocks4:
        for j in range(4):
            greet(block * 4 + j, x)
    for d in range(1, 8):
        greet(g5 * 8 + lax.rem(a5 + d, 8), x)
    for other in (x_up, x_down, x_far):
        greet(i, other)
    greet(lax.rem(i + 16, SEQ), x)
    greet(lax.rem(i + SEQ - 16, SEQ), x)

    lane = lax.broadcasted_iota(jnp.int32, (1, 128), 1)
    low_half = lane < 64
    lo_f = jnp.where(low_half, 1.0, 0.0).astype(F32)
    lo = lo_f.astype(BF16)
    hi = (1.0 - lo_f).astype(BF16)
    means = averaging()
    for load in loads:
        load.wait()
    last_k, last_v, last_q = [], [], []
    for t in range(4):
        rows = pl.ds(BLOCK + BLOCK * t, BLOCK)
        ck, cv = [
            jnp.dot(means, jnp.concatenate([kv0[n, 0, rows, :], kv0[n, 1, rows, :]], axis=1), preferred_element_type=F32)
            for n in range(2)
        ]
        own = pl.ds(BLOCK * t, BLOCK)
        cq = 0.125 * jnp.dot(means, jnp.concatenate([q0[0, own, :], q0[1, own, :]], axis=1), preferred_element_type=F32)
        for p in range(2):
            lanes = slice(128 * p, 128 * p + 128)
            q1[p, pl.ds(128 * t, 128), :] = cq[0:128, lanes].astype(BF16)
            q2[p, pl.ds(64 * t, 64), :] = cq[128:192, lanes].astype(BF16)
            sq3[p, pl.ds(32 * t, 32), :] = cq[192:224, lanes].astype(BF16)
            for n, c in enumerate((ck, cv)):
                kv1[n, p, pl.ds(BLOCK + 128 * t, 128), :] = c[0:128, lanes].astype(BF16)
                kv2[n, p, pl.ds(BLOCK + 64 * t, 64), :] = c[128:192, lanes].astype(BF16)
                s3[p, n, pl.ds(32 * t, 32), :] = c[192:224, lanes].astype(BF16)
        for h in range(4):
            s4[h, pl.ds(16 * t, 16), :] = packed(ck[224:240], cv[224:240], h, low_half).astype(BF16)
            sq4[h, pl.ds(16 * t, 16), :] = packed(cq[224:240], None, h, low_half).astype(BF16)
        last_k.append(ck[240:248])
        last_v.append(cv[240:248])
        last_q.append(cq[240:248])
    k5, v5, q5 = [jnp.concatenate(rows, axis=0) for rows in (last_k, last_v, last_q)]
    for h in range(4):
        s5[h] = packed(k5, v5, h, low_half).astype(BF16)
        sq5[h] = packed(q5, None, h, low_half).astype(BF16)

    segf[pl.ds(8, 8), :] = segi[1].astype(F32)

    def bias_of(b, j):
        exists = (4 * i + b + j >= 1) & (4 * i + b + j <= 4 * SEQ)
        first = 6 + 2 * (b + j)
        return [jnp.where(exists, segf[pl.ds(first + n, 1), :], -1.0) for n in range(2)]

    def level0(b, p):
        queries = q0[p, pl.ds(pl.multiple_of(b * BLOCK, BLOCK), BLOCK), :] * jnp.asarray(0.125, BF16)
        own = [
            jnp.transpose(jnp.broadcast_to(segf[pl.ds(8 + 2 * b + n, 1), :], (128, 128))) for n in range(2)
        ]
        own = jnp.concatenate(own, axis=0)
        keys, values, biases = [], [], []
        for j in range(3):
            rows = pl.ds(pl.multiple_of((b + j) * BLOCK, BLOCK), BLOCK)
            keys.append(kv0[0, p, rows, :])
            values.append(kv0[1, p, rows, :])
            biases.append(
                jnp.concatenate([jnp.where(own == near, 0.0, NEG) for near in bias_of(b, j)], axis=1)
            )
        state = pair(queries, keys, values, biases, None, low_half, lo, hi)
        for n in range(3):
            st0[n, p, pl.ds(pl.multiple_of(b * BLOCK, BLOCK), BLOCK), :] = state[n]

    @pl.when(late == 0)
    def _():
        @pl.loop(0, 4)
        def _(u):
            level0(1 + lax.div(u, 2), lax.rem(u, 2))

    pl.semaphore_wait(barrier, 28)
    sends = []

    def send(src, dst, slot, seq, head=x):
        copy = remote(src, dst, slot, {"seq": seq, "head": head})
        copy.start()
        return copy

    def received(ref, slot):
        pltpu.make_async_copy(ref, ref, rcv.at[slot]).wait()

    def sent(ref, slot):
        pltpu.make_async_copy(ref, ref, snd.at[slot]).wait()

    def to_sides(ref, count, skip, slot):
        n = BLOCK - skip
        sends.append(send(ref.at[:, :, pl.ds(count, n)], ref.at[:, :, pl.ds(0, n)], slot, right))
        sends.append(
            send(
                ref.at[:, :, pl.ds(BLOCK + skip, n)], ref.at[:, :, pl.ds(BLOCK + count + skip, n)], slot + 1, left
            )
        )

    half = pl.ds(128 * core, 128)
    sends.append(send(w_hbm.at[half], wbuf.at[x, half], W_L, i, x_up))
    sends.append(send(w_hbm.at[half], wbuf.at[x, half], W_R, i, x_down))
    for h in range(4):
        send(s5.at[h], r5.at[late, a5], KV5, beside5 * 8 + OWNER5[h])

        @pl.when(a5 != OWNER5[h])
        def _():
            send(sq5.at[h], rq5.at[a5], Q5, g5 * 8 + OWNER5[h])

        @pl.when(a5 == OWNER5[h])
        def _():
            rq5[a5] = sq5[h]

    sends.append(send(segi.at[1], segi.at[0], SEG_P, right))
    sends.append(send(segi.at[1], segi.at[2], SEG_N, left))
    to_sides(kv0, ROWS, 0, L0_P)
    to_sides(kv2, 256, 64, L2_P)
    to_sides(kv1, 512, 128, L1_P)
    for direction, block in enumerate(blocks4):
        for j in range(4):
            send(s4.at[j], r4.at[direction, a4], KV4, block * 4 + j)
    for d in range(1, 4):
        other = lax.rem(a4 + d, 4)
        sends.append(send(sq4.at[other], rq4.at[a4], Q4 + d, g4 * 4 + other))
    sends.append(send(sq3.at[1 - core], rq3.at[core], Q3, sibling))
    for direction, by in enumerate((1, SEQ // 2 - 1)):
        beside = lax.rem(chip + by, SEQ // 2)
        for p in range(2):
            send(s3.at[p], r3.at[direction, :, core], KV3, beside * 2 + p)
    rq3[core] = sq3[core]
    rq4[a4] = sq4[a4]

    @pl.when(late == 1)
    def _():
        @pl.loop(0, 4)
        def _(u):
            level0(1 + lax.div(u, 2), lax.rem(u, 2))

    @pl.when(owner5)
    def _():
        received(r5.at[1 - late], KV5)
        send(r5.at[1 - late], r5.at[late], KV5_Y, y_on)

    quarter = [pl.ds(128 * core, 64), pl.ds(128 * core + 64, 64)]
    received(wbuf.at[x_down, half], W_L)
    sends.append(send(wbuf.at[x_down, quarter[0]], wbuf.at[x_down, quarter[0]], W2_L, i, x_up))
    sends.append(send(wbuf.at[x_down, half], wbuf.at[x_down, half], W_ON_L, sibling))
    received(wbuf.at[x_up, half], W_R)
    sends.append(send(wbuf.at[x_up, quarter[1]], wbuf.at[x_up, quarter[1]], W2_R, i, x_down))
    sends.append(send(wbuf.at[x_up, half], wbuf.at[x_up, half], W_ON_R, sibling))

    received(segi.at[0], SEG_P)
    received(segi.at[2], SEG_N)
    segf[pl.ds(0, 8), :] = segi[0].astype(F32)
    segf[pl.ds(16, 8), :] = segi[2].astype(F32)
    for side, (first, row1, row2) in enumerate(((0, 128, 192), (5 * BLOCK, 3 * BLOCK, 2 * BLOCK))):
        received(kv0.at[:, :, pl.ds(first, BLOCK)], L0_P + side)
        for n in range(2):
            rim = jnp.concatenate([kv0[n, p, pl.ds(first, BLOCK), :] for p in range(2)], axis=1)
            rim = jnp.dot(means[:192], rim, preferred_element_type=F32).astype(BF16)
            for p in range(2):
                kv1[n, p, pl.ds(row1, 128), :] = rim[:128, 128 * p : 128 * p + 128]
                kv2[n, p, pl.ds(row2, 64), :] = rim[128:, 128 * p : 128 * p + 128]

    received(kv2.at[:, :, pl.ds(0, 192)], L2_P)
    received(kv2.at[:, :, pl.ds(2 * BLOCK + 64, 192)], L2_N)

    @pl.loop(0, 2)
    def _(p):
        sides = [pl.ds(0, BLOCK), pl.ds(2 * BLOCK, BLOCK)]
        state = pair(
            q2[p], [kv2[0, p, s, :] for s in sides], [kv2[1, p, s, :] for s in sides],
            None, (i > 0, i < SEQ - 1), low_half, lo, hi,
        )
        for n in range(3):
            st2[n, p] = state[n]

    received(kv1.at[:, :, pl.ds(0, 128)], L1_P)
    received(kv1.at[:, :, pl.ds(3 * BLOCK + 128, 128)], L1_N)

    @pl.loop(0, 4)
    def _(u):
        b, p = lax.div(u, 2), lax.rem(u, 2)
        own = pl.ds(pl.multiple_of(b * BLOCK, BLOCK), BLOCK)
        sides = [own, pl.ds(pl.multiple_of((b + 2) * BLOCK, BLOCK), BLOCK)]
        place = 2 * i + b
        state = pair(
            q1[p, own, :], [kv1[0, p, s, :] for s in sides], [kv1[1, p, s, :] for s in sides],
            None, (place > 0, place < 2 * SEQ - 1), low_half, lo, hi,
        )
        for n in range(3):
            st1[n, p, own, :] = state[n]

    for p in range(2):
        state = expand(tuple(st2[n, p] for n in range(3)), ex)
        state = merge(state, tuple(st1[n, p] for n in range(3)))
        for n in range(3):
            st1[n, p] = state[n]

    row = lax.broadcasted_iota(jnp.int32, (8, BLOCK), 0)

    def finish(t):
        d = lax.rem(t + HEADX - x, HEADX)
        sums = []
        for p in range(2):
            coarse = expand(tuple(st1[n, p, pl.ds(pl.multiple_of(128 * t, 128), 128), :] for n in range(3)), ex)
            fine = tuple(st0[n, p, pl.ds(pl.multiple_of(BLOCK * t, BLOCK), BLOCK), :] for n in range(3))
            num, total, peak = merge(fine, coarse)
            mean = (num / total).astype(BF16)
            sums.append(jnp.transpose(peak + jnp.log(total)))
            at[t, p] = mean

            @pl.when(d == 0)
            def _():
                ra[x, p] = mean

            @pl.when(d == 1)
            def _():
                send(at.at[t, p], ra.at[x, p], AT_L + p, i, x_up)

            @pl.when(d == 3)
            def _():
                send(at.at[t, p], ra.at[x, p], AT_R + p, i, x_down)

            @pl.when(d == 2)
            def _():
                send(at.at[t, p], via.at[p], VIA + p, i, x_down if p else x_up)

        stat = jnp.where(row < 2, sums[0][0:8], sums[1][0:8])
        stat = jnp.where(row == 1, sums[0][64:72], jnp.where(row == 3, sums[1][64:72], stat))
        sstat[t] = stat

        @pl.when(d == 0)
        def _():
            rstat[x] = stat

        @pl.when(d > 0)
        def _():
            send(sstat.at[t], rstat.at[x], STAT + d, i, t)

    finish(1)
    finish(2)

    def one_head(ref, queries, place, count):
        tiles = [ref[n].reshape(BLOCK, 128) for n in range(2)]
        out, peak = attend(queries, tiles, [t * hi + lo for t in tiles], None, (place > 0, place < count - 1))
        return jnp.where((lane >= 32) & low_half, peak, out)

    for d in range(1, 4):
        received(rq4.at[lax.rem(a4 + 4 - d, 4)], Q4 + d)
    received(r4, KV4)
    srow4[...] = one_head(r4, rq4[...].reshape(BLOCK, 128), g4, SEQ // 4).reshape(4, 64, 128)
    for d in range(1, 4):
        other = lax.rem(a4 + d, 4)
        sends.append(send(srow4.at[other], rrow4.at[a4], RES4 + d, g4 * 4 + other))
    rrow4[a4] = srow4[a4]

    @pl.when(owner5)
    def _():
        received(rq5.at[pl.ds(0, 7)], Q5)
        received(r5.at[late], KV5_Y)
        srow5[...] = one_head(r5, rq5[...].reshape(BLOCK, 128), g5, SEQ // 8).reshape(8, 32, 128)
        for d in range(1, 8):
            other = lax.rem(a5 + d, 8)
            send(srow5.at[other], rrow5.at[head5], RES5, g5 * 8 + other)
        rrow5[head5] = srow5[a5]

    received(r3, KV3)
    received(rq3.at[1 - core], Q3)
    state = pair(
        rq3[...].reshape(BLOCK, 128),
        [r3[n, 0].reshape(BLOCK, 128) for n in range(2)],
        [r3[n, 1].reshape(BLOCK, 128) for n in range(2)],
        None,
        (chip > 0, chip < SEQ // 2 - 1),
        low_half, lo, hi,
    )
    for n in range(3):
        for m in range(2):
            rs3[m, n] = state[n][128 * m : 128 * m + 128]
    sends.append(send(rs3.at[1 - core], st3.at[core], RES3, sibling))
    st3[core] = rs3[core]

    received(wbuf.at[x_far, quarter[0]], W2_L)
    received(wbuf.at[x_far, quarter[1]], W2_R)
    sends.append(send(wbuf.at[x_far, half], wbuf.at[x_far, half], W_ON_2, sibling))

    first = jnp.where(x < 2, 3, 0)
    for t in (first, 3 - first):
        for p in range(2):
            level0(t, p)
        finish(t)
    received(via.at[0], VIA)
    sends.append(send(via.at[0], ra.at[x_down, 0], AT_2, i, x_up))
    received(via.at[1], VIA + 1)
    sends.append(send(via.at[1], ra.at[x_up, 1], AT_2 + 1, i, x_down))

    for d in range(1, 4):
        received(rrow4.at[lax.rem(a4 + 4 - d, 4)], RES4 + d)

    @pl.when(owner5)
    def _():
        received(rrow5.at[pl.ds(0, 3)], RES5)

    @pl.when(jnp.logical_not(owner5))
    def _():
        received(rrow5, RES5)

    received(st3.at[1 - core], RES3)
    sums = []
    for p in range(2):

        def far(ref):
            even, odd = ref[2 * p], ref[2 * p + 1]
            num = jnp.where(low_half, pltpu.roll(even, 64, 1), odd)
            total = jnp.where(low_half, even[:, 0:1], odd[:, 0:1])
            return num, total, jnp.where(low_half, even[:, 32:33], odd[:, 32:33])

        state = merge(expand(far(rrow5), ex), far(rrow4))
        num, total, peak = merge(expand(state, ex), tuple(st3[p, n] for n in range(3)))
        mean = num / total
        sums.append(peak + jnp.log(total))
        for t in range(4):
            sfar[t, p] = mean[32 * t : 32 * t + 32]
    both = jnp.where(lane < 96, pltpu.roll(sums[1], 64, 1), sums[1])
    both = jnp.where(lane < 32, sums[0], jnp.where(low_half, pltpu.roll(sums[0], 96, 1), both))
    for t in range(4):
        sfar[t, 2] = both[32 * t : 32 * t + 32]
    for d in (2, 1, 3):
        other = lax.rem(x + d, HEADX)
        sends.append(send(sfar.at[other], rfar.at[x], FAR + d, i, other))
    rfar[x] = sfar[x]

    for d in range(1, 4):
        received(rstat.at[lax.rem(x + HEADX - d, HEADX)], STAT + d)
    for m in range(4):
        for p in range(2):
            lines = [jnp.broadcast_to(rstat[m, 2 * p + n : 2 * p + n + 1, :], (64, BLOCK)) for n in range(2)]
            near[m, p] = jnp.transpose(jnp.concatenate(lines, axis=0))

    load_w.wait()
    other_half = pl.ds(128 * (1 - core), 128)
    for owner, slot in ((x_down, W_ON_L), (x_up, W_ON_R), (x_far, W_ON_2)):
        received(wbuf.at[owner, other_half], slot)
    for p in range(2):
        for owner, slot in ((x_down, AT_L), (x_up, AT_R), (x_far, AT_2)):
            received(ra.at[owner, p], slot + p)
    for d in range(1, 4):
        received(rfar.at[lax.rem(x + HEADX - d, HEADX)], FAR + d)

    def spread(rows):
        return jnp.broadcast_to(rows[:, None, :], (32, 8, 128)).reshape(BLOCK, 128)

    attention = []
    for m in range(4):
        for p in range(2):
            sums = jnp.where(low_half, rfar[m, 2, :, 64 * p : 64 * p + 1], rfar[m, 2, :, 64 * p + 32 : 64 * p + 33])
            weight = 1.0 / (1.0 + jnp.exp(spread(sums) - near[m, p]))
            coarse = spread(rfar[m, p])
            attention.append((coarse + weight * (ra[m, p].astype(F32) - coarse)).astype(BF16))
    for n in range(4):
        columns = pl.ds(256 * n, 256)
        total = None
        for m in range(4):
            rows = jnp.concatenate(attention[2 * m : 2 * m + 2], axis=1)
            part = jnp.dot(rows, wbuf[m, :, columns], preferred_element_type=F32)
            total = part if total is None else total + part
        out_ref[:, columns] = total.astype(BF16)

    for copy in sends:
        copy.wait_send()
    sent(s5, KV5)
    for h in range(4):

        @pl.when(a5 != OWNER5[h])
        def _():
            sent(sq5.at[h], Q5)

    @pl.when(owner5)
    def _():
        sent(r5.at[0], KV5_Y)
        sent(srow5.at[pl.ds(0, 7)], RES5)

    sent(r4, KV4)
    sent(r3, KV3)
    for p in range(2):
        for slot in (AT_L, AT_R, VIA):
            sent(at.at[0, p], slot + p)
    for d in range(1, 4):
        sent(sstat.at[0], STAT + d)


def packed(first, second, h, low_half):
    lanes = slice(128 * (h // 2), 128 * (h // 2) + 128)
    first = first[:, lanes]
    if h % 2:
        first = pltpu.roll(first, 64, 1)
    if second is None:
        return jnp.where(low_half, first, 0.0)
    second = second[:, lanes]
    if h % 2 == 0:
        second = pltpu.roll(second, 64, 1)
    return jnp.where(low_half, first, second)


def on_device(query_rows, key_rows, value_rows, segment, w_out):
    vmem = pltpu.VMEM
    return pl.pallas_call(
        kernel,
        out_shape=jax.ShapeDtypeStruct((BLOCK, 1024), BF16),
        in_specs=[pl.BlockSpec(memory_space=pl.ANY)] * 5,
        out_specs=pl.BlockSpec(memory_space=vmem),
        scratch_shapes=[
            vmem((2, ROWS, 128), BF16),
            vmem((2, 2, ROWS + 512, 128), BF16),
            vmem((3, 8, 128), jnp.int32),
            vmem((24, 128), F32),
            vmem((2, 512, 128), BF16),
            vmem((2, 2, 1024, 128), BF16),
            vmem((2, 256, 128), BF16),
            vmem((2, 2, 768, 128), BF16),
            vmem((2, 2, 128, 128), BF16),
            vmem((2, 2, 2, 128, 128), BF16),
            vmem((2, 128, 128), BF16),
            vmem((2, 128, 128), BF16),
            vmem((4, 64, 128), BF16),
            vmem((2, 4, 64, 128), BF16),
            vmem((4, 32, 128), BF16),
            vmem((2, 8, 32, 128), BF16),
            vmem((4, 64, 128), BF16),
            vmem((4, 64, 128), BF16),
            vmem((4, 32, 128), BF16),
            vmem((8, 32, 128), BF16),
            vmem((3, 2, ROWS, 128), F32),
            vmem((3, 2, 512, 128), F32),
            vmem((3, 2, 256, 128), F32),
            vmem((2, 3, 128, 128), F32),
            vmem((2, 3, 128, 128), F32),
            vmem((4, 64, 128), F32),
            vmem((4, 64, 128), F32),
            vmem((8, 32, 128), F32),
            vmem((4, 32, 128), F32),
            vmem((3, 512, 128), F32),
            vmem((4, 2, BLOCK, 128), BF16),
            vmem((4, 2, BLOCK, 128), BF16),
            vmem((2, BLOCK, 128), BF16),
            vmem((4, 8, BLOCK), F32),
            vmem((4, 8, BLOCK), F32),
            vmem((4, 3, 32, 128), F32),
            vmem((4, 3, 32, 128), F32),
            vmem((4, 2, BLOCK, 128), F32),
            vmem((4, 256, 1024), BF16),
            pltpu.SemaphoreType.DMA((8,)),
            pltpu.SemaphoreType.DMA((N_SEM,)),
            pltpu.SemaphoreType.DMA((N_SEM,)),
        ],
        compiler_params=pltpu.CompilerParams(
            collective_id=0, has_side_effects=True, vmem_limit_bytes=62 * 2**20
        ),
        name="block_attention",
    )(query_rows, key_rows, value_rows, segment.reshape(8, 128), w_out)


def solution(mesh):
    placed = (P("seq", "head"), P("seq", "head"), P("seq", "head"), P("seq"), P("head", None))
    return jax.shard_map(
        on_device, mesh=mesh, in_specs=placed, out_specs=P(("seq", "head"), None), check_vma=False
    )
```

```python
import jax
import jax.numpy as jnp
from jax import lax
from jax.experimental import pallas as pl
from jax.experimental.pallas import tpu as pltpu
from jax.sharding import PartitionSpec as P

MESH = pl.DeviceIdType.MESH
F32 = jnp.float32
BF16 = jnp.bfloat16

SEQ = 64
HEADX = 4
BLOCK = 256
ROWS = 1024
NEG = -1e30
BIG = 1e30

SEG_P, SEG_N, L0_P, L0_N, L1_P, L1_N, L2_P, L2_N = range(8)
KV3, KV4, KV5, KV5_Y, Q3, Q5, RES3, RES5 = range(8, 16)
Q4, RES4 = 15, 18
W_L, W_R, W2_L, W2_R, W_ON_L, W_ON_R, W_ON_2 = range(22, 29)
AT_L, AT_R, VIA, AT_2 = 29, 31, 33, 35
STAT, FAR = 36, 39
D3 = 43
N_SEM = 44

OWNER5 = (0, 1, 6, 7)


def averaging():
    row = lax.broadcasted_iota(jnp.int32, (BLOCK, BLOCK), 0)
    token = lax.broadcasted_iota(jnp.int32, (BLOCK, BLOCK), 1)
    result = jnp.zeros((BLOCK, BLOCK), F32)
    base = 0
    for level in range(1, 6):
        count = BLOCK >> level
        first = (row - base) << level
        hit = (row >= base) & (row < base + count) & (token >= first) & (token < first + (1 << level))
        result = jnp.where(hit, 0.5**level, result)
        base += count
    return result.astype(BF16)


def scores_of(q, k):
    return lax.dot_general(q, k, (((1,), (1,)), ((), ())), preferred_element_type=F32)


def attend(q, keys, values, biases, present):
    scores = [scores_of(q, k) for k in keys]
    if biases is not None:
        scores = [s + b for s, b in zip(scores, biases)]
    tops = [jnp.max(s, axis=1, keepdims=True) for s in scores]
    if present is not None:
        tops = [jnp.where(ok, t, NEG) for ok, t in zip(present, tops)]
    peak = tops[0]
    for t in tops[1:]:
        peak = jnp.maximum(peak, t)
    total = None
    for index, (s, v) in enumerate(zip(scores, values)):
        shift = peak if present is None else jnp.where(present[index], peak, BIG)
        probs = jnp.exp(s - shift).astype(BF16)
        part = jnp.dot(probs, v, preferred_element_type=F32)
        total = part if total is None else total + part
    return total, peak


def pairs(groups, low_half, lo, hi):
    all_scores = []
    for q, keys, _, biases, _ in groups:
        q = jnp.concatenate([q * lo, q * hi], axis=0)
        scores = [scores_of(q, k) for k in keys]
        if biases is not None:
            scores = [s + jnp.concatenate([b, b], axis=0) for s, b in zip(scores, biases)]
        all_scores.append(scores)
    ones = jnp.ones((BLOCK, 128), BF16)
    results = []
    for (q, _, values, _, present), scores in zip(groups, all_scores):
        tops = [jnp.max(s, axis=1, keepdims=True) for s in scores]
        if present is not None:
            tops = [jnp.where(ok, t, NEG) for ok, t in zip(present, tops)]
        peak = tops[0]
        for t in tops[1:]:
            peak = jnp.maximum(peak, t)
        out = None
        for index, (s, v) in enumerate(zip(scores, values)):
            shift = peak if present is None else jnp.where(present[index], peak, BIG)
            probs = jnp.exp(s - shift).astype(BF16)
            part = jnp.dot(probs, jnp.concatenate([v, ones], axis=1), preferred_element_type=F32)
            out = part if out is None else out + part
        n = q.shape[0]
        results.append(
            tuple(jnp.where(low_half, w[:n], w[n:]) for w in (out[:, :128], out[:, 128:], peak))
        )
    return results


def merge(a, b):
    peak = jnp.maximum(a[2], b[2])
    scale_a, scale_b = jnp.exp(a[2] - peak), jnp.exp(b[2] - peak)
    return a[0] * scale_a + b[0] * scale_b, a[1] * scale_a + b[1] * scale_b, peak


def expand(parts, ref):
    count = parts[0].shape[0]
    for index, part in enumerate(parts):
        ref[index, pl.ds(0, count, stride=2), :] = part
        ref[index, pl.ds(1, count, stride=2), :] = part
    return tuple(ref[index, 0 : 2 * count, :] for index in range(3))


def kernel(
    q_hbm, k_hbm, v_hbm, seg_hbm, w_hbm, out_ref,
    q0, kv0, segi, segf, q1, kv1, q2, kv2,
    s3, sd3, r3, sq3, rq3, s4, r4, s5, r5, sq4, rq4, sq5, rq5,
    st0, st1, st2, st3, rs3, srow4, rrow4, srow5, rrow5, ex, at, ra, via, sstat, rstat, sfar, rfar, near, wbuf,
    local, snd, rcv,
):
    i = lax.axis_index("seq")
    x = lax.axis_index("head")
    core = lax.rem(i, 2)
    chip = lax.div(i, 2)
    g4, a4 = lax.div(i, 4), lax.rem(i, 4)
    g5, a5 = lax.div(i, 8), lax.rem(i, 8)
    sibling = i + 1 - 2 * core
    right, left = lax.rem(i + 1, SEQ), lax.rem(i + SEQ - 1, SEQ)
    x_up, x_down, x_far = [lax.rem(x + d, HEADX) for d in (1, 3, 2)]
    late = lax.rem(g5, 2)
    beside5 = g5 + 1 - 2 * late
    owner5 = (a5 < 2) | (a5 >= 6)
    head5 = jnp.where(a5 < 2, a5, lax.rem(a5, 4))
    y_on = lax.rem(i + SEQ + 16 - 32 * late, SEQ)

    def remote(src, dst, slot, device):
        return pltpu.make_async_remote_copy(
            src_ref=src, dst_ref=dst, send_sem=snd.at[slot], recv_sem=rcv.at[slot], device_id=device, device_id_type=MESH
        )

    loads = []
    for p in range(2):
        lanes = pl.ds(128 * p, 128)
        loads.append(pltpu.make_async_copy(k_hbm.at[:, lanes], kv0.at[0, p, pl.ds(BLOCK, ROWS)], local.at[p]))
        loads.append(pltpu.make_async_copy(v_hbm.at[:, lanes], kv0.at[1, p, pl.ds(BLOCK, ROWS)], local.at[2 + p]))
        loads.append(pltpu.make_async_copy(q_hbm.at[:, lanes], q0.at[p], local.at[4 + p]))
    loads.append(pltpu.make_async_copy(seg_hbm, segi.at[1], local.at[6]))
    load_w = pltpu.make_async_copy(w_hbm, wbuf.at[x], local.at[7])
    for load in loads:
        load.start()
    load_w.start()

    barrier = pltpu.get_barrier_semaphore()

    def greet(seq, head):
        pl.semaphore_signal(barrier, inc=1, device_id={"seq": seq, "head": head}, device_id_type=MESH)

    blocks4 = [lax.rem(g4 + 1, SEQ // 4), lax.rem(g4 + SEQ // 4 - 1, SEQ // 4)]
    for j in range(8):
        greet(beside5 * 8 + j, x)
    for block in blocks4:
        for j in range(4):
            greet(block * 4 + j, x)
    for d in range(1, 8):
        greet(g5 * 8 + lax.rem(a5 + d, 8), x)
    for other in (x_up, x_down, x_far):
        greet(i, other)
    greet(lax.rem(i + 16, SEQ), x)
    greet(lax.rem(i + SEQ - 16, SEQ), x)

    lane = lax.broadcasted_iota(jnp.int32, (1, 128), 1)
    low_half = lane < 64
    lo_f = jnp.where(low_half, 1.0, 0.0).astype(F32)
    lo = lo_f.astype(BF16)
    hi = (1.0 - lo_f).astype(BF16)
    means = averaging()
    for load in loads:
        load.wait()
    last_k, last_v, last_q = [], [], []
    for t in range(4):
        rows = pl.ds(BLOCK + BLOCK * t, BLOCK)
        ck, cv = [
            jnp.dot(means, jnp.concatenate([kv0[n, 0, rows, :], kv0[n, 1, rows, :]], axis=1), preferred_element_type=F32)
            for n in range(2)
        ]
        own = pl.ds(BLOCK * t, BLOCK)
        cq = 0.125 * jnp.dot(means, jnp.concatenate([q0[0, own, :], q0[1, own, :]], axis=1), preferred_element_type=F32)
        for p in range(2):
            lanes = slice(128 * p, 128 * p + 128)
            q1[p, pl.ds(128 * t, 128), :] = cq[0:128, lanes].astype(BF16)
            q2[p, pl.ds(64 * t, 64), :] = cq[128:192, lanes].astype(BF16)
            sq3[p, pl.ds(32 * t, 32), :] = cq[192:224, lanes].astype(BF16)
            for n, c in enumerate((ck, cv)):
                kv1[n, p, pl.ds(BLOCK + 128 * t, 128), :] = c[0:128, lanes].astype(BF16)
                kv2[n, p, pl.ds(BLOCK + 64 * t, 64), :] = c[128:192, lanes].astype(BF16)
                s3[p, n, pl.ds(32 * t, 32), :] = c[192:224, lanes].astype(BF16)
        for h in range(4):
            s4[h, pl.ds(16 * t, 16), :] = packed(ck[224:240], cv[224:240], h, low_half).astype(BF16)
            sq4[h, pl.ds(16 * t, 16), :] = packed(cq[224:240], None, h, low_half).astype(BF16)
        last_k.append(ck[240:248])
        last_v.append(cv[240:248])
        last_q.append(cq[240:248])
    k5, v5, q5 = [jnp.concatenate(rows, axis=0) for rows in (last_k, last_v, last_q)]
    for h in range(4):
        s5[h] = packed(k5, v5, h, low_half).astype(BF16)
        sq5[h] = packed(q5, None, h, low_half).astype(BF16)

    segf[pl.ds(8, 8), :] = segi[1].astype(F32)

    def bias_of(b, j):
        exists = (4 * i + b + j >= 1) & (4 * i + b + j <= 4 * SEQ)
        first = 6 + 2 * (b + j)
        return [jnp.where(exists, segf[pl.ds(first + n, 1), :], -1.0) for n in range(2)]

    def level0(b):
        own = [
            jnp.transpose(jnp.broadcast_to(segf[pl.ds(8 + 2 * b + n, 1), :], (128, 128))) for n in range(2)
        ]
        own = jnp.concatenate(own, axis=0)
        biases = [
            jnp.concatenate([jnp.where(own == near_by, 0.0, NEG) for near_by in bias_of(b, j)], axis=1) for j in range(3)
        ]
        here = pl.ds(pl.multiple_of(b * BLOCK, BLOCK), BLOCK)
        rows = [pl.ds(pl.multiple_of((b + j) * BLOCK, BLOCK), BLOCK) for j in range(3)]
        groups = [
            (
                q0[p, here, :] * jnp.asarray(0.125, BF16),
                [kv0[0, p, r, :] for r in rows],
                [kv0[1, p, r, :] for r in rows],
                biases,
                None,
            )
            for p in range(2)
        ]
        for p, state in enumerate(pairs(groups, low_half, lo, hi)):
            for n in range(3):
                st0[n, p, here, :] = state[n]

    @pl.when(late == 0)
    def _():
        level0(1)
        level0(2)

    pl.semaphore_wait(barrier, 28)
    sends = []

    def send(src, dst, slot, seq, head=x):
        copy = remote(src, dst, slot, {"seq": seq, "head": head})
        copy.start()
        return copy

    def received(ref, slot):
        pltpu.make_async_copy(ref, ref, rcv.at[slot]).wait()

    def sent(ref, slot):
        pltpu.make_async_copy(ref, ref, snd.at[slot]).wait()

    def to_sides(ref, count, skip, slot):
        n = BLOCK - skip
        sends.append(send(ref.at[:, :, pl.ds(count, n)], ref.at[:, :, pl.ds(0, n)], slot, right))
        sends.append(
            send(
                ref.at[:, :, pl.ds(BLOCK + skip, n)], ref.at[:, :, pl.ds(BLOCK + count + skip, n)], slot + 1, left
            )
        )

    half = pl.ds(128 * core, 128)
    sends.append(send(w_hbm.at[half], wbuf.at[x, half], W_L, i, x_up))
    sends.append(send(w_hbm.at[half], wbuf.at[x, half], W_R, i, x_down))
    for h in range(4):
        send(s5.at[h], r5.at[late, a5], KV5, beside5 * 8 + OWNER5[h])

        @pl.when(a5 != OWNER5[h])
        def _():
            send(sq5.at[h], rq5.at[a5], Q5, g5 * 8 + OWNER5[h])

        @pl.when(a5 == OWNER5[h])
        def _():
            rq5[a5] = sq5[h]

    for direction, block in enumerate(blocks4):
        for j in range(4):
            send(s4.at[j], r4.at[direction, a4], KV4, block * 4 + j)
    for d in range(1, 4):
        other = lax.rem(a4 + d, 4)
        sends.append(send(sq4.at[other], rq4.at[a4], Q4 + d, g4 * 4 + other))
    sends.append(send(segi.at[1], segi.at[0], SEG_P, right))
    sends.append(send(segi.at[1], segi.at[2], SEG_N, left))
    to_sides(kv0, ROWS, 0, L0_P)
    to_sides(kv1, 512, 128, L1_P)
    to_sides(kv2, 256, 128, L2_P)
    sends.append(send(sq3.at[1 - core], rq3.at[core], Q3, sibling))
    beside = lax.rem(chip + 1 + core * (SEQ // 2 - 2), SEQ // 2)
    for p in range(2):
        send(s3.at[p], r3.at[core, :, core], KV3, beside * 2 + p)
    rq3[core] = sq3[core]
    rq4[a4] = sq4[a4]

    @pl.when(late == 1)
    def _():
        level0(1)
        level0(2)

    @pl.when(owner5)
    def _():
        received(r5.at[1 - late], KV5)
        send(r5.at[1 - late], r5.at[late], KV5_Y, y_on)

    quarter = [pl.ds(128 * core, 64), pl.ds(128 * core + 64, 64)]
    received(wbuf.at[x_down, half], W_L)
    sends.append(send(wbuf.at[x_down, quarter[0]], wbuf.at[x_down, quarter[0]], W2_L, i, x_up))
    sends.append(send(wbuf.at[x_down, half], wbuf.at[x_down, half], W_ON_L, sibling))
    received(wbuf.at[x_up, half], W_R)
    sends.append(send(wbuf.at[x_up, quarter[1]], wbuf.at[x_up, quarter[1]], W2_R, i, x_down))
    sends.append(send(wbuf.at[x_up, half], wbuf.at[x_up, half], W_ON_R, sibling))

    def one_head(ref, queries, place, count):
        tiles = [ref[n].reshape(BLOCK, 128) for n in range(2)]
        out, peak = attend(queries, tiles, [t * hi + lo for t in tiles], None, (place > 0, place < count - 1))
        return jnp.where((lane >= 32) & low_half, peak, out)

    for d in range(1, 4):
        received(rq4.at[lax.rem(a4 + 4 - d, 4)], Q4 + d)
    received(r4, KV4)
    srow4[...] = one_head(r4, rq4[...].reshape(BLOCK, 128), g4, SEQ // 4).reshape(4, 64, 128)
    for d in range(1, 4):
        other = lax.rem(a4 + d, 4)
        sends.append(send(srow4.at[other], rrow4.at[a4], RES4 + d, g4 * 4 + other))
    rrow4[a4] = srow4[a4]

    @pl.when(owner5)
    def _():
        received(rq5.at[pl.ds(0, 7)], Q5)
        received(r5.at[late], KV5_Y)
        srow5[...] = one_head(r5, rq5[...].reshape(BLOCK, 128), g5, SEQ // 8).reshape(8, 32, 128)
        for d in range(1, 8):
            other = lax.rem(a5 + d, 8)
            send(srow5.at[other], rrow5.at[head5], RES5, g5 * 8 + other)
        rrow5[head5] = srow5[a5]

    received(segi.at[0], SEG_P)
    received(segi.at[2], SEG_N)
    segf[pl.ds(0, 8), :] = segi[0].astype(F32)
    segf[pl.ds(16, 8), :] = segi[2].astype(F32)
    for side, (first, row1, row2) in enumerate(((0, 128, 192), (5 * BLOCK, 3 * BLOCK, 2 * BLOCK))):
        received(kv0.at[:, :, pl.ds(first, BLOCK)], L0_P + side)
        for n in range(2):
            rim = jnp.concatenate([kv0[n, p, pl.ds(first, BLOCK), :] for p in range(2)], axis=1)
            rim = jnp.dot(means[:192], rim, preferred_element_type=F32).astype(BF16)
            for p in range(2):
                kv1[n, p, pl.ds(row1, 128), :] = rim[:128, 128 * p : 128 * p + 128]
                kv2[n, p, pl.ds(row2, 64), :] = rim[128:, 128 * p : 128 * p + 128]
    for side, (first, row2) in enumerate(((0, 128), (3 * BLOCK + 128, 2 * BLOCK + 64))):
        received(kv1.at[:, :, pl.ds(first, 128)], L1_P + side)
        for n in range(2):
            rim = jnp.concatenate([kv1[n, p, pl.ds(first, 128), :] for p in range(2)], axis=1)
            rim = jnp.dot(means[:64, :128], rim, preferred_element_type=F32).astype(BF16)
            for p in range(2):
                kv2[n, p, pl.ds(row2, 64), :] = rim[:, 128 * p : 128 * p + 128]

    received(kv2.at[:, :, pl.ds(0, 128)], L2_P)
    received(kv2.at[:, :, pl.ds(2 * BLOCK + 128, 128)], L2_N)

    for n in range(2):
        rows = pl.ds(pl.multiple_of(2 * BLOCK * core, BLOCK), BLOCK)
        rim = jnp.concatenate([kv2[n, p, rows, :] for p in range(2)], axis=1)
        rim = jnp.dot(means[:128], rim, preferred_element_type=F32).astype(BF16)
        for p in range(2):
            sd3[p, n] = rim[:, 128 * p : 128 * p + 128]
    sends.append(send(sd3.at[1 - core], r3.at[core, :, 1 - core], D3, sibling))
    r3[core, :, 1 - core] = sd3[core]

    sides = [pl.ds(0, BLOCK), pl.ds(2 * BLOCK, BLOCK)]
    present = (i > 0, i < SEQ - 1)
    groups = [(q2[p], [kv2[0, p, r, :] for r in sides], [kv2[1, p, r, :] for r in sides], None, present) for p in range(2)]
    for p, state in enumerate(pairs(groups, low_half, lo, hi)):
        for n in range(3):
            st2[n, p] = state[n]
    for b in range(2):
        own = pl.ds(b * BLOCK, BLOCK)
        sides = [own, pl.ds((b + 2) * BLOCK, BLOCK)]
        present = (2 * i + b > 0, 2 * i + b < 2 * SEQ - 1)
        groups = [
            (q1[p, own, :], [kv1[0, p, r, :] for r in sides], [kv1[1, p, r, :] for r in sides], None, present)
            for p in range(2)
        ]
        for p, state in enumerate(pairs(groups, low_half, lo, hi)):
            for n in range(3):
                st1[n, p, own, :] = state[n]

    for p in range(2):
        state = expand(tuple(st2[n, p] for n in range(3)), ex)
        state = merge(state, tuple(st1[n, p] for n in range(3)))
        for n in range(3):
            st1[n, p] = state[n]

    row = lax.broadcasted_iota(jnp.int32, (8, BLOCK), 0)

    def finish(t):
        d = lax.rem(t + HEADX - x, HEADX)
        sums = []
        for p in range(2):
            coarse = expand(tuple(st1[n, p, pl.ds(pl.multiple_of(128 * t, 128), 128), :] for n in range(3)), ex)
            fine = tuple(st0[n, p, pl.ds(pl.multiple_of(BLOCK * t, BLOCK), BLOCK), :] for n in range(3))
            num, total, peak = merge(fine, coarse)
            mean = (num / total).astype(BF16)
            sums.append(jnp.transpose(peak + jnp.log(total)))
            at[t, p] = mean

            @pl.when(d == 0)
            def _():
                ra[x, p] = mean

            @pl.when(d == 1)
            def _():
                send(at.at[t, p], ra.at[x, p], AT_L + p, i, x_up)

            @pl.when(d == 3)
            def _():
                send(at.at[t, p], ra.at[x, p], AT_R + p, i, x_down)

            @pl.when(d == 2)
            def _():
                send(at.at[t, p], via.at[p], VIA + p, i, x_down if p else x_up)

        stat = jnp.where(row < 2, sums[0][0:8], sums[1][0:8])
        stat = jnp.where(row == 1, sums[0][64:72], jnp.where(row == 3, sums[1][64:72], stat))
        sstat[t] = stat

        @pl.when(d == 0)
        def _():
            rstat[x] = stat

        @pl.when(d > 0)
        def _():
            send(sstat.at[t], rstat.at[x], STAT + d, i, t)

    finish(1)
    finish(2)

    received(r3.at[0], KV3)
    received(r3.at[1 - core, :, core], D3)
    received(rq3.at[1 - core], Q3)
    group = (
        rq3[...].reshape(BLOCK, 128),
        [r3[n, 0].reshape(BLOCK, 128) for n in range(2)],
        [r3[n, 1].reshape(BLOCK, 128) for n in range(2)],
        None,
        (chip > 0, chip < SEQ // 2 - 1),
    )
    state = pairs([group], low_half, lo, hi)[0]
    for n in range(3):
        for m in range(2):
            rs3[m, n] = state[n][128 * m : 128 * m + 128]
    sends.append(send(rs3.at[1 - core], st3.at[core], RES3, sibling))
    st3[core] = rs3[core]

    received(wbuf.at[x_far, quarter[0]], W2_L)
    received(wbuf.at[x_far, quarter[1]], W2_R)
    sends.append(send(wbuf.at[x_far, half], wbuf.at[x_far, half], W_ON_2, sibling))

    first = jnp.where(x < 2, 3, 0)
    for t in (first, 3 - first):
        level0(t)
        finish(t)
    received(via.at[0], VIA)
    sends.append(send(via.at[0], ra.at[x_down, 0], AT_2, i, x_up))
    received(via.at[1], VIA + 1)
    sends.append(send(via.at[1], ra.at[x_up, 1], AT_2 + 1, i, x_down))

    for d in range(1, 4):
        received(rrow4.at[lax.rem(a4 + 4 - d, 4)], RES4 + d)

    @pl.when(owner5)
    def _():
        received(rrow5.at[pl.ds(0, 3)], RES5)

    @pl.when(jnp.logical_not(owner5))
    def _():
        received(rrow5, RES5)

    received(st3.at[1 - core], RES3)
    sums = []
    for p in range(2):

        def far(ref):
            even, odd = ref[2 * p], ref[2 * p + 1]
            num = jnp.where(low_half, pltpu.roll(even, 64, 1), odd)
            total = jnp.where(low_half, even[:, 0:1], odd[:, 0:1])
            return num, total, jnp.where(low_half, even[:, 32:33], odd[:, 32:33])

        state = merge(expand(far(rrow5), ex), far(rrow4))
        num, total, peak = merge(expand(state, ex), tuple(st3[p, n] for n in range(3)))
        mean = num / total
        sums.append(peak + jnp.log(total))
        for t in range(4):
            sfar[t, p] = mean[32 * t : 32 * t + 32]
    both = jnp.where(lane < 96, pltpu.roll(sums[1], 64, 1), sums[1])
    both = jnp.where(lane < 32, sums[0], jnp.where(low_half, pltpu.roll(sums[0], 96, 1), both))
    for t in range(4):
        sfar[t, 2] = both[32 * t : 32 * t + 32]
    for d in (2, 1, 3):
        other = lax.rem(x + d, HEADX)
        sends.append(send(sfar.at[other], rfar.at[x], FAR + d, i, other))
    rfar[x] = sfar[x]

    for d in range(1, 4):
        received(rstat.at[lax.rem(x + HEADX - d, HEADX)], STAT + d)
    for m in range(4):
        for p in range(2):
            lines = [jnp.broadcast_to(rstat[m, 2 * p + n : 2 * p + n + 1, :], (64, BLOCK)) for n in range(2)]
            near[m, p] = jnp.transpose(jnp.concatenate(lines, axis=0))

    load_w.wait()
    other_half = pl.ds(128 * (1 - core), 128)
    for owner, slot in ((x_down, W_ON_L), (x_up, W_ON_R), (x_far, W_ON_2)):
        received(wbuf.at[owner, other_half], slot)
    for p in range(2):
        for owner, slot in ((x_down, AT_L), (x_up, AT_R), (x_far, AT_2)):
            received(ra.at[owner, p], slot + p)
    for d in range(1, 4):
        received(rfar.at[lax.rem(x + HEADX - d, HEADX)], FAR + d)

    def spread(rows):
        return jnp.broadcast_to(rows[:, None, :], (32, 8, 128)).reshape(BLOCK, 128)

    attention = []
    for m in range(4):
        for p in range(2):
            sums = jnp.where(low_half, rfar[m, 2, :, 64 * p : 64 * p + 1], rfar[m, 2, :, 64 * p + 32 : 64 * p + 33])
            weight = 1.0 / (1.0 + jnp.exp(spread(sums) - near[m, p]))
            coarse = spread(rfar[m, p])
            attention.append((coarse + weight * (ra[m, p].astype(F32) - coarse)).astype(BF16))
    for n in range(4):
        columns = pl.ds(256 * n, 256)
        total = None
        for m in range(4):
            rows = jnp.concatenate(attention[2 * m : 2 * m + 2], axis=1)
            part = jnp.dot(rows, wbuf[m, :, columns], preferred_element_type=F32)
            total = part if total is None else total + part
        out_ref[:, columns] = total.astype(BF16)

    for copy in sends:
        copy.wait_send()
    sent(s5, KV5)
    for h in range(4):

        @pl.when(a5 != OWNER5[h])
        def _():
            sent(sq5.at[h], Q5)

    @pl.when(owner5)
    def _():
        sent(r5.at[0], KV5_Y)
        sent(srow5.at[pl.ds(0, 7)], RES5)

    sent(r4, KV4)
    sent(r3.at[0], KV3)
    for p in range(2):
        for slot in (AT_L, AT_R, VIA):
            sent(at.at[0, p], slot + p)
    for d in range(1, 4):
        sent(sstat.at[0], STAT + d)


def packed(first, second, h, low_half):
    lanes = slice(128 * (h // 2), 128 * (h // 2) + 128)
    first = first[:, lanes]
    if h % 2:
        first = pltpu.roll(first, 64, 1)
    if second is None:
        return jnp.where(low_half, first, 0.0)
    second = second[:, lanes]
    if h % 2 == 0:
        second = pltpu.roll(second, 64, 1)
    return jnp.where(low_half, first, second)


def on_device(query_rows, key_rows, value_rows, segment, w_out):
    vmem = pltpu.VMEM
    operands = (query_rows, key_rows, value_rows, segment.reshape(8, 128), w_out)
    return pl.pallas_call(
        kernel,
        out_shape=jax.ShapeDtypeStruct((BLOCK, 1024), BF16),
        in_specs=[pl.BlockSpec(memory_space=pl.ANY)] * 5,
        out_specs=pl.BlockSpec(memory_space=vmem),
        scratch_shapes=[
            vmem((2, ROWS, 128), BF16),
            vmem((2, 2, ROWS + 512, 128), BF16),
            vmem((3, 8, 128), jnp.int32),
            vmem((24, 128), F32),
            vmem((2, 512, 128), BF16),
            vmem((2, 2, 1024, 128), BF16),
            vmem((2, 256, 128), BF16),
            vmem((2, 2, 768, 128), BF16),
            vmem((2, 2, 128, 128), BF16),
            vmem((2, 2, 128, 128), BF16),
            vmem((2, 2, 2, 128, 128), BF16),
            vmem((2, 128, 128), BF16),
            vmem((2, 128, 128), BF16),
            vmem((4, 64, 128), BF16),
            vmem((2, 4, 64, 128), BF16),
            vmem((4, 32, 128), BF16),
            vmem((2, 8, 32, 128), BF16),
            vmem((4, 64, 128), BF16),
            vmem((4, 64, 128), BF16),
            vmem((4, 32, 128), BF16),
            vmem((8, 32, 128), BF16),
            vmem((3, 2, ROWS, 128), F32),
            vmem((3, 2, 512, 128), F32),
            vmem((3, 2, 256, 128), F32),
            vmem((2, 3, 128, 128), F32),
            vmem((2, 3, 128, 128), F32),
            vmem((4, 64, 128), F32),
            vmem((4, 64, 128), F32),
            vmem((8, 32, 128), F32),
            vmem((4, 32, 128), F32),
            vmem((3, 512, 128), F32),
            vmem((4, 2, BLOCK, 128), BF16),
            vmem((4, 2, BLOCK, 128), BF16),
            vmem((2, BLOCK, 128), BF16),
            vmem((4, 8, BLOCK), F32),
            vmem((4, 8, BLOCK), F32),
            vmem((4, 3, 32, 128), F32),
            vmem((4, 3, 32, 128), F32),
            vmem((4, 2, BLOCK, 128), F32),
            vmem((4, 256, 1024), BF16),
            pltpu.SemaphoreType.DMA((8,)),
            pltpu.SemaphoreType.DMA((N_SEM,)),
            pltpu.SemaphoreType.DMA((N_SEM,)),
        ],
        compiler_params=pltpu.CompilerParams(
            collective_id=0, has_side_effects=True, vmem_limit_bytes=48 * 2**20
        ),
        name="block_attention",
    )(*[pltpu.with_memory_space_constraint(a, pltpu.HBM) for a in operands])


def solution(mesh):
    placed = (P("seq", "head"), P("seq", "head"), P("seq", "head"), P("seq"), P("head", None))
    return jax.shard_map(
        on_device, mesh=mesh, in_specs=placed, out_specs=P(("seq", "head"), None), check_vma=False
    )
```

```python
import jax
import jax.numpy as jnp
from jax import lax
from jax.experimental import pallas as pl
from jax.experimental.pallas import tpu as pltpu
from jax.sharding import PartitionSpec as P

MESH = pl.DeviceIdType.MESH
F32 = jnp.float32
BF16 = jnp.bfloat16

SEQ = 64
HEADX = 4
BLOCK = 256
ROWS = 1024
NEG = -1e30
BIG = 1e30

SEG_P, SEG_N, L0_P, L0_N, L1_P, L1_N, L2_P, L2_N = range(8)
KV3, KV4, KV5, KV5_Y, Q3, Q5, RES3, RES5 = range(8, 16)
Q4, RES4 = 15, 18
W_L, W_R, W2_L, W2_R, W_ON_L, W_ON_R, W_ON_2 = range(22, 29)
AT_L, AT_R, VIA, AT_2 = 29, 31, 33, 35
STAT, FAR = 36, 39
D3 = 43
N_SEM = 44

OWNER5 = (0, 1, 6, 7)


def averaging():
    row = lax.broadcasted_iota(jnp.int32, (BLOCK, BLOCK), 0)
    token = lax.broadcasted_iota(jnp.int32, (BLOCK, BLOCK), 1)
    result = jnp.zeros((BLOCK, BLOCK), F32)
    base = 0
    for level in range(1, 6):
        count = BLOCK >> level
        first = (row - base) << level
        hit = (row >= base) & (row < base + count) & (token >= first) & (token < first + (1 << level))
        result = jnp.where(hit, 0.5**level, result)
        base += count
    return result.astype(BF16)


def scores_of(q, k):
    return lax.dot_general(q, k, (((1,), (1,)), ((), ())), preferred_element_type=F32)


def attend(q, keys, values, biases, present):
    scores = [scores_of(q, k) for k in keys]
    if biases is not None:
        scores = [s + b for s, b in zip(scores, biases)]
    tops = [jnp.max(s, axis=1, keepdims=True) for s in scores]
    if present is not None:
        tops = [jnp.where(ok, t, NEG) for ok, t in zip(present, tops)]
    peak = tops[0]
    for t in tops[1:]:
        peak = jnp.maximum(peak, t)
    total = None
    for index, (s, v) in enumerate(zip(scores, values)):
        shift = peak if present is None else jnp.where(present[index], peak, BIG)
        probs = jnp.exp(s - shift).astype(BF16)
        part = jnp.dot(probs, v, preferred_element_type=F32)
        total = part if total is None else total + part
    return total, peak


def pairs(groups, low_half, lo, hi):
    all_scores = []
    for q, keys, _, biases, _ in groups:
        q = jnp.concatenate([q * lo, q * hi], axis=0)
        scores = [scores_of(q, k) for k in keys]
        if biases is not None:
            scores = [s + jnp.concatenate([b, b], axis=0) for s, b in zip(scores, biases)]
        all_scores.append(scores)
    ones = jnp.ones((BLOCK, 128), BF16)
    results = []
    for (q, _, values, _, present), scores in zip(groups, all_scores):
        tops = [jnp.max(s, axis=1, keepdims=True) for s in scores]
        if present is not None:
            tops = [jnp.where(ok, t, NEG) for ok, t in zip(present, tops)]
        peak = tops[0]
        for t in tops[1:]:
            peak = jnp.maximum(peak, t)
        out = None
        for index, (s, v) in enumerate(zip(scores, values)):
            shift = peak if present is None else jnp.where(present[index], peak, BIG)
            probs = jnp.exp(s - shift).astype(BF16)
            part = jnp.dot(probs, jnp.concatenate([v, ones], axis=1), preferred_element_type=F32)
            out = part if out is None else out + part
        n = q.shape[0]
        results.append(
            tuple(jnp.where(low_half, w[:n], w[n:]) for w in (out[:, :128], out[:, 128:], peak))
        )
    return results


def merge(a, b):
    peak = jnp.maximum(a[2], b[2])
    scale_a, scale_b = jnp.exp(a[2] - peak), jnp.exp(b[2] - peak)
    return a[0] * scale_a + b[0] * scale_b, a[1] * scale_a + b[1] * scale_b, peak


def expand(parts, ref):
    count = parts[0].shape[0]
    for index, part in enumerate(parts):
        ref[index, pl.ds(0, count, stride=2), :] = part
        ref[index, pl.ds(1, count, stride=2), :] = part
    return tuple(ref[index, 0 : 2 * count, :] for index in range(3))


def kernel(
    q_hbm, k_hbm, v_hbm, seg_hbm, w_hbm, out_ref,
    q0, kv0, segi, segf, q1, kv1, q2, kv2,
    s3, sd3, r3, sq3, rq3, s4, r4, s5, r5, sq4, rq4, sq5, rq5,
    st0, st1, st2, st3, rs3, srow4, rrow4, srow5, rrow5, ex, at, ra, via, sstat, rstat, sfar, rfar, near, wbuf,
    local, snd, rcv,
):
    i = lax.axis_index("seq")
    x = lax.axis_index("head")
    core = lax.rem(i, 2)
    chip = lax.div(i, 2)
    g4, a4 = lax.div(i, 4), lax.rem(i, 4)
    g5, a5 = lax.div(i, 8), lax.rem(i, 8)
    sibling = i + 1 - 2 * core
    right, left = lax.rem(i + 1, SEQ), lax.rem(i + SEQ - 1, SEQ)
    x_up, x_down, x_far = [lax.rem(x + d, HEADX) for d in (1, 3, 2)]
    late = lax.rem(g5, 2)
    beside5 = g5 + 1 - 2 * late
    owner5 = (a5 < 2) | (a5 >= 6)
    head5 = jnp.where(a5 < 2, a5, lax.rem(a5, 4))
    y_on = lax.rem(i + SEQ + 16 - 32 * late, SEQ)

    def remote(src, dst, slot, device):
        return pltpu.make_async_remote_copy(
            src_ref=src, dst_ref=dst, send_sem=snd.at[slot], recv_sem=rcv.at[slot], device_id=device, device_id_type=MESH
        )

    loads = []
    for p in range(2):
        lanes = pl.ds(128 * p, 128)
        loads.append(pltpu.make_async_copy(k_hbm.at[:, lanes], kv0.at[0, p, pl.ds(BLOCK, ROWS)], local.at[p]))
        loads.append(pltpu.make_async_copy(v_hbm.at[:, lanes], kv0.at[1, p, pl.ds(BLOCK, ROWS)], local.at[2 + p]))
        loads.append(pltpu.make_async_copy(q_hbm.at[:, lanes], q0.at[p], local.at[4 + p]))
    loads.append(pltpu.make_async_copy(seg_hbm, segi.at[1], local.at[6]))
    load_w = pltpu.make_async_copy(w_hbm, wbuf.at[x], local.at[7])
    for load in loads:
        load.start()
    load_w.start()

    barrier = pltpu.get_barrier_semaphore()

    def greet(seq, head):
        pl.semaphore_signal(barrier, inc=1, device_id={"seq": seq, "head": head}, device_id_type=MESH)

    blocks4 = [lax.rem(g4 + 1, SEQ // 4), lax.rem(g4 + SEQ // 4 - 1, SEQ // 4)]
    for j in range(8):
        greet(beside5 * 8 + j, x)
    for block in blocks4:
        for j in range(4):
            greet(block * 4 + j, x)
    for d in range(1, 8):
        greet(g5 * 8 + lax.rem(a5 + d, 8), x)
    for other in (x_up, x_down, x_far):
        greet(i, other)
    greet(lax.rem(i + 16, SEQ), x)
    greet(lax.rem(i + SEQ - 16, SEQ), x)

    lane = lax.broadcasted_iota(jnp.int32, (1, 128), 1)
    low_half = lane < 64
    lo_f = jnp.where(low_half, 1.0, 0.0).astype(F32)
    lo = lo_f.astype(BF16)
    hi = (1.0 - lo_f).astype(BF16)
    means = averaging()
    for load in loads:
        load.wait()
    last_k, last_v, last_q = [], [], []
    for t in range(4):
        rows = pl.ds(BLOCK + BLOCK * t, BLOCK)
        ck, cv = [
            jnp.dot(means, jnp.concatenate([kv0[n, 0, rows, :], kv0[n, 1, rows, :]], axis=1), preferred_element_type=F32)
            for n in range(2)
        ]
        own = pl.ds(BLOCK * t, BLOCK)
        cq = 0.125 * jnp.dot(means, jnp.concatenate([q0[0, own, :], q0[1, own, :]], axis=1), preferred_element_type=F32)
        for p in range(2):
            lanes = slice(128 * p, 128 * p + 128)
            q1[p, pl.ds(128 * t, 128), :] = cq[0:128, lanes].astype(BF16)
            q2[p, pl.ds(64 * t, 64), :] = cq[128:192, lanes].astype(BF16)
            sq3[p, pl.ds(32 * t, 32), :] = cq[192:224, lanes].astype(BF16)
            for n, c in enumerate((ck, cv)):
                kv1[n, p, pl.ds(BLOCK + 128 * t, 128), :] = c[0:128, lanes].astype(BF16)
                kv2[n, p, pl.ds(BLOCK + 64 * t, 64), :] = c[128:192, lanes].astype(BF16)
                s3[p, n, pl.ds(32 * t, 32), :] = c[192:224, lanes].astype(BF16)
        for h in range(4):
            s4[h, pl.ds(16 * t, 16), :] = packed(ck[224:240], cv[224:240], h, low_half).astype(BF16)
            sq4[h, pl.ds(16 * t, 16), :] = packed(cq[224:240], None, h, low_half).astype(BF16)
        last_k.append(ck[240:248])
        last_v.append(cv[240:248])
        last_q.append(cq[240:248])
    k5, v5, q5 = [jnp.concatenate(rows, axis=0) for rows in (last_k, last_v, last_q)]
    for h in range(4):
        s5[h] = packed(k5, v5, h, low_half).astype(BF16)
        sq5[h] = packed(q5, None, h, low_half).astype(BF16)

    segf[pl.ds(8, 8), :] = segi[1].astype(F32)

    def bias_of(b, j):
        exists = (4 * i + b + j >= 1) & (4 * i + b + j <= 4 * SEQ)
        first = 6 + 2 * (b + j)
        return [jnp.where(exists, segf[pl.ds(first + n, 1), :], -1.0) for n in range(2)]

    def level0(b):
        own = [
            jnp.transpose(jnp.broadcast_to(segf[pl.ds(8 + 2 * b + n, 1), :], (128, 128))) for n in range(2)
        ]
        own = jnp.concatenate(own, axis=0)
        biases = [
            jnp.concatenate([jnp.where(own == near_by, 0.0, NEG) for near_by in bias_of(b, j)], axis=1) for j in range(3)
        ]
        here = pl.ds(pl.multiple_of(b * BLOCK, BLOCK), BLOCK)
        rows = [pl.ds(pl.multiple_of((b + j) * BLOCK, BLOCK), BLOCK) for j in range(3)]
        groups = [
            (
                q0[p, here, :] * jnp.asarray(0.125, BF16),
                [kv0[0, p, r, :] for r in rows],
                [kv0[1, p, r, :] for r in rows],
                biases,
                None,
            )
            for p in range(2)
        ]
        for p, state in enumerate(pairs(groups, low_half, lo, hi)):
            for n in range(3):
                st0[n, p, here, :] = state[n]

    @pl.when(late == 0)
    def _():
        level0(1)
        level0(2)

    pl.semaphore_wait(barrier, 28)
    sends = []

    def send(src, dst, slot, seq, head=x):
        copy = remote(src, dst, slot, {"seq": seq, "head": head})
        copy.start()
        return copy

    def received(ref, slot):
        pltpu.make_async_copy(ref, ref, rcv.at[slot]).wait()

    def sent(ref, slot):
        pltpu.make_async_copy(ref, ref, snd.at[slot]).wait()

    def to_sides(ref, count, skip, slot):
        n = BLOCK - skip
        sends.append(send(ref.at[:, :, pl.ds(count, n)], ref.at[:, :, pl.ds(0, n)], slot, right))
        sends.append(
            send(
                ref.at[:, :, pl.ds(BLOCK + skip, n)], ref.at[:, :, pl.ds(BLOCK + count + skip, n)], slot + 1, left
            )
        )

    half = pl.ds(128 * core, 128)
    sends.append(send(w_hbm.at[half], wbuf.at[x, half], W_L, i, x_up))
    sends.append(send(w_hbm.at[half], wbuf.at[x, half], W_R, i, x_down))
    for h in range(4):
        send(s5.at[h], r5.at[late, a5], KV5, beside5 * 8 + OWNER5[h])

        @pl.when(a5 != OWNER5[h])
        def _():
            send(sq5.at[h], rq5.at[a5], Q5, g5 * 8 + OWNER5[h])

        @pl.when(a5 == OWNER5[h])
        def _():
            rq5[a5] = sq5[h]

    sends.append(send(segi.at[1], segi.at[0], SEG_P, right))
    sends.append(send(segi.at[1], segi.at[2], SEG_N, left))
    to_sides(kv0, ROWS, 0, L0_P)
    to_sides(kv1, 512, 128, L1_P)
    to_sides(kv2, 256, 128, L2_P)
    for direction, block in enumerate(blocks4):
        for j in range(4):
            send(s4.at[j], r4.at[direction, a4], KV4, block * 4 + j)
    for d in range(1, 4):
        other = lax.rem(a4 + d, 4)
        sends.append(send(sq4.at[other], rq4.at[a4], Q4 + d, g4 * 4 + other))
    sends.append(send(sq3.at[1 - core], rq3.at[core], Q3, sibling))
    beside = lax.rem(chip + 1 + core * (SEQ // 2 - 2), SEQ // 2)
    for p in range(2):
        send(s3.at[p], r3.at[core, :, core], KV3, beside * 2 + p)
    rq3[core] = sq3[core]
    rq4[a4] = sq4[a4]

    @pl.when(late == 1)
    def _():
        level0(1)
        level0(2)

    @pl.when(owner5)
    def _():
        received(r5.at[1 - late], KV5)
        send(r5.at[1 - late], r5.at[late], KV5_Y, y_on)

    quarter = [pl.ds(128 * core, 64), pl.ds(128 * core + 64, 64)]
    received(wbuf.at[x_down, half], W_L)
    sends.append(send(wbuf.at[x_down, quarter[0]], wbuf.at[x_down, quarter[0]], W2_L, i, x_up))
    sends.append(send(wbuf.at[x_down, half], wbuf.at[x_down, half], W_ON_L, sibling))
    received(wbuf.at[x_up, half], W_R)
    sends.append(send(wbuf.at[x_up, quarter[1]], wbuf.at[x_up, quarter[1]], W2_R, i, x_down))
    sends.append(send(wbuf.at[x_up, half], wbuf.at[x_up, half], W_ON_R, sibling))

    def one_head(ref, queries, place, count):
        tiles = [ref[n].reshape(BLOCK, 128) for n in range(2)]
        out, peak = attend(queries, tiles, [t * hi + lo for t in tiles], None, (place > 0, place < count - 1))
        sums = peak + jnp.log(jnp.where(low_half, out, 1.0))
        first = sums.astype(BF16).astype(F32)
        second = (sums - first).astype(BF16).astype(F32)
        third = sums - first - second
        mean = out / pltpu.roll(out, 64, 1)
        parts = jnp.where(lane < 16, first, jnp.where(lane < 32, second, third))
        return jnp.where(low_half, parts, mean).astype(BF16)

    received(segi.at[0], SEG_P)
    received(segi.at[2], SEG_N)
    segf[pl.ds(0, 8), :] = segi[0].astype(F32)
    segf[pl.ds(16, 8), :] = segi[2].astype(F32)
    for side, (first, row1, row2) in enumerate(((0, 128, 192), (5 * BLOCK, 3 * BLOCK, 2 * BLOCK))):
        received(kv0.at[:, :, pl.ds(first, BLOCK)], L0_P + side)
        for n in range(2):
            rim = jnp.concatenate([kv0[n, p, pl.ds(first, BLOCK), :] for p in range(2)], axis=1)
            rim = jnp.dot(means[:192], rim, preferred_element_type=F32).astype(BF16)
            for p in range(2):
                kv1[n, p, pl.ds(row1, 128), :] = rim[:128, 128 * p : 128 * p + 128]
                kv2[n, p, pl.ds(row2, 64), :] = rim[128:, 128 * p : 128 * p + 128]
    level0(0)
    level0(3)

    for side, (first, row2) in enumerate(((0, 128), (3 * BLOCK + 128, 2 * BLOCK + 64))):
        received(kv1.at[:, :, pl.ds(first, 128)], L1_P + side)
        for n in range(2):
            rim = jnp.concatenate([kv1[n, p, pl.ds(first, 128), :] for p in range(2)], axis=1)
            rim = jnp.dot(means[:64, :128], rim, preferred_element_type=F32).astype(BF16)
            for p in range(2):
                kv2[n, p, pl.ds(row2, 64), :] = rim[:, 128 * p : 128 * p + 128]

    received(kv2.at[:, :, pl.ds(0, 128)], L2_P)
    received(kv2.at[:, :, pl.ds(2 * BLOCK + 128, 128)], L2_N)

    for n in range(2):
        rows = pl.ds(pl.multiple_of(2 * BLOCK * core, BLOCK), BLOCK)
        rim = jnp.concatenate([kv2[n, p, rows, :] for p in range(2)], axis=1)
        rim = jnp.dot(means[:128], rim, preferred_element_type=F32).astype(BF16)
        for p in range(2):
            sd3[p, n] = rim[:, 128 * p : 128 * p + 128]
    sends.append(send(sd3.at[1 - core], r3.at[core, :, 1 - core], D3, sibling))
    r3[core, :, 1 - core] = sd3[core]

    sides = [pl.ds(0, BLOCK), pl.ds(2 * BLOCK, BLOCK)]
    present = (i > 0, i < SEQ - 1)
    groups = [(q2[p], [kv2[0, p, r, :] for r in sides], [kv2[1, p, r, :] for r in sides], None, present) for p in range(2)]
    for p, state in enumerate(pairs(groups, low_half, lo, hi)):
        for n in range(3):
            st2[n, p] = state[n]
    for b in range(2):
        own = pl.ds(b * BLOCK, BLOCK)
        sides = [own, pl.ds((b + 2) * BLOCK, BLOCK)]
        present = (2 * i + b > 0, 2 * i + b < 2 * SEQ - 1)
        groups = [
            (q1[p, own, :], [kv1[0, p, r, :] for r in sides], [kv1[1, p, r, :] for r in sides], None, present)
            for p in range(2)
        ]
        for p, state in enumerate(pairs(groups, low_half, lo, hi)):
            for n in range(3):
                st1[n, p, own, :] = state[n]

    for p in range(2):
        state = expand(tuple(st2[n, p] for n in range(3)), ex)
        state = merge(state, tuple(st1[n, p] for n in range(3)))
        for n in range(3):
            st1[n, p] = state[n]

    @pl.when(owner5)
    def _():
        received(rq5.at[pl.ds(0, 7)], Q5)
        received(r5.at[late], KV5_Y)
        srow5[...] = one_head(r5, rq5[...].reshape(BLOCK, 128), g5, SEQ // 8).reshape(8, 32, 128)
        for d in range(1, 8):
            other = lax.rem(a5 + d, 8)
            send(srow5.at[other], rrow5.at[head5], RES5, g5 * 8 + other)
        rrow5[head5] = srow5[a5]

    row = lax.broadcasted_iota(jnp.int32, (8, BLOCK), 0)

    def finish(d):
        t = lax.rem(x + d, HEADX)
        sums = []
        for p in range(2):
            coarse = expand(tuple(st1[n, p, pl.ds(pl.multiple_of(128 * t, 128), 128), :] for n in range(3)), ex)
            fine = tuple(st0[n, p, pl.ds(pl.multiple_of(BLOCK * t, BLOCK), BLOCK), :] for n in range(3))
            num, total, peak = merge(fine, coarse)
            mean = (num / total).astype(BF16)
            sums.append(jnp.transpose(peak + jnp.log(total)))
            if d == 0:
                ra[x, p] = mean
                continue
            at[t, p] = mean
            if d == 1:
                sends.append(send(at.at[t, p], ra.at[x, p], AT_L + p, i, x_up))
            if d == 3:
                sends.append(send(at.at[t, p], ra.at[x, p], AT_R + p, i, x_down))
            if d == 2:
                sends.append(send(at.at[t, p], via.at[p], VIA + p, i, x_down if p else x_up))
        stat = jnp.where(row < 2, sums[0][0:8], sums[1][0:8])
        stat = jnp.where(row == 1, sums[0][64:72], jnp.where(row == 3, sums[1][64:72], stat))
        if d == 0:
            rstat[x] = stat
        else:
            sstat[t] = stat
            sends.append(send(sstat.at[t], rstat.at[x], STAT + d, i, t))

    for d in (2, 1, 3, 0):
        finish(d)

    for d in range(1, 4):
        received(rq4.at[lax.rem(a4 + 4 - d, 4)], Q4 + d)
    received(r4, KV4)
    srow4[...] = one_head(r4, rq4[...].reshape(BLOCK, 128), g4, SEQ // 4).reshape(4, 64, 128)
    for d in range(1, 4):
        other = lax.rem(a4 + d, 4)
        sends.append(send(srow4.at[other], rrow4.at[a4], RES4 + d, g4 * 4 + other))
    rrow4[a4] = srow4[a4]

    received(r3.at[0], KV3)
    received(r3.at[1 - core, :, core], D3)
    received(rq3.at[1 - core], Q3)
    group = (
        rq3[...].reshape(BLOCK, 128),
        [r3[n, 0].reshape(BLOCK, 128) for n in range(2)],
        [r3[n, 1].reshape(BLOCK, 128) for n in range(2)],
        None,
        (chip > 0, chip < SEQ // 2 - 1),
    )
    state = pairs([group], low_half, lo, hi)[0]
    for n in range(3):
        for m in range(2):
            rs3[m, n] = state[n][128 * m : 128 * m + 128]
    sends.append(send(rs3.at[1 - core], st3.at[core], RES3, sibling))
    st3[core] = rs3[core]

    received(wbuf.at[x_far, quarter[0]], W2_L)
    received(wbuf.at[x_far, quarter[1]], W2_R)
    sends.append(send(wbuf.at[x_far, half], wbuf.at[x_far, half], W_ON_2, sibling))

    received(via.at[0], VIA)
    sends.append(send(via.at[0], ra.at[x_down, 0], AT_2, i, x_up))
    received(via.at[1], VIA + 1)
    sends.append(send(via.at[1], ra.at[x_up, 1], AT_2 + 1, i, x_down))

    for d in range(1, 4):
        received(rrow4.at[lax.rem(a4 + 4 - d, 4)], RES4 + d)

    @pl.when(owner5)
    def _():
        received(rrow5.at[pl.ds(0, 3)], RES5)

    @pl.when(jnp.logical_not(owner5))
    def _():
        received(rrow5, RES5)

    received(st3.at[1 - core], RES3)
    sums = []
    for p in range(2):

        def far(ref):
            even, odd = ref[2 * p].astype(F32), ref[2 * p + 1].astype(F32)
            num = jnp.where(low_half, pltpu.roll(even, 64, 1), odd)
            even, odd = [w[:, 0:1] + w[:, 16:17] + w[:, 32:33] for w in (even, odd)]
            return num, jnp.ones_like(num), jnp.where(low_half, even, odd)

        state = merge(expand(far(rrow5), ex), far(rrow4))
        num, total, peak = merge(expand(state, ex), tuple(st3[p, n] for n in range(3)))
        mean = num / total
        sums.append(peak + jnp.log(total))
        for t in range(4):
            sfar[t, p] = mean[32 * t : 32 * t + 32]
    both = jnp.where(lane < 96, pltpu.roll(sums[1], 64, 1), sums[1])
    both = jnp.where(lane < 32, sums[0], jnp.where(low_half, pltpu.roll(sums[0], 96, 1), both))
    for t in range(4):
        sfar[t, 2] = both[32 * t : 32 * t + 32]
    for d in (2, 1, 3):
        other = lax.rem(x + d, HEADX)
        sends.append(send(sfar.at[other], rfar.at[x], FAR + d, i, other))
    rfar[x] = sfar[x]

    for d in range(1, 4):
        received(rstat.at[lax.rem(x + HEADX - d, HEADX)], STAT + d)
    for m in range(4):
        for p in range(2):
            lines = [jnp.broadcast_to(rstat[m, 2 * p + n : 2 * p + n + 1, :], (64, BLOCK)) for n in range(2)]
            near[m, p] = jnp.transpose(jnp.concatenate(lines, axis=0))

    load_w.wait()
    other_half = pl.ds(128 * (1 - core), 128)
    for owner, slot in ((x_down, W_ON_L), (x_up, W_ON_R), (x_far, W_ON_2)):
        received(wbuf.at[owner, other_half], slot)
    for p in range(2):
        for owner, slot in ((x_down, AT_L), (x_up, AT_R), (x_far, AT_2)):
            received(ra.at[owner, p], slot + p)
    for d in range(1, 4):
        received(rfar.at[lax.rem(x + HEADX - d, HEADX)], FAR + d)

    def spread(rows):
        return jnp.broadcast_to(rows[:, None, :], (32, 8, 128)).reshape(BLOCK, 128)

    attention = []
    for m in range(4):
        for p in range(2):
            sums = jnp.where(low_half, rfar[m, 2, :, 64 * p : 64 * p + 1], rfar[m, 2, :, 64 * p + 32 : 64 * p + 33])
            weight = 1.0 / (1.0 + jnp.exp(spread(sums) - near[m, p]))
            coarse = spread(rfar[m, p])
            attention.append((coarse + weight * (ra[m, p].astype(F32) - coarse)).astype(BF16))
    for n in range(4):
        columns = pl.ds(256 * n, 256)
        total = None
        for m in range(4):
            rows = jnp.concatenate(attention[2 * m : 2 * m + 2], axis=1)
            part = jnp.dot(rows, wbuf[m, :, columns], preferred_element_type=F32)
            total = part if total is None else total + part
        out_ref[:, columns] = total.astype(BF16)

    for copy in sends:
        copy.wait_send()
    sent(s5, KV5)
    for h in range(4):

        @pl.when(a5 != OWNER5[h])
        def _():
            sent(sq5.at[h], Q5)

    @pl.when(owner5)
    def _():
        sent(r5.at[0], KV5_Y)
        sent(srow5.at[pl.ds(0, 7)], RES5)

    sent(r4, KV4)
    sent(r3.at[0], KV3)


def packed(first, second, h, low_half):
    lanes = slice(128 * (h // 2), 128 * (h // 2) + 128)
    first = first[:, lanes]
    if h % 2:
        first = pltpu.roll(first, 64, 1)
    if second is None:
        return jnp.where(low_half, first, 0.0)
    second = second[:, lanes]
    if h % 2 == 0:
        second = pltpu.roll(second, 64, 1)
    return jnp.where(low_half, first, second)


def on_device(query_rows, key_rows, value_rows, segment, w_out):
    vmem = pltpu.VMEM
    operands = (query_rows, key_rows, value_rows, segment.reshape(8, 128), w_out)
    return pl.pallas_call(
        kernel,
        out_shape=jax.ShapeDtypeStruct((BLOCK, 1024), BF16),
        in_specs=[pl.BlockSpec(memory_space=pl.ANY)] * 5,
        out_specs=pl.BlockSpec(memory_space=vmem),
        scratch_shapes=[
            vmem((2, ROWS, 128), BF16),
            vmem((2, 2, ROWS + 512, 128), BF16),
            vmem((3, 8, 128), jnp.int32),
            vmem((24, 128), F32),
            vmem((2, 512, 128), BF16),
            vmem((2, 2, 1024, 128), BF16),
            vmem((2, 256, 128), BF16),
            vmem((2, 2, 768, 128), BF16),
            vmem((2, 2, 128, 128), BF16),
            vmem((2, 2, 128, 128), BF16),
            vmem((2, 2, 2, 128, 128), BF16),
            vmem((2, 128, 128), BF16),
            vmem((2, 128, 128), BF16),
            vmem((4, 64, 128), BF16),
            vmem((2, 4, 64, 128), BF16),
            vmem((4, 32, 128), BF16),
            vmem((2, 8, 32, 128), BF16),
            vmem((4, 64, 128), BF16),
            vmem((4, 64, 128), BF16),
            vmem((4, 32, 128), BF16),
            vmem((8, 32, 128), BF16),
            vmem((3, 2, ROWS, 128), F32),
            vmem((3, 2, 512, 128), F32),
            vmem((3, 2, 256, 128), F32),
            vmem((2, 3, 128, 128), F32),
            vmem((2, 3, 128, 128), F32),
            vmem((4, 64, 128), BF16),
            vmem((4, 64, 128), BF16),
            vmem((8, 32, 128), BF16),
            vmem((4, 32, 128), BF16),
            vmem((3, 512, 128), F32),
            vmem((4, 2, BLOCK, 128), BF16),
            vmem((4, 2, BLOCK, 128), BF16),
            vmem((2, BLOCK, 128), BF16),
            vmem((4, 8, BLOCK), F32),
            vmem((4, 8, BLOCK), F32),
            vmem((4, 3, 32, 128), F32),
            vmem((4, 3, 32, 128), F32),
            vmem((4, 2, BLOCK, 128), F32),
            vmem((4, 256, 1024), BF16),
            pltpu.SemaphoreType.DMA((8,)),
            pltpu.SemaphoreType.DMA((N_SEM,)),
            pltpu.SemaphoreType.DMA((N_SEM,)),
        ],
        compiler_params=pltpu.CompilerParams(
            collective_id=0, has_side_effects=True, vmem_limit_bytes=48 * 2**20
        ),
        name="block_attention",
    )(*[pltpu.with_memory_space_constraint(a, pltpu.HBM) for a in operands])


def solution(mesh):
    placed = (P("seq", "head"), P("seq", "head"), P("seq", "head"), P("seq"), P("head", None))
    return jax.shard_map(
        on_device, mesh=mesh, in_specs=placed, out_specs=P(("seq", "head"), None), check_vma=False
    )
```

```python
import jax
import jax.numpy as jnp
from jax import lax
from jax.experimental import pallas as pl
from jax.experimental.pallas import tpu as pltpu
from jax.sharding import PartitionSpec as P

MESH = pl.DeviceIdType.MESH
F32 = jnp.float32
BF16 = jnp.bfloat16

SEQ = 64
HEADX = 4
BLOCK = 256
ROWS = 1024
NEG = -1e30
BIG = 1e30

SEG_P, SEG_N, L0_P, L0_N, L1_P, L1_N, L2_P, L2_N = range(8)
KV3, KV4, KV5, KV5_Y, Q3, Q5, RES3, RES5 = range(8, 16)
Q4, RES4 = 15, 18
W_L, W_R, W2_L, W2_R, W_ON_L, W_ON_R, W_ON_2 = range(22, 29)
AT_L, AT_R, VIA, AT_2 = 29, 31, 33, 35
STAT, FAR = 36, 39
D3 = 43
N_SEM = 44

OWNER5 = (0, 1, 6, 7)


def averaging():
    row = lax.broadcasted_iota(jnp.int32, (BLOCK, BLOCK), 0)
    token = lax.broadcasted_iota(jnp.int32, (BLOCK, BLOCK), 1)
    result = jnp.zeros((BLOCK, BLOCK), F32)
    base = 0
    for level in range(1, 6):
        count = BLOCK >> level
        first = (row - base) << level
        hit = (row >= base) & (row < base + count) & (token >= first) & (token < first + (1 << level))
        result = jnp.where(hit, 0.5**level, result)
        base += count
    return result.astype(BF16)


def scores_of(q, k):
    return lax.dot_general(q, k, (((1,), (1,)), ((), ())), preferred_element_type=F32)


def attend(q, keys, values, biases, present):
    scores = [scores_of(q, k) for k in keys]
    if biases is not None:
        scores = [s + b for s, b in zip(scores, biases)]
    tops = [jnp.max(s, axis=1, keepdims=True) for s in scores]
    if present is not None:
        tops = [jnp.where(ok, t, NEG) for ok, t in zip(present, tops)]
    peak = tops[0]
    for t in tops[1:]:
        peak = jnp.maximum(peak, t)
    total = None
    for index, (s, v) in enumerate(zip(scores, values)):
        shift = peak if present is None else jnp.where(present[index], peak, BIG)
        probs = jnp.exp(s - shift).astype(BF16)
        part = jnp.dot(probs, v, preferred_element_type=F32)
        total = part if total is None else total + part
    return total, peak


def pairs(groups, low_half, lo, hi):
    all_scores = []
    for q, keys, _, biases, _ in groups:
        q = jnp.concatenate([q * lo, q * hi], axis=0)
        scores = [scores_of(q, k) for k in keys]
        if biases is not None:
            scores = [s + jnp.concatenate([b, b], axis=0) for s, b in zip(scores, biases)]
        all_scores.append(scores)
    ones = jnp.ones((BLOCK, 128), BF16)
    results = []
    for (q, _, values, _, present), scores in zip(groups, all_scores):
        tops = [jnp.max(s, axis=1, keepdims=True) for s in scores]
        if present is not None:
            tops = [jnp.where(ok, t, NEG) for ok, t in zip(present, tops)]
        peak = tops[0]
        for t in tops[1:]:
            peak = jnp.maximum(peak, t)
        out = None
        for index, (s, v) in enumerate(zip(scores, values)):
            shift = peak if present is None else jnp.where(present[index], peak, BIG)
            probs = jnp.exp(s - shift).astype(BF16)
            part = jnp.dot(probs, jnp.concatenate([v, ones], axis=1), preferred_element_type=F32)
            out = part if out is None else out + part
        n = q.shape[0]
        results.append(
            tuple(jnp.where(low_half, w[:n], w[n:]) for w in (out[:, :128], out[:, 128:], peak))
        )
    return results


def merge(a, b):
    peak = jnp.maximum(a[2], b[2])
    scale_a, scale_b = jnp.exp(a[2] - peak), jnp.exp(b[2] - peak)
    return a[0] * scale_a + b[0] * scale_b, a[1] * scale_a + b[1] * scale_b, peak


def expand(parts, ref):
    count = parts[0].shape[0]
    for index, part in enumerate(parts):
        ref[index, pl.ds(0, count, stride=2), :] = part
        ref[index, pl.ds(1, count, stride=2), :] = part
    return tuple(ref[index, 0 : 2 * count, :] for index in range(3))


def kernel(
    q_hbm, k_hbm, v_hbm, seg_hbm, w_hbm, out_ref,
    q0, kv0, segi, segf, q1, kv1, q2, kv2,
    s3, sd3, r3, sq3, rq3, s4, r4, s5, r5, sq4, rq4, sq5, rq5,
    st0, st1, st2, st3, rs3, srow4, rrow4, srow5, rrow5, ex, at, ra, via, sstat, rstat, sfar, rfar, near, wbuf,
    local, snd, rcv,
):
    i = lax.axis_index("seq")
    x = lax.axis_index("head")
    core = lax.rem(i, 2)
    chip = lax.div(i, 2)
    g4, a4 = lax.div(i, 4), lax.rem(i, 4)
    g5, a5 = lax.div(i, 8), lax.rem(i, 8)
    sibling = i + 1 - 2 * core
    right, left = lax.rem(i + 1, SEQ), lax.rem(i + SEQ - 1, SEQ)
    x_up, x_down, x_far = [lax.rem(x + d, HEADX) for d in (1, 3, 2)]
    late = lax.rem(g5, 2)
    beside5 = g5 + 1 - 2 * late
    owner5 = (a5 < 2) | (a5 >= 6)
    head5 = jnp.where(a5 < 2, a5, lax.rem(a5, 4))
    y_on = lax.rem(i + SEQ + 16 - 32 * late, SEQ)

    def remote(src, dst, slot, device):
        return pltpu.make_async_remote_copy(
            src_ref=src, dst_ref=dst, send_sem=snd.at[slot], recv_sem=rcv.at[slot], device_id=device, device_id_type=MESH
        )

    loads = []
    for p in range(2):
        lanes = pl.ds(128 * p, 128)
        loads.append(pltpu.make_async_copy(k_hbm.at[:, lanes], kv0.at[0, p, pl.ds(BLOCK, ROWS)], local.at[p]))
        loads.append(pltpu.make_async_copy(v_hbm.at[:, lanes], kv0.at[1, p, pl.ds(BLOCK, ROWS)], local.at[2 + p]))
        loads.append(pltpu.make_async_copy(q_hbm.at[:, lanes], q0.at[p], local.at[4 + p]))
    loads.append(pltpu.make_async_copy(seg_hbm, segi.at[1], local.at[6]))
    load_w = pltpu.make_async_copy(w_hbm, wbuf.at[x], local.at[7])
    for load in loads:
        load.start()
    load_w.start()

    barrier = pltpu.get_barrier_semaphore()

    def greet(seq, head):
        pl.semaphore_signal(barrier, inc=1, device_id={"seq": seq, "head": head}, device_id_type=MESH)

    blocks4 = [lax.rem(g4 + 1, SEQ // 4), lax.rem(g4 + SEQ // 4 - 1, SEQ // 4)]
    for j in range(8):
        greet(beside5 * 8 + j, x)
    for block in blocks4:
        for j in range(4):
            greet(block * 4 + j, x)
    for d in range(1, 8):
        greet(g5 * 8 + lax.rem(a5 + d, 8), x)
    for other in (x_up, x_down, x_far):
        greet(i, other)
    greet(lax.rem(i + 16, SEQ), x)
    greet(lax.rem(i + SEQ - 16, SEQ), x)

    lane = lax.broadcasted_iota(jnp.int32, (1, 128), 1)
    low_half = lane < 64
    lo_f = jnp.where(low_half, 1.0, 0.0).astype(F32)
    lo = lo_f.astype(BF16)
    hi = (1.0 - lo_f).astype(BF16)
    means = averaging()
    for load in loads:
        load.wait()
    last_k, last_v, last_q = [], [], []
    for t in range(4):
        rows = pl.ds(BLOCK + BLOCK * t, BLOCK)
        ck, cv = [
            jnp.dot(means, jnp.concatenate([kv0[n, 0, rows, :], kv0[n, 1, rows, :]], axis=1), preferred_element_type=F32)
            for n in range(2)
        ]
        own = pl.ds(BLOCK * t, BLOCK)
        cq = 0.125 * jnp.dot(means, jnp.concatenate([q0[0, own, :], q0[1, own, :]], axis=1), preferred_element_type=F32)
        for p in range(2):
            lanes = slice(128 * p, 128 * p + 128)
            q1[p, pl.ds(128 * t, 128), :] = cq[0:128, lanes].astype(BF16)
            q2[p, pl.ds(64 * t, 64), :] = cq[128:192, lanes].astype(BF16)
            sq3[p, pl.ds(32 * t, 32), :] = cq[192:224, lanes].astype(BF16)
            for n, c in enumerate((ck, cv)):
                kv1[n, p, pl.ds(BLOCK + 128 * t, 128), :] = c[0:128, lanes].astype(BF16)
                kv2[n, p, pl.ds(BLOCK + 64 * t, 64), :] = c[128:192, lanes].astype(BF16)
                s3[p, n, pl.ds(32 * t, 32), :] = c[192:224, lanes].astype(BF16)
        for h in range(4):
            s4[h, pl.ds(16 * t, 16), :] = packed(ck[224:240], cv[224:240], h, low_half).astype(BF16)
            sq4[h, pl.ds(16 * t, 16), :] = packed(cq[224:240], None, h, low_half).astype(BF16)
        last_k.append(ck[240:248])
        last_v.append(cv[240:248])
        last_q.append(cq[240:248])
    k5, v5, q5 = [jnp.concatenate(rows, axis=0) for rows in (last_k, last_v, last_q)]
    for h in range(4):
        s5[h] = packed(k5, v5, h, low_half).astype(BF16)
        sq5[h] = packed(q5, None, h, low_half).astype(BF16)

    segf[pl.ds(8, 8), :] = segi[1].astype(F32)

    def bias_of(b, j):
        exists = (4 * i + b + j >= 1) & (4 * i + b + j <= 4 * SEQ)
        first = 6 + 2 * (b + j)
        return [jnp.where(exists, segf[pl.ds(first + n, 1), :], -1.0) for n in range(2)]

    def level0(b):
        own = [
            jnp.transpose(jnp.broadcast_to(segf[pl.ds(8 + 2 * b + n, 1), :], (128, 128))) for n in range(2)
        ]
        own = jnp.concatenate(own, axis=0)
        biases = [
            jnp.concatenate([jnp.where(own == near_by, 0.0, NEG) for near_by in bias_of(b, j)], axis=1) for j in range(3)
        ]
        here = pl.ds(pl.multiple_of(b * BLOCK, BLOCK), BLOCK)
        rows = [pl.ds(pl.multiple_of((b + j) * BLOCK, BLOCK), BLOCK) for j in range(3)]
        groups = [
            (
                q0[p, here, :] * jnp.asarray(0.125, BF16),
                [kv0[0, p, r, :] for r in rows],
                [kv0[1, p, r, :] for r in rows],
                biases,
                None,
            )
            for p in range(2)
        ]
        for p, state in enumerate(pairs(groups, low_half, lo, hi)):
            for n in range(3):
                st0[n, p, here, :] = state[n]

    @pl.when(late == 0)
    def _():
        level0(1)
        level0(2)

    pl.semaphore_wait(barrier, 28)
    sends = []

    def send(src, dst, slot, seq, head=x):
        copy = remote(src, dst, slot, {"seq": seq, "head": head})
        copy.start()
        return copy

    def received(ref, slot):
        pltpu.make_async_copy(ref, ref, rcv.at[slot]).wait()

    def sent(ref, slot):
        pltpu.make_async_copy(ref, ref, snd.at[slot]).wait()

    def to_sides(ref, count, skip, slot):
        n = BLOCK - skip
        sends.append(send(ref.at[:, :, pl.ds(count, n)], ref.at[:, :, pl.ds(0, n)], slot, right))
        sends.append(
            send(
                ref.at[:, :, pl.ds(BLOCK + skip, n)], ref.at[:, :, pl.ds(BLOCK + count + skip, n)], slot + 1, left
            )
        )

    half = pl.ds(128 * core, 128)
    sends.append(send(w_hbm.at[half], wbuf.at[x, half], W_L, i, x_up))
    sends.append(send(w_hbm.at[half], wbuf.at[x, half], W_R, i, x_down))
    for h in range(4):
        send(s5.at[h], r5.at[late, a5], KV5, beside5 * 8 + OWNER5[h])

        @pl.when(a5 != OWNER5[h])
        def _():
            send(sq5.at[h], rq5.at[a5], Q5, g5 * 8 + OWNER5[h])

        @pl.when(a5 == OWNER5[h])
        def _():
            rq5[a5] = sq5[h]

    sends.append(send(segi.at[1], segi.at[0], SEG_P, right))
    sends.append(send(segi.at[1], segi.at[2], SEG_N, left))
    to_sides(kv0, ROWS, 0, L0_P)
    to_sides(kv1, 512, 128, L1_P)
    to_sides(kv2, 256, 128, L2_P)
    for direction, block in enumerate(blocks4):
        for j in range(4):
            send(s4.at[j], r4.at[direction, a4], KV4, block * 4 + j)
    for d in range(1, 4):
        other = lax.rem(a4 + d, 4)
        sends.append(send(sq4.at[other], rq4.at[a4], Q4 + d, g4 * 4 + other))
    sends.append(send(sq3.at[1 - core], rq3.at[core], Q3, sibling))
    beside = lax.rem(chip + 1 + core * (SEQ // 2 - 2), SEQ // 2)
    for p in range(2):
        send(s3.at[p], r3.at[core, :, core], KV3, beside * 2 + p)
    rq3[core] = sq3[core]
    rq4[a4] = sq4[a4]

    @pl.when(late == 1)
    def _():
        level0(1)
        level0(2)

    @pl.when(owner5)
    def _():
        received(r5.at[1 - late], KV5)
        send(r5.at[1 - late], r5.at[late], KV5_Y, y_on)

    def one_head(ref, queries, place, count):
        tiles = [ref[n].reshape(BLOCK, 128) for n in range(2)]
        out, peak = attend(queries, tiles, [t * hi + lo for t in tiles], None, (place > 0, place < count - 1))
        sums = peak + jnp.log(jnp.where(low_half, out, 1.0))
        first = sums.astype(BF16).astype(F32)
        second = (sums - first).astype(BF16).astype(F32)
        third = sums - first - second
        mean = out / pltpu.roll(out, 64, 1)
        parts = jnp.where(lane < 16, first, jnp.where(lane < 32, second, third))
        return jnp.where(low_half, parts, mean).astype(BF16)

    received(segi.at[0], SEG_P)
    received(segi.at[2], SEG_N)
    segf[pl.ds(0, 8), :] = segi[0].astype(F32)
    segf[pl.ds(16, 8), :] = segi[2].astype(F32)
    for side, (first, row1, row2) in enumerate(((0, 128, 192), (5 * BLOCK, 3 * BLOCK, 2 * BLOCK))):
        received(kv0.at[:, :, pl.ds(first, BLOCK)], L0_P + side)
        for n in range(2):
            rim = jnp.concatenate([kv0[n, p, pl.ds(first, BLOCK), :] for p in range(2)], axis=1)
            rim = jnp.dot(means[:192], rim, preferred_element_type=F32).astype(BF16)
            for p in range(2):
                kv1[n, p, pl.ds(row1, 128), :] = rim[:128, 128 * p : 128 * p + 128]
                kv2[n, p, pl.ds(row2, 64), :] = rim[128:, 128 * p : 128 * p + 128]
    level0(0)
    level0(3)

    quarter = [pl.ds(128 * core, 64), pl.ds(128 * core + 64, 64)]
    received(wbuf.at[x_down, half], W_L)
    sends.append(send(wbuf.at[x_down, quarter[0]], wbuf.at[x_down, quarter[0]], W2_L, i, x_up))
    sends.append(send(wbuf.at[x_down, half], wbuf.at[x_down, half], W_ON_L, sibling))
    received(wbuf.at[x_up, half], W_R)
    sends.append(send(wbuf.at[x_up, quarter[1]], wbuf.at[x_up, quarter[1]], W2_R, i, x_down))
    sends.append(send(wbuf.at[x_up, half], wbuf.at[x_up, half], W_ON_R, sibling))

    for side, (first, row2) in enumerate(((0, 128), (3 * BLOCK + 128, 2 * BLOCK + 64))):
        received(kv1.at[:, :, pl.ds(first, 128)], L1_P + side)
        for n in range(2):
            rim = jnp.concatenate([kv1[n, p, pl.ds(first, 128), :] for p in range(2)], axis=1)
            rim = jnp.dot(means[:64, :128], rim, preferred_element_type=F32).astype(BF16)
            for p in range(2):
                kv2[n, p, pl.ds(row2, 64), :] = rim[:, 128 * p : 128 * p + 128]

    received(kv2.at[:, :, pl.ds(0, 128)], L2_P)
    received(kv2.at[:, :, pl.ds(2 * BLOCK + 128, 128)], L2_N)

    for n in range(2):
        rows = pl.ds(pl.multiple_of(2 * BLOCK * core, BLOCK), BLOCK)
        rim = jnp.concatenate([kv2[n, p, rows, :] for p in range(2)], axis=1)
        rim = jnp.dot(means[:128], rim, preferred_element_type=F32).astype(BF16)
        for p in range(2):
            sd3[p, n] = rim[:, 128 * p : 128 * p + 128]
    sends.append(send(sd3.at[1 - core], r3.at[core, :, 1 - core], D3, sibling))
    r3[core, :, 1 - core] = sd3[core]

    sides = [pl.ds(0, BLOCK), pl.ds(2 * BLOCK, BLOCK)]
    present = (i > 0, i < SEQ - 1)
    groups = [(q2[p], [kv2[0, p, r, :] for r in sides], [kv2[1, p, r, :] for r in sides], None, present) for p in range(2)]
    for p, state in enumerate(pairs(groups, low_half, lo, hi)):
        for n in range(3):
            st2[n, p] = state[n]
    for b in range(2):
        own = pl.ds(b * BLOCK, BLOCK)
        sides = [own, pl.ds((b + 2) * BLOCK, BLOCK)]
        present = (2 * i + b > 0, 2 * i + b < 2 * SEQ - 1)
        groups = [
            (q1[p, own, :], [kv1[0, p, r, :] for r in sides], [kv1[1, p, r, :] for r in sides], None, present)
            for p in range(2)
        ]
        for p, state in enumerate(pairs(groups, low_half, lo, hi)):
            for n in range(3):
                st1[n, p, own, :] = state[n]

    for p in range(2):
        state = expand(tuple(st2[n, p] for n in range(3)), ex)
        state = merge(state, tuple(st1[n, p] for n in range(3)))
        for n in range(3):
            st1[n, p] = state[n]

    @pl.when(owner5)
    def _():
        received(rq5.at[pl.ds(0, 7)], Q5)
        received(r5.at[late], KV5_Y)
        srow5[...] = one_head(r5, rq5[...].reshape(BLOCK, 128), g5, SEQ // 8).reshape(8, 32, 128)
        for d in range(1, 8):
            other = lax.rem(a5 + d, 8)
            send(srow5.at[other], rrow5.at[head5], RES5, g5 * 8 + other)
        rrow5[head5] = srow5[a5]

    row = lax.broadcasted_iota(jnp.int32, (8, BLOCK), 0)

    def finish(d):
        t = lax.rem(x + d, HEADX)
        sums = []
        for p in range(2):
            coarse = expand(tuple(st1[n, p, pl.ds(pl.multiple_of(128 * t, 128), 128), :] for n in range(3)), ex)
            fine = tuple(st0[n, p, pl.ds(pl.multiple_of(BLOCK * t, BLOCK), BLOCK), :] for n in range(3))
            num, total, peak = merge(fine, coarse)
            mean = (num / total).astype(BF16)
            sums.append(jnp.transpose(peak + jnp.log(total)))
            if d == 0:
                ra[x, p] = mean
                continue
            at[t, p] = mean
            if d == 1:
                sends.append(send(at.at[t, p], ra.at[x, p], AT_L + p, i, x_up))
            if d == 3:
                sends.append(send(at.at[t, p], ra.at[x, p], AT_R + p, i, x_down))
            if d == 2:
                sends.append(send(at.at[t, p], via.at[p], VIA + p, i, x_down if p else x_up))
        stat = jnp.where(row < 2, sums[0][0:8], sums[1][0:8])
        stat = jnp.where(row == 1, sums[0][64:72], jnp.where(row == 3, sums[1][64:72], stat))
        if d == 0:
            rstat[x] = stat
        else:
            sstat[t] = stat
            sends.append(send(sstat.at[t], rstat.at[x], STAT + d, i, t))

    for d in (2, 1, 3, 0):
        finish(d)

    for d in range(1, 4):
        received(rq4.at[lax.rem(a4 + 4 - d, 4)], Q4 + d)
    received(r4, KV4)
    srow4[...] = one_head(r4, rq4[...].reshape(BLOCK, 128), g4, SEQ // 4).reshape(4, 64, 128)
    for d in range(1, 4):
        other = lax.rem(a4 + d, 4)
        sends.append(send(srow4.at[other], rrow4.at[a4], RES4 + d, g4 * 4 + other))
    rrow4[a4] = srow4[a4]

    received(r3.at[0], KV3)
    received(r3.at[1 - core, :, core], D3)
    received(rq3.at[1 - core], Q3)
    group = (
        rq3[...].reshape(BLOCK, 128),
        [r3[n, 0].reshape(BLOCK, 128) for n in range(2)],
        [r3[n, 1].reshape(BLOCK, 128) for n in range(2)],
        None,
        (chip > 0, chip < SEQ // 2 - 1),
    )
    state = pairs([group], low_half, lo, hi)[0]
    for n in range(3):
        for m in range(2):
            rs3[m, n] = state[n][128 * m : 128 * m + 128]
    sends.append(send(rs3.at[1 - core], st3.at[core], RES3, sibling))
    st3[core] = rs3[core]

    received(wbuf.at[x_far, quarter[0]], W2_L)
    received(wbuf.at[x_far, quarter[1]], W2_R)
    sends.append(send(wbuf.at[x_far, half], wbuf.at[x_far, half], W_ON_2, sibling))

    received(via.at[0], VIA)
    sends.append(send(via.at[0], ra.at[x_down, 0], AT_2, i, x_up))
    received(via.at[1], VIA + 1)
    sends.append(send(via.at[1], ra.at[x_up, 1], AT_2 + 1, i, x_down))

    for d in range(1, 4):
        received(rrow4.at[lax.rem(a4 + 4 - d, 4)], RES4 + d)

    @pl.when(owner5)
    def _():
        received(rrow5.at[pl.ds(0, 3)], RES5)

    @pl.when(jnp.logical_not(owner5))
    def _():
        received(rrow5, RES5)

    received(st3.at[1 - core], RES3)
    sums = []
    for p in range(2):

        def far(ref):
            even, odd = ref[2 * p].astype(F32), ref[2 * p + 1].astype(F32)
            num = jnp.where(low_half, pltpu.roll(even, 64, 1), odd)
            even, odd = [w[:, 0:1] + w[:, 16:17] + w[:, 32:33] for w in (even, odd)]
            return num, jnp.ones_like(num), jnp.where(low_half, even, odd)

        state = merge(expand(far(rrow5), ex), far(rrow4))
        num, total, peak = merge(expand(state, ex), tuple(st3[p, n] for n in range(3)))
        mean = num / total
        sums.append(peak + jnp.log(total))
        for t in range(4):
            sfar[t, p] = mean[32 * t : 32 * t + 32].astype(BF16)
    both = jnp.where(lane < 96, pltpu.roll(sums[1], 64, 1), sums[1])
    both = jnp.where(lane < 32, sums[0], jnp.where(low_half, pltpu.roll(sums[0], 96, 1), both))
    high = both.astype(BF16).astype(F32)
    middle = (both - high).astype(BF16).astype(F32)
    place = lax.rem(lane, 32)
    both = jnp.where(place < 8, high, jnp.where(place < 16, middle, both - high - middle)).astype(BF16)
    for t in range(4):
        sfar[t, 2] = both[32 * t : 32 * t + 32]
    for d in (2, 1, 3):
        other = lax.rem(x + d, HEADX)
        sends.append(send(sfar.at[other], rfar.at[x], FAR + d, i, other))
    rfar[x] = sfar[x]

    for d in range(1, 4):
        received(rstat.at[lax.rem(x + HEADX - d, HEADX)], STAT + d)
    for m in range(4):
        for p in range(2):
            lines = [jnp.broadcast_to(rstat[m, 2 * p + n : 2 * p + n + 1, :], (64, BLOCK)) for n in range(2)]
            near[m, p] = jnp.transpose(jnp.concatenate(lines, axis=0))

    load_w.wait()
    other_half = pl.ds(128 * (1 - core), 128)
    for owner, slot in ((x_down, W_ON_L), (x_up, W_ON_R), (x_far, W_ON_2)):
        received(wbuf.at[owner, other_half], slot)
    for p in range(2):
        for owner, slot in ((x_down, AT_L), (x_up, AT_R), (x_far, AT_2)):
            received(ra.at[owner, p], slot + p)
    for d in range(1, 4):
        received(rfar.at[lax.rem(x + HEADX - d, HEADX)], FAR + d)

    def spread(rows):
        return jnp.broadcast_to(rows[:, None, :], (32, 8, 128)).reshape(BLOCK, 128)

    attention = []
    for m in range(4):
        for p in range(2):
            parts = rfar[m, 2].astype(F32)
            even, odd = [
                parts[:, n : n + 1] + parts[:, n + 8 : n + 9] + parts[:, n + 16 : n + 17] for n in (64 * p, 64 * p + 32)
            ]
            sums = jnp.where(low_half, even, odd)
            weight = 1.0 / (1.0 + jnp.exp(spread(sums) - near[m, p]))
            coarse = spread(rfar[m, p].astype(F32))
            attention.append((coarse + weight * (ra[m, p].astype(F32) - coarse)).astype(BF16))
    for n in range(4):
        columns = pl.ds(256 * n, 256)
        total = None
        for m in range(4):
            rows = jnp.concatenate(attention[2 * m : 2 * m + 2], axis=1)
            part = jnp.dot(rows, wbuf[m, :, columns], preferred_element_type=F32)
            total = part if total is None else total + part
        out_ref[:, columns] = total.astype(BF16)

    for copy in sends:
        copy.wait_send()
    sent(s5, KV5)
    for h in range(4):

        @pl.when(a5 != OWNER5[h])
        def _():
            sent(sq5.at[h], Q5)

    @pl.when(owner5)
    def _():
        sent(r5.at[0], KV5_Y)
        sent(srow5.at[pl.ds(0, 7)], RES5)

    sent(r4, KV4)
    sent(r3.at[0], KV3)


def packed(first, second, h, low_half):
    lanes = slice(128 * (h // 2), 128 * (h // 2) + 128)
    first = first[:, lanes]
    if h % 2:
        first = pltpu.roll(first, 64, 1)
    if second is None:
        return jnp.where(low_half, first, 0.0)
    second = second[:, lanes]
    if h % 2 == 0:
        second = pltpu.roll(second, 64, 1)
    return jnp.where(low_half, first, second)


def on_device(query_rows, key_rows, value_rows, segment, w_out):
    vmem = pltpu.VMEM
    operands = (query_rows, key_rows, value_rows, segment.reshape(8, 128), w_out)
    return pl.pallas_call(
        kernel,
        out_shape=jax.ShapeDtypeStruct((BLOCK, 1024), BF16),
        in_specs=[pl.BlockSpec(memory_space=pl.ANY)] * 5,
        out_specs=pl.BlockSpec(memory_space=vmem),
        scratch_shapes=[
            vmem((2, ROWS, 128), BF16),
            vmem((2, 2, ROWS + 512, 128), BF16),
            vmem((3, 8, 128), jnp.int32),
            vmem((24, 128), F32),
            vmem((2, 512, 128), BF16),
            vmem((2, 2, 1024, 128), BF16),
            vmem((2, 256, 128), BF16),
            vmem((2, 2, 768, 128), BF16),
            vmem((2, 2, 128, 128), BF16),
            vmem((2, 2, 128, 128), BF16),
            vmem((2, 2, 2, 128, 128), BF16),
            vmem((2, 128, 128), BF16),
            vmem((2, 128, 128), BF16),
            vmem((4, 64, 128), BF16),
            vmem((2, 4, 64, 128), BF16),
            vmem((4, 32, 128), BF16),
            vmem((2, 8, 32, 128), BF16),
            vmem((4, 64, 128), BF16),
            vmem((4, 64, 128), BF16),
            vmem((4, 32, 128), BF16),
            vmem((8, 32, 128), BF16),
            vmem((3, 2, ROWS, 128), F32),
            vmem((3, 2, 512, 128), F32),
            vmem((3, 2, 256, 128), F32),
            vmem((2, 3, 128, 128), F32),
            vmem((2, 3, 128, 128), F32),
            vmem((4, 64, 128), BF16),
            vmem((4, 64, 128), BF16),
            vmem((8, 32, 128), BF16),
            vmem((4, 32, 128), BF16),
            vmem((3, 512, 128), F32),
            vmem((4, 2, BLOCK, 128), BF16),
            vmem((4, 2, BLOCK, 128), BF16),
            vmem((2, BLOCK, 128), BF16),
            vmem((4, 8, BLOCK), F32),
            vmem((4, 8, BLOCK), F32),
            vmem((4, 3, 32, 128), BF16),
            vmem((4, 3, 32, 128), BF16),
            vmem((4, 2, BLOCK, 128), F32),
            vmem((4, 256, 1024), BF16),
            pltpu.SemaphoreType.DMA((8,)),
            pltpu.SemaphoreType.DMA((N_SEM,)),
            pltpu.SemaphoreType.DMA((N_SEM,)),
        ],
        compiler_params=pltpu.CompilerParams(
            collective_id=0, has_side_effects=True, vmem_limit_bytes=48 * 2**20
        ),
        name="block_attention",
    )(*[pltpu.with_memory_space_constraint(a, pltpu.HBM) for a in operands])


def solution(mesh):
    placed = (P("seq", "head"), P("seq", "head"), P("seq", "head"), P("seq"), P("head", None))
    return jax.shard_map(
        on_device, mesh=mesh, in_specs=placed, out_specs=P(("seq", "head"), None), check_vma=False
    )
```

```python
import jax
import jax.numpy as jnp
from jax import lax
from jax.experimental import pallas as pl
from jax.experimental.pallas import tpu as pltpu
from jax.sharding import PartitionSpec as P

MESH = pl.DeviceIdType.MESH
F32 = jnp.float32
BF16 = jnp.bfloat16

SEQ = 64
HEADX = 4
BLOCK = 256
ROWS = 1024
NEG = -1e30
BIG = 1e30

SEG_P, SEG_N, L0_P, L0_N, L1_P, L1_N, L2_P, L2_N = range(8)
KV3, KV4, KV5, KV5_Y, Q3, Q5, RES3, RES5 = range(8, 16)
Q4, RES4 = 15, 18
W_L, W_R, W2_L, W2_R, W_ON_L, W_ON_R, W_ON_2 = range(22, 29)
AT_L, AT_R, VIA, AT_2 = 29, 31, 33, 35
STAT, FAR = 36, 39
D3 = 43
N_SEM = 44

OWNER5 = (0, 1, 6, 7)


def averaging():
    row = lax.broadcasted_iota(jnp.int32, (BLOCK, BLOCK), 0)
    token = lax.broadcasted_iota(jnp.int32, (BLOCK, BLOCK), 1)
    result = jnp.zeros((BLOCK, BLOCK), F32)
    base = 0
    for level in range(1, 6):
        count = BLOCK >> level
        first = (row - base) << level
        hit = (row >= base) & (row < base + count) & (token >= first) & (token < first + (1 << level))
        result = jnp.where(hit, 0.5**level, result)
        base += count
    return result.astype(BF16)


def scores_of(q, k):
    return lax.dot_general(q, k, (((1,), (1,)), ((), ())), preferred_element_type=F32)


def attend(q, keys, values, biases, present):
    scores = [scores_of(q, k) for k in keys]
    if biases is not None:
        scores = [s + b for s, b in zip(scores, biases)]
    tops = [jnp.max(s, axis=1, keepdims=True) for s in scores]
    if present is not None:
        tops = [jnp.where(ok, t, NEG) for ok, t in zip(present, tops)]
    peak = tops[0]
    for t in tops[1:]:
        peak = jnp.maximum(peak, t)
    total = None
    for index, (s, v) in enumerate(zip(scores, values)):
        shift = peak if present is None else jnp.where(present[index], peak, BIG)
        probs = jnp.exp(s - shift).astype(BF16)
        part = jnp.dot(probs, v, preferred_element_type=F32)
        total = part if total is None else total + part
    return total, peak


def pairs(groups, low_half, lo, hi):
    all_scores = []
    for q, keys, _, biases, _ in groups:
        q = jnp.concatenate([q * lo, q * hi], axis=0)
        scores = [scores_of(q, k) for k in keys]
        if biases is not None:
            scores = [s + jnp.concatenate([b, b], axis=0) for s, b in zip(scores, biases)]
        all_scores.append(scores)
    ones = jnp.ones((BLOCK, 128), BF16)
    results = []
    for (q, _, values, _, present), scores in zip(groups, all_scores):
        tops = [jnp.max(s, axis=1, keepdims=True) for s in scores]
        if present is not None:
            tops = [jnp.where(ok, t, NEG) for ok, t in zip(present, tops)]
        peak = tops[0]
        for t in tops[1:]:
            peak = jnp.maximum(peak, t)
        out = None
        for index, (s, v) in enumerate(zip(scores, values)):
            shift = peak if present is None else jnp.where(present[index], peak, BIG)
            probs = jnp.exp(s - shift).astype(BF16)
            part = jnp.dot(probs, jnp.concatenate([v, ones], axis=1), preferred_element_type=F32)
            out = part if out is None else out + part
        n = q.shape[0]
        results.append(
            tuple(jnp.where(low_half, w[:n], w[n:]) for w in (out[:, :128], out[:, 128:], peak))
        )
    return results


def merge(a, b):
    peak = jnp.maximum(a[2], b[2])
    scale_a, scale_b = jnp.exp(a[2] - peak), jnp.exp(b[2] - peak)
    return a[0] * scale_a + b[0] * scale_b, a[1] * scale_a + b[1] * scale_b, peak


def expand(parts, ref):
    count = parts[0].shape[0]
    for index, part in enumerate(parts):
        ref[index, pl.ds(0, count, stride=2), :] = part
        ref[index, pl.ds(1, count, stride=2), :] = part
    return tuple(ref[index, 0 : 2 * count, :] for index in range(3))


def kernel(
    q_hbm, k_hbm, v_hbm, seg_hbm, w_hbm, out_ref,
    q0, kv0, segi, segf, q1, kv1, q2, kv2,
    s3, sd3, r3, sq3, rq3, s4, r4, s5, r5, sq4, rq4, sq5, rq5,
    st0, st1, st2, st3, rs3, srow4, rrow4, srow5, rrow5, ex, at, ra, via, sstat, rstat, sfar, rfar, near, wbuf,
    local, snd, rcv,
):
    i = lax.axis_index("seq")
    x = lax.axis_index("head")
    core = lax.rem(i, 2)
    chip = lax.div(i, 2)
    g4, a4 = lax.div(i, 4), lax.rem(i, 4)
    g5, a5 = lax.div(i, 8), lax.rem(i, 8)
    sibling = i + 1 - 2 * core
    right, left = lax.rem(i + 1, SEQ), lax.rem(i + SEQ - 1, SEQ)
    x_up, x_down, x_far = [lax.rem(x + d, HEADX) for d in (1, 3, 2)]
    late = lax.rem(g5, 2)
    beside5 = g5 + 1 - 2 * late
    owner5 = (a5 < 2) | (a5 >= 6)
    head5 = jnp.where(a5 < 2, a5, lax.rem(a5, 4))
    y_on = lax.rem(i + SEQ + 16 - 32 * late, SEQ)

    def remote(src, dst, slot, device):
        return pltpu.make_async_remote_copy(
            src_ref=src, dst_ref=dst, send_sem=snd.at[slot], recv_sem=rcv.at[slot], device_id=device, device_id_type=MESH
        )

    loads = []
    for p in range(2):
        lanes = pl.ds(128 * p, 128)
        loads.append(pltpu.make_async_copy(k_hbm.at[:, lanes], kv0.at[0, p, pl.ds(BLOCK, ROWS)], local.at[p]))
        loads.append(pltpu.make_async_copy(v_hbm.at[:, lanes], kv0.at[1, p, pl.ds(BLOCK, ROWS)], local.at[2 + p]))
        loads.append(pltpu.make_async_copy(q_hbm.at[:, lanes], q0.at[p], local.at[4 + p]))
    loads.append(pltpu.make_async_copy(seg_hbm, segi.at[1], local.at[6]))
    load_w = pltpu.make_async_copy(w_hbm, wbuf.at[x], local.at[7])
    for load in loads:
        load.start()
    load_w.start()

    barrier = pltpu.get_barrier_semaphore()

    def greet(seq, head):
        pl.semaphore_signal(barrier, inc=1, device_id={"seq": seq, "head": head}, device_id_type=MESH)

    blocks4 = [lax.rem(g4 + 1, SEQ // 4), lax.rem(g4 + SEQ // 4 - 1, SEQ // 4)]
    for j in range(8):
        greet(beside5 * 8 + j, x)
    for block in blocks4:
        for j in range(4):
            greet(block * 4 + j, x)
    for d in range(1, 8):
        greet(g5 * 8 + lax.rem(a5 + d, 8), x)
    for other in (x_up, x_down, x_far):
        greet(i, other)
    greet(lax.rem(i + 16, SEQ), x)
    greet(lax.rem(i + SEQ - 16, SEQ), x)

    lane = lax.broadcasted_iota(jnp.int32, (1, 128), 1)
    low_half = lane < 64
    lo_f = jnp.where(low_half, 1.0, 0.0).astype(F32)
    lo = lo_f.astype(BF16)
    hi = (1.0 - lo_f).astype(BF16)
    means = averaging()
    for load in loads:
        load.wait()
    last_k, last_v, last_q = [], [], []
    for t in range(4):
        rows = pl.ds(BLOCK + BLOCK * t, BLOCK)
        ck, cv = [
            jnp.dot(means, jnp.concatenate([kv0[n, 0, rows, :], kv0[n, 1, rows, :]], axis=1), preferred_element_type=F32)
            for n in range(2)
        ]
        own = pl.ds(BLOCK * t, BLOCK)
        cq = 0.125 * jnp.dot(means, jnp.concatenate([q0[0, own, :], q0[1, own, :]], axis=1), preferred_element_type=F32)
        for p in range(2):
            lanes = slice(128 * p, 128 * p + 128)
            q1[p, pl.ds(128 * t, 128), :] = cq[0:128, lanes].astype(BF16)
            q2[p, pl.ds(64 * t, 64), :] = cq[128:192, lanes].astype(BF16)
            sq3[p, pl.ds(32 * t, 32), :] = cq[192:224, lanes].astype(BF16)
            for n, c in enumerate((ck, cv)):
                kv1[n, p, pl.ds(BLOCK + 128 * t, 128), :] = c[0:128, lanes].astype(BF16)
                kv2[n, p, pl.ds(BLOCK + 64 * t, 64), :] = c[128:192, lanes].astype(BF16)
                s3[p, n, pl.ds(32 * t, 32), :] = c[192:224, lanes].astype(BF16)
        for h in range(4):
            s4[h, pl.ds(16 * t, 16), :] = packed(ck[224:240], cv[224:240], h, low_half).astype(BF16)
            sq4[h, pl.ds(16 * t, 16), :] = packed(cq[224:240], None, h, low_half).astype(BF16)
        last_k.append(ck[240:248])
        last_v.append(cv[240:248])
        last_q.append(cq[240:248])
    k5, v5, q5 = [jnp.concatenate(rows, axis=0) for rows in (last_k, last_v, last_q)]
    for h in range(4):
        s5[h] = packed(k5, v5, h, low_half).astype(BF16)
        sq5[h] = packed(q5, None, h, low_half).astype(BF16)

    segf[pl.ds(8, 8), :] = segi[1].astype(F32)

    def bias_of(b, j):
        exists = (4 * i + b + j >= 1) & (4 * i + b + j <= 4 * SEQ)
        first = 6 + 2 * (b + j)
        return [jnp.where(exists, segf[pl.ds(first + n, 1), :], -1.0) for n in range(2)]

    def level0(b):
        own = [
            jnp.transpose(jnp.broadcast_to(segf[pl.ds(8 + 2 * b + n, 1), :], (128, 128))) for n in range(2)
        ]
        own = jnp.concatenate(own, axis=0)
        biases = [
            jnp.concatenate([jnp.where(own == near_by, 0.0, NEG) for near_by in bias_of(b, j)], axis=1) for j in range(3)
        ]
        here = pl.ds(pl.multiple_of(b * BLOCK, BLOCK), BLOCK)
        rows = [pl.ds(pl.multiple_of((b + j) * BLOCK, BLOCK), BLOCK) for j in range(3)]
        groups = [
            (
                q0[p, here, :] * jnp.asarray(0.125, BF16),
                [kv0[0, p, r, :] for r in rows],
                [kv0[1, p, r, :] for r in rows],
                biases,
                None,
            )
            for p in range(2)
        ]
        for p, state in enumerate(pairs(groups, low_half, lo, hi)):
            for n in range(3):
                st0[n, p, here, :] = state[n]

    @pl.when(late == 0)
    def _():
        level0(1)
        level0(2)

    pl.semaphore_wait(barrier, 28)
    sends = []

    def send(src, dst, slot, seq, head=x):
        copy = remote(src, dst, slot, {"seq": seq, "head": head})
        copy.start()
        return copy

    def received(ref, slot):
        pltpu.make_async_copy(ref, ref, rcv.at[slot]).wait()

    def sent(ref, slot):
        pltpu.make_async_copy(ref, ref, snd.at[slot]).wait()

    def to_sides(ref, count, skip, slot):
        n = BLOCK - skip
        sends.append(send(ref.at[:, :, pl.ds(count, n)], ref.at[:, :, pl.ds(0, n)], slot, right))
        sends.append(
            send(
                ref.at[:, :, pl.ds(BLOCK + skip, n)], ref.at[:, :, pl.ds(BLOCK + count + skip, n)], slot + 1, left
            )
        )

    half = pl.ds(128 * core, 128)
    sends.append(send(w_hbm.at[half], wbuf.at[x, half], W_L, i, x_up))
    sends.append(send(w_hbm.at[half], wbuf.at[x, half], W_R, i, x_down))
    for h in range(4):
        send(s5.at[h], r5.at[late, a5], KV5, beside5 * 8 + OWNER5[h])

        @pl.when(a5 != OWNER5[h])
        def _():
            send(sq5.at[h], rq5.at[a5], Q5, g5 * 8 + OWNER5[h])

        @pl.when(a5 == OWNER5[h])
        def _():
            rq5[a5] = sq5[h]

    sends.append(send(segi.at[1], segi.at[0], SEG_P, right))
    sends.append(send(segi.at[1], segi.at[2], SEG_N, left))
    to_sides(kv0, ROWS, 0, L0_P)
    to_sides(kv1, 512, 128, L1_P)
    to_sides(kv2, 256, 128, L2_P)
    for direction, block in enumerate(blocks4):
        for j in range(4):
            send(s4.at[j], r4.at[direction, a4], KV4, block * 4 + j)
    for d in range(1, 4):
        other = lax.rem(a4 + d, 4)
        sends.append(send(sq4.at[other], rq4.at[a4], Q4 + d, g4 * 4 + other))
    sends.append(send(sq3.at[1 - core], rq3.at[core], Q3, sibling))
    beside = lax.rem(chip + 1 + core * (SEQ // 2 - 2), SEQ // 2)
    for p in range(2):
        send(s3.at[p], r3.at[core, :, core], KV3, beside * 2 + p)
    rq3[core] = sq3[core]
    rq4[a4] = sq4[a4]

    @pl.when(late == 1)
    def _():
        level0(1)
        level0(2)

    @pl.when(owner5)
    def _():
        received(r5.at[1 - late], KV5)
        send(r5.at[1 - late], r5.at[late], KV5_Y, y_on)

    def one_head(ref, queries, place, count):
        tiles = [ref[n].reshape(BLOCK, 128) for n in range(2)]
        out, peak = attend(queries, tiles, [t * hi + lo for t in tiles], None, (place > 0, place < count - 1))
        sums = peak + jnp.log(jnp.where(low_half, out, 1.0))
        first = sums.astype(BF16).astype(F32)
        second = (sums - first).astype(BF16).astype(F32)
        third = sums - first - second
        mean = out / pltpu.roll(out, 64, 1)
        parts = jnp.where(lane < 16, first, jnp.where(lane < 32, second, third))
        return jnp.where(low_half, parts, mean).astype(BF16)

    received(segi.at[0], SEG_P)
    received(segi.at[2], SEG_N)
    segf[pl.ds(0, 8), :] = segi[0].astype(F32)
    segf[pl.ds(16, 8), :] = segi[2].astype(F32)
    for side, (first, row1, row2) in enumerate(((0, 128, 192), (5 * BLOCK, 3 * BLOCK, 2 * BLOCK))):
        received(kv0.at[:, :, pl.ds(first, BLOCK)], L0_P + side)
        for n in range(2):
            rim = jnp.concatenate([kv0[n, p, pl.ds(first, BLOCK), :] for p in range(2)], axis=1)
            rim = jnp.dot(means[:192], rim, preferred_element_type=F32).astype(BF16)
            for p in range(2):
                kv1[n, p, pl.ds(row1, 128), :] = rim[:128, 128 * p : 128 * p + 128]
                kv2[n, p, pl.ds(row2, 64), :] = rim[128:, 128 * p : 128 * p + 128]
    level0(0)
    level0(3)

    quarter = [pl.ds(128 * core, 64), pl.ds(128 * core + 64, 64)]
    received(wbuf.at[x_down, half], W_L)
    sends.append(send(wbuf.at[x_down, quarter[0]], wbuf.at[x_down, quarter[0]], W2_L, i, x_up))
    sends.append(send(wbuf.at[x_down, half], wbuf.at[x_down, half], W_ON_L, sibling))
    received(wbuf.at[x_up, half], W_R)
    sends.append(send(wbuf.at[x_up, quarter[1]], wbuf.at[x_up, quarter[1]], W2_R, i, x_down))
    sends.append(send(wbuf.at[x_up, half], wbuf.at[x_up, half], W_ON_R, sibling))

    for side, (first, row2) in enumerate(((0, 128), (3 * BLOCK + 128, 2 * BLOCK + 64))):
        received(kv1.at[:, :, pl.ds(first, 128)], L1_P + side)
        for n in range(2):
            rim = jnp.concatenate([kv1[n, p, pl.ds(first, 128), :] for p in range(2)], axis=1)
            rim = jnp.dot(means[:64, :128], rim, preferred_element_type=F32).astype(BF16)
            for p in range(2):
                kv2[n, p, pl.ds(row2, 64), :] = rim[:, 128 * p : 128 * p + 128]

    received(kv2.at[:, :, pl.ds(0, 128)], L2_P)
    received(kv2.at[:, :, pl.ds(2 * BLOCK + 128, 128)], L2_N)

    for n in range(2):
        rows = pl.ds(pl.multiple_of(2 * BLOCK * core, BLOCK), BLOCK)
        rim = jnp.concatenate([kv2[n, p, rows, :] for p in range(2)], axis=1)
        rim = jnp.dot(means[:128], rim, preferred_element_type=F32).astype(BF16)
        for p in range(2):
            sd3[p, n] = rim[:, 128 * p : 128 * p + 128]
    sends.append(send(sd3.at[1 - core], r3.at[core, :, 1 - core], D3, sibling))
    r3[core, :, 1 - core] = sd3[core]

    sides = [pl.ds(0, BLOCK), pl.ds(2 * BLOCK, BLOCK)]
    present = (i > 0, i < SEQ - 1)
    groups = [(q2[p], [kv2[0, p, r, :] for r in sides], [kv2[1, p, r, :] for r in sides], None, present) for p in range(2)]
    for p, state in enumerate(pairs(groups, low_half, lo, hi)):
        for n in range(3):
            st2[n, p] = state[n]
    for b in range(2):
        own = pl.ds(b * BLOCK, BLOCK)
        sides = [own, pl.ds((b + 2) * BLOCK, BLOCK)]
        present = (2 * i + b > 0, 2 * i + b < 2 * SEQ - 1)
        groups = [
            (q1[p, own, :], [kv1[0, p, r, :] for r in sides], [kv1[1, p, r, :] for r in sides], None, present)
            for p in range(2)
        ]
        for p, state in enumerate(pairs(groups, low_half, lo, hi)):
            for n in range(3):
                st1[n, p, own, :] = state[n]

    for p in range(2):
        state = expand(tuple(st2[n, p] for n in range(3)), ex)
        state = merge(state, tuple(st1[n, p] for n in range(3)))
        for n in range(3):
            st1[n, p] = state[n]

    @pl.when(owner5)
    def _():
        received(rq5.at[pl.ds(0, 7)], Q5)
        received(r5.at[late], KV5_Y)
        srow5[...] = one_head(r5, rq5[...].reshape(BLOCK, 128), g5, SEQ // 8).reshape(8, 32, 128)
        for d in range(1, 8):
            other = lax.rem(a5 + d, 8)
            send(srow5.at[other], rrow5.at[head5], RES5, g5 * 8 + other)
        rrow5[head5] = srow5[a5]

    row = lax.broadcasted_iota(jnp.int32, (8, BLOCK), 0)

    def finish(d):
        t = lax.rem(x + d, HEADX)
        sums = []
        for p in range(2):
            coarse = expand(tuple(st1[n, p, pl.ds(pl.multiple_of(128 * t, 128), 128), :] for n in range(3)), ex)
            fine = tuple(st0[n, p, pl.ds(pl.multiple_of(BLOCK * t, BLOCK), BLOCK), :] for n in range(3))
            num, total, peak = merge(fine, coarse)
            mean = (num / total).astype(BF16)
            sums.append(jnp.transpose(peak + jnp.log(total)))
            if d == 0:
                ra[x, p] = mean
                continue
            at[t, p] = mean
            if d == 1:
                sends.append(send(at.at[t, p], ra.at[x, p], AT_L + p, i, x_up))
            if d == 3:
                sends.append(send(at.at[t, p], ra.at[x, p], AT_R + p, i, x_down))
            if d == 2:
                sends.append(send(at.at[t, p], via.at[p], VIA + p, i, x_down if p else x_up))
        stat = jnp.where(row < 2, sums[0][0:8], sums[1][0:8])
        stat = jnp.where(row == 1, sums[0][64:72], jnp.where(row == 3, sums[1][64:72], stat))
        if d == 0:
            rstat[x] = stat
        else:
            sstat[t] = stat
            sends.append(send(sstat.at[t], rstat.at[x], STAT + d, i, t))

    for d in (2, 1, 3, 0):
        finish(d)

    for d in range(1, 4):
        received(rq4.at[lax.rem(a4 + 4 - d, 4)], Q4 + d)
    received(r4, KV4)
    srow4[...] = one_head(r4, rq4[...].reshape(BLOCK, 128), g4, SEQ // 4).reshape(4, 64, 128)
    for d in range(1, 4):
        other = lax.rem(a4 + d, 4)
        sends.append(send(srow4.at[other], rrow4.at[a4], RES4 + d, g4 * 4 + other))
    rrow4[a4] = srow4[a4]

    received(r3.at[0], KV3)
    received(r3.at[1 - core, :, core], D3)
    received(rq3.at[1 - core], Q3)
    group = (
        rq3[...].reshape(BLOCK, 128),
        [r3[n, 0].reshape(BLOCK, 128) for n in range(2)],
        [r3[n, 1].reshape(BLOCK, 128) for n in range(2)],
        None,
        (chip > 0, chip < SEQ // 2 - 1),
    )
    state = pairs([group], low_half, lo, hi)[0]
    for n in range(3):
        for m in range(2):
            rs3[m, n] = state[n][128 * m : 128 * m + 128]
    sends.append(send(rs3.at[1 - core], st3.at[core], RES3, sibling))
    st3[core] = rs3[core]

    received(wbuf.at[x_far, quarter[0]], W2_L)
    received(wbuf.at[x_far, quarter[1]], W2_R)
    sends.append(send(wbuf.at[x_far, half], wbuf.at[x_far, half], W_ON_2, sibling))

    received(via.at[0], VIA)
    sends.append(send(via.at[0], ra.at[x_down, 0], AT_2, i, x_up))
    received(via.at[1], VIA + 1)
    sends.append(send(via.at[1], ra.at[x_up, 1], AT_2 + 1, i, x_down))

    for d in range(1, 4):
        received(rrow4.at[lax.rem(a4 + 4 - d, 4)], RES4 + d)

    @pl.when(owner5)
    def _():
        received(rrow5.at[pl.ds(0, 3)], RES5)

    @pl.when(jnp.logical_not(owner5))
    def _():
        received(rrow5, RES5)

    received(st3.at[1 - core], RES3)
    sums = []
    for p in range(2):

        def far(ref):
            even, odd = ref[2 * p].astype(F32), ref[2 * p + 1].astype(F32)
            num = jnp.where(low_half, pltpu.roll(even, 64, 1), odd)
            even, odd = [w[:, 0:1] + w[:, 16:17] + w[:, 32:33] for w in (even, odd)]
            return num, jnp.ones_like(num), jnp.where(low_half, even, odd)

        state = merge(expand(far(rrow5), ex), far(rrow4))
        num, total, peak = merge(expand(state, ex), tuple(st3[p, n] for n in range(3)))
        mean = num / total
        sums.append(peak + jnp.log(total))
        for t in range(4):
            sfar[t, p] = mean[32 * t : 32 * t + 32].astype(BF16)
    both = jnp.where(lane < 96, pltpu.roll(sums[1], 64, 1), sums[1])
    both = jnp.where(lane < 32, sums[0], jnp.where(low_half, pltpu.roll(sums[0], 96, 1), both))
    high = both.astype(BF16).astype(F32)
    middle = (both - high).astype(BF16).astype(F32)
    place = lax.rem(lane, 32)
    both = jnp.where(place < 8, high, jnp.where(place < 16, middle, both - high - middle)).astype(BF16)
    for t in range(4):
        sfar[t, 2] = both[32 * t : 32 * t + 32]
    for d in (2, 1, 3):
        other = lax.rem(x + d, HEADX)
        sends.append(send(sfar.at[other], rfar.at[x], FAR + d, i, other))
    rfar[x] = sfar[x]

    for d in range(1, 4):
        received(rstat.at[lax.rem(x + HEADX - d, HEADX)], STAT + d)
    for m in range(4):
        for p in range(2):
            lines = [jnp.broadcast_to(rstat[m, 2 * p + n : 2 * p + n + 1, :], (64, BLOCK)) for n in range(2)]
            near[m, p] = jnp.transpose(jnp.concatenate(lines, axis=0))

    load_w.wait()
    other_half = pl.ds(128 * (1 - core), 128)
    for owner, slot in ((x_down, W_ON_L), (x_up, W_ON_R), (x_far, W_ON_2)):
        received(wbuf.at[owner, other_half], slot)
    for p in range(2):
        for owner, slot in ((x_down, AT_L), (x_up, AT_R), (x_far, AT_2)):
            received(ra.at[owner, p], slot + p)
    for d in range(1, 4):
        received(rfar.at[lax.rem(x + HEADX - d, HEADX)], FAR + d)

    def spread(rows):
        return jnp.broadcast_to(rows[:, None, :], (32, 8, 128)).reshape(BLOCK, 128)

    attention = []
    for m in range(4):
        for p in range(2):
            parts = rfar[m, 2].astype(F32)
            even, odd = [
                parts[:, n : n + 1] + parts[:, n + 8 : n + 9] + parts[:, n + 16 : n + 17] for n in (64 * p, 64 * p + 32)
            ]
            sums = jnp.where(low_half, even, odd)
            weight = 1.0 / (1.0 + jnp.exp(spread(sums) - near[m, p]))
            coarse = spread(rfar[m, p].astype(F32))
            attention.append((coarse + weight * (ra[m, p].astype(F32) - coarse)).astype(BF16))
    for n in range(4):
        columns = pl.ds(256 * n, 256)
        total = None
        for m in range(4):
            rows = jnp.concatenate(attention[2 * m : 2 * m + 2], axis=1)
            part = jnp.dot(rows, wbuf[m, :, columns], preferred_element_type=F32)
            total = part if total is None else total + part
        out_ref[:, columns] = total.astype(BF16)

    for copy in sends:
        copy.wait_send()
    sent(s5, KV5)
    for h in range(4):

        @pl.when(a5 != OWNER5[h])
        def _():
            sent(sq5.at[h], Q5)

    @pl.when(owner5)
    def _():
        sent(r5.at[0], KV5_Y)
        sent(srow5.at[pl.ds(0, 7)], RES5)

    sent(r4, KV4)
    sent(r3.at[0], KV3)


def packed(first, second, h, low_half):
    lanes = slice(128 * (h // 2), 128 * (h // 2) + 128)
    first = first[:, lanes]
    if h % 2:
        first = pltpu.roll(first, 64, 1)
    if second is None:
        return jnp.where(low_half, first, 0.0)
    second = second[:, lanes]
    if h % 2 == 0:
        second = pltpu.roll(second, 64, 1)
    return jnp.where(low_half, first, second)


def on_device(query_rows, key_rows, value_rows, segment, w_out):
    vmem = pltpu.VMEM
    operands = (query_rows, key_rows, value_rows, segment.reshape(8, 128), w_out)
    return pl.pallas_call(
        kernel,
        out_shape=jax.ShapeDtypeStruct((BLOCK, 1024), BF16),
        in_specs=[pl.BlockSpec(memory_space=pl.ANY)] * 5,
        out_specs=pl.BlockSpec(memory_space=vmem),
        scratch_shapes=[
            vmem((2, ROWS, 128), BF16),
            vmem((2, 2, ROWS + 512, 128), BF16),
            vmem((3, 8, 128), jnp.int32),
            vmem((24, 128), F32),
            vmem((2, 512, 128), BF16),
            vmem((2, 2, 1024, 128), BF16),
            vmem((2, 256, 128), BF16),
            vmem((2, 2, 768, 128), BF16),
            vmem((2, 2, 128, 128), BF16),
            vmem((2, 2, 128, 128), BF16),
            vmem((2, 2, 2, 128, 128), BF16),
            vmem((2, 128, 128), BF16),
            vmem((2, 128, 128), BF16),
            vmem((4, 64, 128), BF16),
            vmem((2, 4, 64, 128), BF16),
            vmem((4, 32, 128), BF16),
            vmem((2, 8, 32, 128), BF16),
            vmem((4, 64, 128), BF16),
            vmem((4, 64, 128), BF16),
            vmem((4, 32, 128), BF16),
            vmem((8, 32, 128), BF16),
            vmem((3, 2, ROWS, 128), F32),
            vmem((3, 2, 512, 128), F32),
            vmem((3, 2, 256, 128), F32),
            vmem((2, 3, 128, 128), F32),
            vmem((2, 3, 128, 128), F32),
            vmem((4, 64, 128), BF16),
            vmem((4, 64, 128), BF16),
            vmem((8, 32, 128), BF16),
            vmem((4, 32, 128), BF16),
            vmem((3, 520, 128), F32),
            vmem((4, 2, BLOCK, 128), BF16),
            vmem((4, 2, BLOCK, 128), BF16),
            vmem((2, BLOCK, 128), BF16),
            vmem((4, 8, BLOCK), F32),
            vmem((4, 8, BLOCK), F32),
            vmem((4, 3, 32, 128), BF16),
            vmem((4, 3, 32, 128), BF16),
            vmem((4, 2, BLOCK, 128), F32),
            vmem((4, 256, 1024), BF16),
            pltpu.SemaphoreType.DMA((8,)),
            pltpu.SemaphoreType.DMA((N_SEM,)),
            pltpu.SemaphoreType.DMA((N_SEM,)),
        ],
        compiler_params=pltpu.CompilerParams(
            collective_id=0, has_side_effects=True, vmem_limit_bytes=48 * 2**20
        ),
        name="block_attention",
    )(*[pltpu.with_memory_space_constraint(a, pltpu.HBM) for a in operands])


def solution(mesh):
    placed = (P("seq", "head"), P("seq", "head"), P("seq", "head"), P("seq"), P("head", None))
    return jax.shard_map(
        on_device, mesh=mesh, in_specs=placed, out_specs=P(("seq", "head"), None), check_vma=False
    )
```
